32 devices in a mesh: dirs: 2 (over y), taps: 4 (over z), tm: 2 (over x), floors: 2 (over core).
Axes of the slice: x: 2, y: 2, z: 4, core: 2. Of those that a mesh axis runs over, the one named last changes fastest.
Arguments:
- pressures: bfloat16 [4096, 16384], P(('dirs', 'tm'), ('taps', 'floors')), parts along dimension 0, may hold values from -6 to 6
- tap_area: bfloat16 [16384], P(('taps', 'floors')), may hold values from 0.29882812 to 3
- tap_panel: int32 [16384], P(('taps', 'floors')), may hold values from 0 to 255
- tap_floor: int32 [16384], P(('taps', 'floors')), may hold values from 0 to 15
- panel_shape: bfloat16 [256, 512], replicated, may hold values from -0.046875 to 0.046875
- floor_shape: bfloat16 [16, 512], replicated, may hold values from -0.25 to 0.25
- mode_order: int32 [512], replicated, may hold values from 0 to 511, each once
- mode_decay: float32 [512], replicated, may hold values from 4.8828125e-05 to 0.08
- mode_freq: float32 [512], replicated, may hold values from 0.02 to 1.2
Outputs:
- modal_response: float32 [512, 4096], P(('taps', 'floors'), ('dirs', 'tm')), parts along dimension 1
- floor_motion: float32 [16, 4096], P(('taps', 'floors'), ('dirs', 'tm')), parts along dimension 1
- floor_load: float32 [16, 4096], P(('taps', 'floors'), ('dirs', 'tm')), parts along dimension 1
The draws below stay inside these ranges and needn't reach their ends.
There are 2 independent parts, one for each index of `dirs`. The reference program is written for one: setup_inputs(seed, part) draws one part's arguments, and reference() takes and returns one part's arrays. A program takes and returns all parts, laid end to end along the dimension named above; an argument that names none is the same for every part. Nothing has to cross between parts.
All inputs are finite; a program needn't handle non-finite values.
Results may differ from the reference program's by a relative error of at most 0.0029.
Values sent between devices are 32-bit elements; how exact they have to be, the bound alone decides.
No kernel may reach another device: no remote copies, remote signals or barrier semaphores. Data moves between devices by JAX's collectives and lax.ppermute only.
A program may use at most 64 MiB of HBM per device.

```python
import math
import jax
import jax.numpy as jnp
from jax import lax

M = 512
PANELS = 256
TAP_DEV = 2048
TIME = 2048
TAPS = 16384
FLOORS = 16


def draw_mode_decay(key, part):
    key_pick = jax.random.fold_in(key, 11)
    key_slow = jax.random.fold_in(key, 12)
    key_fast = jax.random.fold_in(key, 13)
    slow_share = 0.5
    slow_pick = jax.random.uniform(key_pick, (M,), jnp.float32) < slow_share
    slow_rates = 0.1 / TIME * jnp.exp(jax.random.uniform(key_slow, (M,), jnp.float32, 0.0, math.log(10.0)))
    fast_rates = jnp.exp(jax.random.uniform(key_fast, (M,), jnp.float32, math.log(0.02), math.log(0.08)))
    return jnp.where(slow_pick, slow_rates, fast_rates).astype(jnp.float32)


def touch_ends(values, own_key, least, largest):
    extent = values.shape
    index_at = [jax.random.randint(jax.random.fold_in(own_key, axis), (), 0, extent[axis]) for axis in range(len(extent))]
    values = values.at[tuple(index_at)].set(least)
    longest = extent.index(max(extent))
    index_at[longest] = (index_at[longest] + 1) % extent[longest]
    return values.at[tuple(index_at)].set(largest)


def block_levels(stream_key, shape, cuts, least, largest):
    level, own = 1.0, jax.random.fold_in(stream_key, 6)
    for position, blocks in cuts:
        heights = jnp.exp(jax.random.uniform(jax.random.fold_in(own, position), (blocks,), jnp.float32, least / len(cuts), largest / len(cuts)))
        level = level * jnp.repeat(heights, shape[position] // blocks).reshape([-1 if axis == position else 1 for axis in range(len(shape))])
    return level


def noise(own_key, extent, spread, limit, shards=(), held_as=jnp.bfloat16):
    result = spread * jax.random.normal(own_key, extent, jnp.float32)
    if shards:
        result = result * block_levels(own_key, extent, shards, -0.22, 0.18)
    return jnp.clip(result, -limit, limit).astype(held_as)


def setup_inputs(seed: int = 0, part: int = 0) -> dict:
    streams_of = jax.random.split(jax.random.key(seed), 10)
    own_keys = jax.random.split(jax.random.fold_in(streams_of[9], part), 10)
    pressures = noise(own_keys[0], (TIME, TAPS), 1.0, 6.0, ((0, 2), (1, 8)))
    tap_area = jnp.clip(jnp.exp(math.log(3.0) - 2.306499 * jax.random.uniform(streams_of[1], (TAPS,), jnp.float32) ** block_levels(streams_of[1], (TAPS,), ((0, 8),), -0.2, 0.2)), 0.29882812, 3.0).astype(jnp.bfloat16)
    tap_panel = touch_ends(jax.random.randint(streams_of[2], (TAPS,), 0, PANELS), jax.random.fold_in(streams_of[2], 1), 0, PANELS - 1).astype(jnp.int32)
    tap_floor = touch_ends(jax.random.randint(streams_of[3], (TAPS,), 0, FLOORS), jax.random.fold_in(streams_of[3], 1), 0, FLOORS - 1).astype(jnp.int32)
    panel_shape = noise(streams_of[4], (PANELS, M), TAPS ** -0.5, 0.046875)
    floor_shape = noise(streams_of[5], (FLOORS, M), M ** -0.5, 0.25)
    mode_order = jax.random.permutation(streams_of[6], M).astype(jnp.int32)
    mode_decay = draw_mode_decay(jax.random.fold_in(streams_of[9], 71), part)
    mode_freq = jnp.clip(jnp.exp(jax.random.uniform(streams_of[8], (M,), jnp.float32, math.log(0.02), math.log(1.2))), 0.02, 1.2)
    return {"pressures": pressures, "tap_area": tap_area, "tap_panel": tap_panel, "tap_floor": tap_floor, "panel_shape": panel_shape, "floor_shape": floor_shape, "mode_order": mode_order, "mode_decay": mode_decay, "mode_freq": mode_freq}


def reference(pressures, tap_area, tap_panel, tap_floor, panel_shape, floor_shape, mode_order, mode_decay, mode_freq):
    ordered = jnp.take(panel_shape, mode_order, axis=1)
    floor_ids = jnp.arange(FLOORS, dtype=jnp.int32)
    block_count = TAPS // TAP_DEV

    def accumulate(carried, block_idx):
        start = (block_idx * TAP_DEV).astype(jnp.int32)
        window = lax.dynamic_slice_in_dim(pressures, start, TAP_DEV, 1)
        area_block = lax.dynamic_slice_in_dim(tap_area, start, TAP_DEV, 0)
        panel_block = lax.dynamic_slice_in_dim(tap_panel, start, TAP_DEV, 0)
        floor_block = lax.dynamic_slice_in_dim(tap_floor, start, TAP_DEV, 0)
        tributary = (jnp.take(ordered, panel_block, axis=0).astype(jnp.float32) * area_block.astype(jnp.float32)[:, None]).astype(jnp.bfloat16)
        forces = carried[0] + lax.dot_general(tributary, window, (((0,), (1,)), ((), ())), preferred_element_type=jnp.float32)
        weights = jnp.where(floor_block[None, :] == floor_ids[:, None], area_block[None, :], jnp.zeros((), jnp.bfloat16))
        loads = carried[1] + lax.dot_general(weights, window, (((1,), (1,)), ((), ())), preferred_element_type=jnp.float32)
        return ((forces, loads), None)
    start_sums = (jnp.zeros((M, TIME), jnp.float32), jnp.zeros((FLOORS, TIME), jnp.float32))
    (forces, loads), _ = lax.scan(accumulate, start_sums, jnp.arange(block_count, dtype=jnp.int32))
    decays = jnp.take(mode_decay, mode_order)
    angles = jnp.take(mode_freq, mode_order)
    input_gain = jnp.sqrt(-jnp.expm1(-2.0 * decays))
    turn_re = jnp.exp(-decays) * jnp.cos(angles)
    turn_im = jnp.exp(-decays) * jnp.sin(angles)

    def advance(carried, force_now):
        real_part, imag_part = carried
        next_real = turn_re * real_part - turn_im * imag_part + input_gain * force_now
        next_imag = turn_im * real_part + turn_re * imag_part
        return ((next_real, next_imag), next_real)
    zeros_state = jnp.zeros((M,), jnp.float32)
    _, history = lax.scan(advance, (zeros_state, zeros_state), forces.T)
    motion = history.T
    local_shape = jnp.take(floor_shape, mode_order, axis=1).astype(jnp.float32)
    floor_motion = jnp.dot(local_shape, motion, precision=lax.Precision.HIGHEST, preferred_element_type=jnp.float32)
    floor_load = loads * (FLOORS / TAPS) ** 0.5
    return (motion, floor_motion, floor_load)
```

```python
import jax
import jax.numpy as jnp
from jax import lax
from jax.experimental import pallas as pl
from jax.experimental.pallas import tpu as pltpu
from jax.sharding import PartitionSpec as P

BLK = 256
TILE = 128
BF = jnp.bfloat16
F32 = jnp.float32
NN = (((1,), (0,)), ((), ()))
NT = (((1,), (1,)), ((), ()))
VMEM_LIMIT = 48 * 1024 * 1024


def dot(a, b, dims=NN):
    return lax.dot_general(a, b, dims, preferred_element_type=F32)


def split(x):
    hi = x.astype(BF)
    return hi, (x - hi.astype(F32)).astype(BF)


def dot_exact_left(a, x, dims=NN):
    hi, lo = split(x)
    return dot(a, hi, dims) + dot(a, lo, dims)


def dot_exact_right(x, b, dims=NN):
    hi, lo = split(x)
    return dot(hi, b, dims) + dot(lo, b, dims)


def params():
    return pltpu.CompilerParams(vmem_limit_bytes=VMEM_LIMIT)


def whole(n):
    return [pl.BlockSpec(memory_space=pltpu.VMEM)] * n


def make_tap_sums(panels, floors, taps, time):
    rows = panels + floors

    def body(press_ref, panel_ref, floor_ref, area_ref, sums_ref, weights):
        @pl.when(pl.program_id(0) == 0)
        def _():
            area = area_ref[...].astype(F32)
            ids = lax.broadcasted_iota(jnp.int32, (panels, taps), 0)
            weights[:panels] = jnp.where(ids == panel_ref[...], area, 0.0).astype(BF)
            ids = lax.broadcasted_iota(jnp.int32, (floors, taps), 0)
            weights[panels:] = jnp.where(ids == floor_ref[...], area, 0.0).astype(BF)

        sums_ref[...] = dot(weights[...], press_ref[...], NT)

    row = pl.BlockSpec((1, taps), lambda i: (0, 0))
    return pl.pallas_call(
        body,
        grid=(time // BLK,),
        in_specs=[pl.BlockSpec((BLK, taps), lambda i: (i, 0)), row, row, row],
        out_specs=pl.BlockSpec((rows, BLK), lambda i: (0, i)),
        out_shape=jax.ShapeDtypeStruct((rows, time), F32),
        scratch_shapes=[pltpu.VMEM((rows, taps), BF)],
        compiler_params=params(),
        name="tap_sums",
    )


def mode_tables(order, decay, freq, panel_shape, floor_shape):
    modes = order.shape[1]
    panels = panel_shape.shape[0]
    floors = floor_shape.shape[0]

    def body(order_ref, decay_ref, freq_ref, panel_ref, floor_ref, pt_ref, fs_ref, rate_ref):
        spread = jnp.broadcast_to(order_ref[...].astype(F32), (TILE, modes))
        column = spread.T[:, :1]
        ids = lax.broadcasted_iota(jnp.int32, (modes, modes), 1).astype(F32)
        hit = column == ids
        rate_ref[:, 0:1] = jnp.sum(jnp.where(hit, decay_ref[...], 0.0), axis=1, keepdims=True)
        rate_ref[:, 1:2] = jnp.sum(jnp.where(hit, freq_ref[...], 0.0), axis=1, keepdims=True)
        pick = jnp.where(hit, 1.0, 0.0).astype(BF)
        pt_ref[...] = dot(pick, panel_ref[...], NT)
        fs_ref[...] = dot(floor_ref[...], pick, NT)

    return pl.pallas_call(
        body,
        in_specs=whole(5),
        out_specs=tuple(whole(3)),
        out_shape=(
            jax.ShapeDtypeStruct((modes, panels), F32),
            jax.ShapeDtypeStruct((floors, modes), F32),
            jax.ShapeDtypeStruct((modes, 2), F32),
        ),
        compiler_params=params(),
        name="mode_tables",
    )(order, decay, freq, panel_shape, floor_shape)


def slot_forces(place, sums, pt, nz, nc, mode_dev):
    panels = pt.shape[1]
    rows, time = sums[0].shape

    def body(place_ref, *refs):
        sum_refs, pt_ref, out_refs = refs[:nc], refs[nc], refs[nc + 1 :]
        z, c = place_ref[0], place_ref[1]
        total = sum_refs[0][:panels]
        for ref in sum_refs[1:]:
            total = total + ref[:panels]
        picked = []
        for d in range(nz):
            owner = lax.rem(z + d, nz) * nc + c
            picked.append(pt_ref[pl.ds(pl.multiple_of(owner * mode_dev, mode_dev), mode_dev), :])
        left = jnp.concatenate(picked, axis=0).astype(BF)
        forces = dot_exact_left(left, total)
        for d in range(nz):
            out_refs[d][...] = forces[d * mode_dev : (d + 1) * mode_dev]

    steps = time // BLK
    return pl.pallas_call(
        body,
        grid=(steps,),
        in_specs=[pl.BlockSpec(memory_space=pltpu.SMEM)]
        + [pl.BlockSpec((rows, BLK), lambda i: (0, i))] * nc
        + [pl.BlockSpec(pt.shape, lambda i: (0, 0))],
        out_specs=[pl.BlockSpec((mode_dev, BLK), lambda i: (0, i))] * nz,
        out_shape=[jax.ShapeDtypeStruct((mode_dev, time), F32)] * nz,
        compiler_params=params(),
        name="slot_forces",
    )(place, *sums, pt)


def turn_tables(decay, freq):
    slots = decay.shape[0]
    lane = lax.broadcasted_iota(jnp.int32, (slots, BLK), 1)
    step_re, step_im = jnp.cos(freq), jnp.sin(freq)
    re = jnp.ones((slots, BLK), F32)
    im = jnp.zeros((slots, BLK), F32)
    bit = 1
    while bit < BLK:
        on = (lane & bit) != 0
        new_re = re * step_re - im * step_im
        new_im = re * step_im + im * step_re
        re = jnp.where(on, new_re, re)
        im = jnp.where(on, new_im, im)
        step_re, step_im = step_re * step_re - step_im * step_im, 2.0 * step_re * step_im
        bit *= 2
    steps = decay * lane.astype(F32)
    shrink = jnp.exp(-steps)
    gain = jnp.sqrt(1.0 - jnp.exp(-2.0 * decay)) * jnp.exp(steps)
    fade = jnp.exp(-decay * float(BLK))
    return (gain * re, -gain * im, shrink * re, shrink * im, fade * step_re, fade * step_im)


def triangle():
    row = lax.broadcasted_iota(jnp.int32, (BLK, BLK), 0)
    col = lax.broadcasted_iota(jnp.int32, (BLK, BLK), 1)
    return jnp.where(row <= col, 1.0, 0.0).astype(BF)


def turned(a, b):
    return (a[0] * b[0] - a[1] * b[1], a[0] * b[1] + a[1] * b[0])


def partial_states(place, sums, pt, rates, floor_slots, mode_dev, floor_dev, nc):
    modes, panels = pt.shape
    rows, time = sums[0].shape
    floors = floor_slots.shape[0]
    blocks = time // BLK

    def body(place_ref, *refs):
        sum_refs = refs[:nc]
        pt_ref, rate_ref, fs_ref = refs[nc : nc + 3]
        motion_ref, ends_ref, qr_ref, qi_ref, own_ref, hi_ref, lo_ref, tab_ref = refs[nc + 3 :]
        total = sum_refs[0][:panels]
        for ref in sum_refs[1:]:
            total = total + ref[:panels]
        hi_ref[...], lo_ref[...] = split(total)
        motion_ref[...] = jnp.zeros_like(motion_ref)
        tri = triangle()

        @pl.loop(0, modes // TILE)
        def _(i):
            at = pl.ds(pl.multiple_of(i * TILE, TILE), TILE)
            rate = rate_ref[at, :]
            pr, pi, qr, qi, zr, zi = turn_tables(rate[:, 0:1], rate[:, 1:2])
            qr_ref[at, :] = qr
            qi_ref[at, :] = qi
            tab_ref[0, at, :] = pr
            tab_ref[1, at, :] = pi
            shape = pt_ref[at, :].astype(BF)
            here = fs_ref[:, at].astype(BF)
            ar = jnp.zeros((TILE, 1), F32)
            ai = jnp.zeros((TILE, 1), F32)
            for b in range(blocks):
                cols = slice(b * BLK, (b + 1) * BLK)
                force = dot(shape, hi_ref[:, cols]) + dot(shape, lo_ref[:, cols])
                cr = dot_exact_right(force * pr, tri) + ar
                ci = dot_exact_right(force * pi, tri) + ai
                resp = qr * cr - qi * ci
                motion_ref[:, cols] += dot_exact_left(here, resp)
                ar, ai = turned((zr, zi), (cr[:, BLK - 1 :], ci[:, BLK - 1 :]))
            pad = jnp.zeros((TILE, TILE - 4), F32)
            ends_ref[:, at] = jnp.concatenate([ar, ai, zr, zi, pad], axis=1).T[:8]

        own = pl.ds(pl.multiple_of(place_ref[2] * mode_dev, mode_dev), mode_dev)
        own_ref[0] = tab_ref[0, own, :]
        own_ref[1] = tab_ref[1, own, :]
        own_ref[2] = qr_ref[own, :]
        own_ref[3] = qi_ref[own, :]

    return pl.pallas_call(
        body,
        in_specs=[pl.BlockSpec(memory_space=pltpu.SMEM)] + whole(nc + 3),
        out_specs=tuple(whole(5)),
        out_shape=(
            jax.ShapeDtypeStruct((floors, time), F32),
            jax.ShapeDtypeStruct((8, modes), F32),
            jax.ShapeDtypeStruct((modes, BLK), F32),
            jax.ShapeDtypeStruct((modes, BLK), F32),
            jax.ShapeDtypeStruct((4, mode_dev, BLK), F32),
        ),
        scratch_shapes=[
            pltpu.VMEM((panels, time), BF),
            pltpu.VMEM((panels, time), BF),
            pltpu.VMEM((2, modes, BLK), F32),
        ],
        compiler_params=params(),
        name="partial_states",
    )(place, *sums, pt, rates, floor_slots)


def floor_shares(place, motion, ends, enter, qr, qi, floor_slots, sums, nz, nc, floor_dev, mode_dev):
    floors, time = motion.shape
    modes = floor_slots.shape[1]
    blocks = time // BLK
    rows = -(-(2 * floor_dev + 2) // 8) * 8
    load_at = sums[0].shape[0] - floors
    owners = nz * nc

    def body(place_ref, motion_ref, ends_ref, enter_ref, qr_ref, qi_ref, fs_ref, *refs):
        sum_refs, out_refs = refs[:nc], refs[nc : nc + nz]
        motions, loads, starts = refs[nc + nz :]
        z, c = place_ref[0], place_ref[1]
        shape = fs_ref[...]
        turn = (ends_ref[2:3, :], ends_ref[3:4, :])
        state = (enter_ref[0:1, :], enter_ref[1:2, :])
        left_re, left_im = [], []
        for b in range(blocks):
            left_re.append(shape * state[0])
            left_im.append(shape * state[1])
            state = turned(turn, state)
        qr_hi, qr_lo = split(qr_ref[...])
        qi_hi, qi_lo = split(qi_ref[...])
        re_hi, re_lo = split(jnp.concatenate(left_re, axis=0))
        im_hi, im_lo = split(jnp.concatenate(left_im, axis=0))
        free = dot(re_hi, qr_hi) + dot(re_hi, qr_lo) + dot(re_lo, qr_hi)
        free = free - (dot(im_hi, qi_hi) + dot(im_hi, qi_lo) + dot(im_lo, qi_hi))
        load = sum_refs[0][load_at:]
        for ref in sum_refs[1:]:
            load = load + ref[load_at:]
        full = jnp.concatenate([free[b * floors : (b + 1) * floors] for b in range(blocks)], axis=1)
        full = full + motion_ref[...]
        for o in range(owners):
            motions[o] = full[o * floor_dev : (o + 1) * floor_dev]
            loads[o] = load[o * floor_dev : (o + 1) * floor_dev]
            starts[o] = enter_ref[0:2, o * mode_dev : (o + 1) * mode_dev]
        for d in range(nz):
            owner = lax.rem(z + d, nz) * nc + c
            out = out_refs[d]
            out[...] = jnp.zeros_like(out)
            out[:floor_dev] = motions[owner]
            out[floor_dev : 2 * floor_dev] = loads[owner]
            out[2 * floor_dev : 2 * floor_dev + 2, :mode_dev] = starts[owner]

    return pl.pallas_call(
        body,
        in_specs=[pl.BlockSpec(memory_space=pltpu.SMEM)] + whole(6 + nc),
        out_specs=whole(nz),
        out_shape=[jax.ShapeDtypeStruct((rows, time), F32)] * nz,
        scratch_shapes=[
            pltpu.VMEM((owners, floor_dev, time), F32),
            pltpu.VMEM((owners, floor_dev, time), F32),
            pltpu.VMEM((owners, 2, mode_dev), F32),
        ],
        compiler_params=params(),
        name="floor_shares",
    )(place, motion, ends, enter, qr, qi, floor_slots, *sums)


def own_response(forces, shares, tables, floor_dev, load_scale):
    mode_dev, time = forces[0].shape
    n = len(forces)
    blocks = time // BLK

    def body(*refs):
        force_refs, share_refs, tab_ref = refs[:n], refs[n : 2 * n], refs[2 * n]
        resp_ref, motion_ref, load_ref = refs[2 * n + 1 :]
        share = share_refs[0][...]
        for ref in share_refs[1:]:
            share = share + ref[...]
        motion_ref[...] = share[:floor_dev]
        load_ref[...] = share[floor_dev : 2 * floor_dev] * load_scale
        pr, pi, qr, qi = tab_ref[0], tab_ref[1], tab_ref[2], tab_ref[3]
        zr = (qr[:, BLK - 1 :] * qr[:, 1:2]) - (qi[:, BLK - 1 :] * qi[:, 1:2])
        zi = (qr[:, BLK - 1 :] * qi[:, 1:2]) + (qi[:, BLK - 1 :] * qr[:, 1:2])
        column = share[:, :TILE].T
        at = 2 * floor_dev
        ar, ai = column[:mode_dev, at : at + 1], column[:mode_dev, at + 1 : at + 2]
        tri = triangle()
        for b in range(blocks):
            cols = slice(b * BLK, (b + 1) * BLK)
            force = force_refs[0][:, cols]
            for ref in force_refs[1:]:
                force = force + ref[:, cols]
            cr = dot_exact_right(force * pr, tri) + ar
            ci = dot_exact_right(force * pi, tri) + ai
            resp_ref[:, cols] = qr * cr - qi * ci
            ar, ai = turned((zr, zi), (cr[:, BLK - 1 :], ci[:, BLK - 1 :]))

    return pl.pallas_call(
        body,
        in_specs=whole(2 * n + 1),
        out_specs=tuple(whole(3)),
        out_shape=(
            jax.ShapeDtypeStruct((mode_dev, time), F32),
            jax.ShapeDtypeStruct((floor_dev, time), F32),
            jax.ShapeDtypeStruct((floor_dev, time), F32),
        ),
        compiler_params=params(),
        name="own_response",
    )(*forces, *shares, tables)


def shifts(x, axis, n):
    return [lax.ppermute(x, axis, [(i, (i + d) % n) for i in range(n)]) for d in range(1, n)]


def on_device(
    pressures,
    tap_area,
    tap_panel,
    tap_floor,
    panel_shape,
    floor_shape,
    mode_order,
    mode_decay,
    mode_freq,
):
    nz = lax.axis_size("taps")
    nc = lax.axis_size("floors")
    nt = lax.axis_size("tm")
    owners = nz * nc
    modes = mode_order.shape[0]
    mode_dev = modes // owners
    time, taps = pressures.shape
    panels = panel_shape.shape[0]
    floors = floor_shape.shape[0]
    floor_dev = floors // owners
    load_scale = (floors / (taps * owners)) ** 0.5
    z, c = lax.axis_index("taps"), lax.axis_index("floors")
    place = jnp.stack([z, c, z * nc + c]).astype(jnp.int32)

    mine = make_tap_sums(panels, floors, taps, time)(
        pressures, tap_panel[None], tap_floor[None], tap_area[None]
    )
    sums = [mine] + shifts(mine, "floors", nc)
    pt, floor_slots, rates = mode_tables(
        mode_order[None], mode_decay[None], mode_freq[None], panel_shape, floor_shape
    )
    forces = slot_forces(place, sums, pt, nz, nc, mode_dev)

    def along(parts):
        return [parts[0]] + [
            lax.ppermute(parts[d], "taps", [(i, (i + d) % nz) for i in range(nz)])
            for d in range(1, nz)
        ]

    got_forces = along(forces)
    motion, ends, qr, qi, tables = partial_states(
        place, sums, pt, rates, floor_slots, mode_dev, floor_dev, nc
    )
    steps = [(i, i + 1) for i in range(nt - 1)]
    enter = jnp.zeros_like(ends)
    for hop in range(nt - 1):
        if hop:
            over = (ends[2:3], ends[3:4])
            for _ in range(time // BLK - 1):
                over = turned(over, (ends[2:3], ends[3:4]))
            re, im = turned(over, (enter[0:1], enter[1:2]))
            passed = ends + jnp.concatenate([re, im, jnp.zeros_like(ends[2:])], axis=0)
        else:
            passed = ends
        enter = lax.ppermute(passed, "tm", steps)
    shares = floor_shares(
        place, motion, ends, enter, qr, qi, floor_slots, sums, nz, nc, floor_dev, mode_dev
    )
    got_shares = along(shares)
    return own_response(got_forces, got_shares, tables, floor_dev, load_scale)


def solution(mesh):
    in_specs = (
        P(("dirs", "tm"), ("taps", "floors")),
        P(("taps", "floors")),
        P(("taps", "floors")),
        P(("taps", "floors")),
        P(),
        P(),
        P(),
        P(),
        P(),
    )
    out_specs = (
        P(("taps", "floors"), ("dirs", "tm")),
        P(("taps", "floors"), ("dirs", "tm")),
        P(("taps", "floors"), ("dirs", "tm")),
    )
    return jax.shard_map(
        on_device, mesh=mesh, in_specs=in_specs, out_specs=out_specs, check_vma=False
    )
```

```python
import jax
import jax.numpy as jnp
from jax import lax
from jax.experimental import pallas as pl
from jax.experimental.pallas import tpu as pltpu
from jax.sharding import PartitionSpec as P

BLK = 256
TILE = 128
BF = jnp.bfloat16
F32 = jnp.float32
NN = (((1,), (0,)), ((), ()))
NT = (((1,), (1,)), ((), ()))
VMEM_LIMIT = 48 * 1024 * 1024


def dot(a, b, dims=NN):
    return lax.dot_general(a, b, dims, preferred_element_type=F32)


def split(x):
    hi = x.astype(BF)
    return hi, (x - hi.astype(F32)).astype(BF)


def dot_exact_left(a, x, dims=NN):
    hi, lo = split(x)
    return dot(a, hi, dims) + dot(a, lo, dims)


def dot_exact_right(x, b, dims=NN):
    hi, lo = split(x)
    return dot(hi, b, dims) + dot(lo, b, dims)


def params():
    return pltpu.CompilerParams(vmem_limit_bytes=VMEM_LIMIT)


def whole(n):
    return [pl.BlockSpec(memory_space=pltpu.VMEM)] * n


def tap_sums(pressures, tap_panel, tap_floor, tap_area, panels, floors):
    time, taps = pressures.shape
    rows = panels + floors
    chunks = time // BLK

    def body(press_hbm, panel_hbm, floor_hbm, area_hbm, sums_ref, press, panel, floor, area, weights, sems):
        small = [
            pltpu.make_async_copy(panel_hbm, panel, sems.at[chunks]),
            pltpu.make_async_copy(floor_hbm, floor, sems.at[chunks + 1]),
            pltpu.make_async_copy(area_hbm, area, sems.at[chunks + 2]),
        ]
        for copy in small:
            copy.start()
        large = []
        for i in range(chunks):
            at = pl.ds(i * BLK, BLK)
            large.append(pltpu.make_async_copy(press_hbm.at[at], press.at[at], sems.at[i]))
            large[i].start()
        for copy in small:
            copy.wait()
        each = area[...].astype(F32).reshape(1, taps)
        ids = lax.broadcasted_iota(jnp.int32, (panels, taps), 0)
        weights[:panels] = jnp.where(ids == panel[...], each, 0.0).astype(BF)
        ids = lax.broadcasted_iota(jnp.int32, (floors, taps), 0)
        weights[panels:] = jnp.where(ids == floor[...], each, 0.0).astype(BF)
        for i in range(chunks):
            at = slice(i * BLK, (i + 1) * BLK)
            large[i].wait()
            sums_ref[:, at] = dot(weights[...], press[at], NT)

    return pl.pallas_call(
        body,
        in_specs=[pl.BlockSpec(memory_space=pltpu.HBM)] * 4,
        out_specs=pl.BlockSpec(memory_space=pltpu.VMEM),
        out_shape=jax.ShapeDtypeStruct((rows, time), F32),
        scratch_shapes=[
            pltpu.VMEM((time, taps), BF),
            pltpu.VMEM((1, taps), jnp.int32),
            pltpu.VMEM((1, taps), jnp.int32),
            pltpu.VMEM(tap_area.shape, BF),
            pltpu.VMEM((rows, taps), BF),
            pltpu.SemaphoreType.DMA((chunks + 3,)),
        ],
        compiler_params=params(),
        name="tap_sums",
    )(pressures, tap_panel[None], tap_floor[None], tap_area)


def mode_tables(place, order, decay, freq, panel_shape, floor_shape, nz, nc):
    modes = order.shape[1]
    panels = panel_shape.shape[0]
    floors = floor_shape.shape[0]
    mode_dev = modes // (nz * nc)
    slots = mode_dev * nz
    bits = BLK.bit_length() - 1
    half = BLK // 2

    def body(place_ref, order_ref, decay_ref, freq_ref, panel_ref, floor_ref, pt_ref, fs_ref, tab_ref, turn_ref, column_ref):
        column_ref[...] = jnp.broadcast_to(order_ref[...].astype(F32), (TILE, modes)).T
        z, c = place_ref[0], place_ref[1]
        picked = []
        for d in range(nz):
            owner = lax.rem(z + d, nz) * nc + c
            picked.append(column_ref[pl.ds(pl.multiple_of(owner * mode_dev, mode_dev), mode_dev), :])
        column = jnp.concatenate(picked, axis=0)[:, :1]
        ids = lax.broadcasted_iota(jnp.int32, (slots, modes), 1).astype(F32)
        pick = jnp.where(column == ids, 1.0, 0.0).astype(BF)
        pt_ref[...] = dot(pick, panel_ref[...], NT).astype(BF)
        fs_ref[...] = dot(floor_ref[...], pick, NT)
        decays, angles = decay_ref[...], freq_ref[...]
        re, im = jnp.cos(angles), jnp.sin(angles)
        rows = [decays]
        square = decays * decays
        loss = 2.0 * jnp.exp(-decays) * decays * (1.0 + square * (1.0 / 6.0 + square * (1.0 / 120.0)))
        rows.append(jnp.sqrt(loss))
        for _ in range(bits + 1):
            rows += [re, im]
            re, im = re * re - im * im, 2.0 * re * im
        rows += [jnp.zeros_like(re)] * (-len(rows) % 16)
        count = len(rows)
        stack = jnp.concatenate(rows, axis=0)
        hi, mid = split(stack)
        low = (stack - hi.astype(F32) - mid.astype(F32)).astype(BF)
        parts = dot(pick, jnp.concatenate([hi, mid, low], axis=0), NT)
        cols = parts[:, :count] + parts[:, count : 2 * count] + parts[:, 2 * count : 3 * count]
        rate, gain = cols[:, 0:1], cols[:, 1:2]
        lane = lax.broadcasted_iota(jnp.int32, (slots, half), 1)
        cos = jnp.where((lane & 1) != 0, cols[:, 2:3], 1.0)
        sin = jnp.where((lane & 1) != 0, cols[:, 3:4], 0.0)
        for b in range(1, bits - 1):
            on = (lane & (1 << b)) != 0
            step = cols[:, 2 + 2 * b : 3 + 2 * b], cols[:, 3 + 2 * b : 4 + 2 * b]
            new_cos, new_sin = turned((cos, sin), step)
            cos, sin = jnp.where(on, new_cos, cos), jnp.where(on, new_sin, sin)
        at = 2 * bits
        far_cos, far_sin = turned((cos, sin), (cols[:, at : at + 1], cols[:, at + 1 : at + 2]))
        steps = rate * lane.astype(F32)
        shrink, grow = jnp.exp(-steps), gain * jnp.exp(steps)
        far_shrink = shrink * jnp.exp(-rate * float(half))
        far_grow = grow * jnp.exp(rate * float(half))
        near, far = slice(0, half), slice(half, BLK)
        tab_ref[0, :, near], tab_ref[0, :, far] = grow * cos, far_grow * far_cos
        tab_ref[1, :, near], tab_ref[1, :, far] = -grow * sin, -far_grow * far_sin
        tab_ref[2, :, near], tab_ref[2, :, far] = shrink * cos, far_shrink * far_cos
        tab_ref[3, :, near], tab_ref[3, :, far] = shrink * sin, far_shrink * far_sin
        fade = jnp.exp(-rate * float(BLK))
        turn_ref[...] = fade * cols[:, at + 2 : at + 4]

    return pl.pallas_call(
        body,
        in_specs=[pl.BlockSpec(memory_space=pltpu.SMEM)] + whole(5),
        out_specs=tuple(whole(4)),
        out_shape=(
            jax.ShapeDtypeStruct((slots, panels), BF),
            jax.ShapeDtypeStruct((floors, slots), F32),
            jax.ShapeDtypeStruct((4, slots, BLK), F32),
            jax.ShapeDtypeStruct((slots, 2), F32),
        ),
        scratch_shapes=[pltpu.VMEM((modes, TILE), F32)],
        compiler_params=params(),
        name="mode_tables",
    )(place, order, decay, freq, panel_shape, floor_shape)


def slot_forces(sums, pt, nz):
    slots, panels = pt.shape
    time = sums[0].shape[1]
    nc = len(sums)
    mode_dev = slots // nz

    def body(*refs):
        sum_refs, pt_ref, out_refs = refs[:nc], refs[nc], refs[nc + 1 :]
        left = pt_ref[...]
        for b in range(time // BLK):
            cols = slice(b * BLK, (b + 1) * BLK)
            total = sum_refs[0][:panels, cols]
            for ref in sum_refs[1:]:
                total = total + ref[:panels, cols]
            forces = dot_exact_left(left, total)
            for d in range(nz):
                out_refs[d][:, cols] = forces[d * mode_dev : (d + 1) * mode_dev]

    return pl.pallas_call(
        body,
        in_specs=whole(nc + 1),
        out_specs=whole(nz),
        out_shape=[jax.ShapeDtypeStruct((mode_dev, time), F32)] * nz,
        compiler_params=params(),
        name="slot_forces",
    )(*sums, pt)


def triangle():
    row = lax.broadcasted_iota(jnp.int32, (BLK, BLK), 0)
    col = lax.broadcasted_iota(jnp.int32, (BLK, BLK), 1)
    return jnp.where(row <= col, 1.0, 0.0).astype(BF)


def turned(a, b):
    return (a[0] * b[0] - a[1] * b[1], a[0] * b[1] + a[1] * b[0])


def partial_states(forces, tables, turns, floor_slots):
    nz = len(forces)
    mode_dev, time = forces[0].shape
    slots = turns.shape[0]
    floors = floor_slots.shape[0]
    blocks = time // BLK

    def body(*refs):
        force_refs = refs[:nz]
        tab_ref, turn_ref, fs_ref, motion_ref, ends_ref, all_ref = refs[nz:]
        for d in range(nz):
            all_ref[d * mode_dev : (d + 1) * mode_dev] = force_refs[d][...]
        tri = triangle()
        pad = jnp.zeros((TILE, TILE - 4), F32)
        for i in range(slots // TILE):
            at = slice(i * TILE, (i + 1) * TILE)
            pr, pi, qr, qi = tab_ref[0, at], tab_ref[1, at], tab_ref[2, at], tab_ref[3, at]
            turn = turn_ref[at, 0:1], turn_ref[at, 1:2]
            here = fs_ref[:, at].astype(BF)
            ar = jnp.zeros((TILE, 1), F32)
            ai = jnp.zeros((TILE, 1), F32)
            for b in range(blocks):
                cols = slice(b * BLK, (b + 1) * BLK)
                force = all_ref[at, cols]
                cr = dot_exact_right(force * pr, tri) + ar
                ci = dot_exact_right(force * pi, tri) + ai
                part = dot_exact_left(here, qr * cr - qi * ci)
                motion_ref[:, cols] = part if i == 0 else motion_ref[:, cols] + part
                ar, ai = turned(turn, (cr[:, BLK - 1 :], ci[:, BLK - 1 :]))
            ends_ref[:, at] = jnp.concatenate([ar, ai, *turn, pad], axis=1).T[:8]

    return pl.pallas_call(
        body,
        in_specs=whole(nz + 3),
        out_specs=tuple(whole(2)),
        out_shape=(
            jax.ShapeDtypeStruct((floors, time), F32),
            jax.ShapeDtypeStruct((8, slots), F32),
        ),
        scratch_shapes=[pltpu.VMEM((slots, time), F32)],
        compiler_params=params(),
        name="partial_states",
    )(*forces, tables, turns, floor_slots)


def floor_motion_share(motion, ends, enter, tables, floor_slots):
    floors, time = motion.shape
    blocks = time // BLK

    def body(motion_ref, ends_ref, enter_ref, tab_ref, fs_ref, out_ref):
        shape = fs_ref[...]
        turn = (ends_ref[2:3, :], ends_ref[3:4, :])
        state = (enter_ref[0:1, :], enter_ref[1:2, :])
        left_re, left_im = [], []
        for b in range(blocks):
            left_re.append(shape * state[0])
            left_im.append(shape * state[1])
            state = turned(turn, state)
        qr_hi, qr_lo = split(tab_ref[2])
        qi_hi, qi_lo = split(tab_ref[3])
        re_hi, re_lo = split(jnp.concatenate(left_re, axis=0))
        im_hi, im_lo = split(jnp.concatenate(left_im, axis=0))
        free = dot(re_hi, qr_hi) + dot(re_hi, qr_lo) + dot(re_lo, qr_hi)
        free = free - (dot(im_hi, qi_hi) + dot(im_hi, qi_lo) + dot(im_lo, qi_hi))
        for b in range(blocks):
            cols = slice(b * BLK, (b + 1) * BLK)
            out_ref[:, cols] = motion_ref[:, cols] + free[b * floors : (b + 1) * floors]

    return pl.pallas_call(
        body,
        in_specs=whole(5),
        out_specs=whole(1)[0],
        out_shape=jax.ShapeDtypeStruct((floors, time), F32),
        compiler_params=params(),
        name="floor_motion_share",
    )(motion, ends, enter, tables, floor_slots)


def owner_shares(place, motions, sums, enter, nz, floor_dev, mode_dev):
    nc = len(sums)
    floors, time = motions[0].shape
    rows = -(-(2 * floor_dev + 2) // 8) * 8
    load_at = sums[0].shape[0] - floors
    owners = nz * nc

    def body(place_ref, *refs):
        motion_refs, sum_refs, enter_ref = refs[:nc], refs[nc : 2 * nc], refs[2 * nc]
        out_refs, motion_all, load_all = refs[2 * nc + 1 : 2 * nc + 1 + nz], refs[-2], refs[-1]
        z, c = place_ref[0], place_ref[1]
        motion = motion_refs[0][...]
        load = sum_refs[0][load_at:]
        for i in range(1, nc):
            motion = motion + motion_refs[i][...]
            load = load + sum_refs[i][load_at:]
        for o in range(owners):
            motion_all[o] = motion[o * floor_dev : (o + 1) * floor_dev]
            load_all[o] = load[o * floor_dev : (o + 1) * floor_dev]
        for d in range(nz):
            owner = lax.rem(z + d, nz) * nc + c
            out = out_refs[d]
            out[...] = jnp.zeros_like(out)
            out[:floor_dev] = motion_all[owner]
            out[floor_dev : 2 * floor_dev] = load_all[owner]
            at = slice(d * mode_dev, (d + 1) * mode_dev)
            out[2 * floor_dev : 2 * floor_dev + 2, :mode_dev] = enter_ref[0:2, at]

    return pl.pallas_call(
        body,
        in_specs=[pl.BlockSpec(memory_space=pltpu.SMEM)] + whole(2 * nc + 1),
        out_specs=whole(nz),
        out_shape=[jax.ShapeDtypeStruct((rows, time), F32)] * nz,
        scratch_shapes=[pltpu.VMEM((owners, floor_dev, time), F32)] * 2,
        compiler_params=params(),
        name="owner_shares",
    )(place, *motions, *sums, enter)


def own_response(forces, shares, tables, turns, floor_dev, load_scale):
    mode_dev, time = forces[0].shape
    n = len(forces)
    blocks = time // BLK

    def body(*refs):
        force_refs, share_refs = refs[:n], refs[n : 2 * n]
        tab_ref, turn_ref, resp_ref, motion_ref, load_ref = refs[2 * n :]
        share = share_refs[0][...]
        for ref in share_refs[1:]:
            share = share + ref[...]
        motion_ref[...] = share[:floor_dev]
        load_ref[...] = share[floor_dev : 2 * floor_dev] * load_scale
        pr, pi, qr, qi = (tab_ref[i, :mode_dev] for i in range(4))
        turn = turn_ref[:mode_dev, 0:1], turn_ref[:mode_dev, 1:2]
        column = share[:, :TILE].T
        at = 2 * floor_dev
        ar, ai = column[:mode_dev, at : at + 1], column[:mode_dev, at + 1 : at + 2]
        tri = triangle()
        for b in range(blocks):
            cols = slice(b * BLK, (b + 1) * BLK)
            force = force_refs[0][:, cols]
            for ref in force_refs[1:]:
                force = force + ref[:, cols]
            cr = dot_exact_right(force * pr, tri) + ar
            ci = dot_exact_right(force * pi, tri) + ai
            resp_ref[:, cols] = qr * cr - qi * ci
            ar, ai = turned(turn, (cr[:, BLK - 1 :], ci[:, BLK - 1 :]))

    return pl.pallas_call(
        body,
        in_specs=whole(2 * n + 2),
        out_specs=tuple(whole(3)),
        out_shape=(
            jax.ShapeDtypeStruct((mode_dev, time), F32),
            jax.ShapeDtypeStruct((floor_dev, time), F32),
            jax.ShapeDtypeStruct((floor_dev, time), F32),
        ),
        compiler_params=params(),
        name="own_response",
    )(*forces, *shares, tables, turns)


def shifts(x, axis, n):
    return [lax.ppermute(x, axis, [(i, (i + d) % n) for i in range(n)]) for d in range(1, n)]


def along(parts, n):
    return [parts[0]] + [
        lax.ppermute(parts[d], "taps", [(i, (i + d) % n) for i in range(n)]) for d in range(1, n)
    ]


def on_device(
    pressures,
    tap_area,
    tap_panel,
    tap_floor,
    panel_shape,
    floor_shape,
    mode_order,
    mode_decay,
    mode_freq,
):
    nz = lax.axis_size("taps")
    nc = lax.axis_size("floors")
    nt = lax.axis_size("tm")
    owners = nz * nc
    modes = mode_order.shape[0]
    mode_dev = modes // owners
    time, taps = pressures.shape
    panels = panel_shape.shape[0]
    floors = floor_shape.shape[0]
    floor_dev = floors // owners
    load_scale = (floors / (taps * owners)) ** 0.5
    z, c = lax.axis_index("taps"), lax.axis_index("floors")
    place = jnp.stack([z, c, z * nc + c]).astype(jnp.int32)

    mine = tap_sums(pressures, tap_panel, tap_floor, tap_area, panels, floors)
    sums = [mine] + shifts(mine, "floors", nc)
    pt, floor_slots, tables, turns = mode_tables(
        place, mode_order[None], mode_decay[None], mode_freq[None], panel_shape, floor_shape, nz, nc
    )
    forces = slot_forces(sums, pt, nz)
    got_forces = along(forces, nz)
    motion, ends = partial_states(forces, tables, turns, floor_slots)
    enter = jnp.zeros_like(ends)
    for hop in range(nt - 1):
        passed = ends
        if hop:
            turn = (ends[2:3], ends[3:4])
            over = turn
            for _ in range(time // BLK - 1):
                over = turned(over, turn)
            passed = ends + jnp.concatenate([*turned(over, (enter[0:1], enter[1:2])), jnp.zeros_like(ends[2:])])
        enter = lax.ppermute(passed, "tm", [(i, (i + 1) % nt) for i in range(nt)])
        enter = jnp.where(lax.axis_index("tm") > 0, enter, 0.0)
    motion = floor_motion_share(motion, ends, enter, tables, floor_slots)
    motions = [motion] + shifts(motion, "floors", nc)
    shares = owner_shares(place, motions, sums, enter, nz, floor_dev, mode_dev)
    return own_response(
        got_forces, along(shares, nz), tables, turns, floor_dev, load_scale
    )


def solution(mesh):
    in_specs = (
        P(("dirs", "tm"), ("taps", "floors")),
        P(("taps", "floors")),
        P(("taps", "floors")),
        P(("taps", "floors")),
        P(),
        P(),
        P(),
        P(),
        P(),
    )
    out_specs = (
        P(("taps", "floors"), ("dirs", "tm")),
        P(("taps", "floors"), ("dirs", "tm")),
        P(("taps", "floors"), ("dirs", "tm")),
    )
    return jax.shard_map(
        on_device, mesh=mesh, in_specs=in_specs, out_specs=out_specs, check_vma=False
    )
```

```python
import jax
import jax.numpy as jnp
from jax import lax
from jax.experimental import pallas as pl
from jax.experimental.pallas import tpu as pltpu
from jax.sharding import PartitionSpec as P

BLK = 256
TILE = 128
BF = jnp.bfloat16
F32 = jnp.float32
NN = (((1,), (0,)), ((), ()))
NT = (((1,), (1,)), ((), ()))
VMEM_LIMIT = 16 * 1024 * 1024


def dot(a, b, dims=NN):
    return lax.dot_general(a, b, dims, preferred_element_type=F32)


def split(x):
    hi = x.astype(BF)
    return hi, (x - hi.astype(F32)).astype(BF)


def dot_exact_left(a, x, dims=NN):
    hi, lo = split(x)
    return dot(a, hi, dims) + dot(a, lo, dims)


def dot_exact_right(x, b, dims=NN):
    hi, lo = split(x)
    return dot(hi, b, dims) + dot(lo, b, dims)


def params():
    return pltpu.CompilerParams(vmem_limit_bytes=VMEM_LIMIT)


def in_hbm(x):
    return pltpu.with_memory_space_constraint(x, pltpu.HBM)


def cost(us):
    return pl.CostEstimate(flops=int(us * 5e8), bytes_accessed=int(us * 2e6), transcendentals=0)


def whole(n):
    return [pl.BlockSpec(memory_space=pltpu.VMEM)] * n


def tap_sums(pressures, tap_panel, tap_floor, tap_area, others, panels, floors):
    time, taps = pressures.shape
    rows = panels + floors
    chunks = 2 if time % (2 * BLK) == 0 else 1
    span = time // chunks
    n = len(others)
    given = (tap_panel, tap_floor, tap_area)

    def body(press_hbm, *refs):
        from_refs, sums_ref, kept = refs[: n + 3], refs[n + 3], refs[n + 4 : 2 * n + 4]
        press, panel, floor, area, weights, sems = refs[2 * n + 4 :]
        small = [
            pltpu.make_async_copy(a, b, sems.at[chunks + i])
            for i, (a, b) in enumerate(zip(from_refs, (panel, floor, area, *kept)))
        ]
        large = []
        for i in range(chunks):
            at = pl.ds(i * span, span)
            large.append(pltpu.make_async_copy(press_hbm.at[at], press.at[at], sems.at[i]))
        for copy in [*small[:3], *large, *small[3:]]:
            copy.start()
        for copy in small[:3]:
            copy.wait()
        each = jnp.broadcast_to(area[...].astype(F32).reshape(1, taps), (16, taps))
        row = lax.broadcasted_iota(jnp.int32, (16, taps), 0)
        for ids, first, count in ((panel, 0, panels), (floor, panels, floors)):
            at = jnp.broadcast_to(ids[...], (16, taps)) - row
            for r in range(0, count, 16):
                weights[first + r : first + r + 16] = jnp.where(at == r, each, 0.0).astype(BF)
        for i in range(chunks):
            at = slice(i * span, (i + 1) * span)
            large[i].wait()
            sums_ref[:, at] = dot(weights[...], press[at], NT)
        for copy in small[3:]:
            copy.wait()

    out = pl.pallas_call(
        body,
        in_specs=[pl.BlockSpec(memory_space=pltpu.HBM)] * (n + 4),
        out_specs=tuple(whole(n + 1)),
        out_shape=(jax.ShapeDtypeStruct((rows, time), F32), *(jax.ShapeDtypeStruct(x.shape, x.dtype) for x in others)),
        scratch_shapes=[
            pltpu.VMEM((time, taps), BF),
            *(pltpu.VMEM(x.shape, x.dtype) for x in given),
            pltpu.VMEM((rows, taps), BF),
            pltpu.SemaphoreType.DMA((chunks + n + 3,)),
        ],
        compiler_params=params(),
        cost_estimate=cost(3),
        name="tap_sums",
    )(in_hbm(pressures), *(in_hbm(x) for x in given), *(in_hbm(x) for x in others))
    return out[0], out[1:]


def mode_tables(order, decay, freq, panel_shape, floor_shape, nz, nc):
    modes = order.shape[1]
    panels = panel_shape.shape[0]
    floors = floor_shape.shape[0]
    mode_dev = modes // (nz * nc)
    slots = mode_dev * nz
    bits = BLK.bit_length() - 1
    half = BLK // 2

    def body(*refs):
        order_ref, decay_ref, freq_ref, panel_ref, floor_ref = refs[:5]
        pt_ref, fs_ref, tab_ref, turn_ref, own_ref, column_ref = refs[5:]
        column_ref[...] = jnp.broadcast_to(order_ref[...].astype(F32), (TILE, modes)).T
        z, c = lax.axis_index("taps"), lax.axis_index("floors")
        picked = []
        for d in range(nz):
            owner = lax.rem(z + d, nz) * nc + c
            picked.append(column_ref[pl.ds(pl.multiple_of(owner * mode_dev, mode_dev), mode_dev), :])
        column = jnp.concatenate(picked, axis=0)[:, :1]
        ids = lax.broadcasted_iota(jnp.int32, (slots, modes), 1).astype(F32)
        pick = jnp.where(column == ids, 1.0, 0.0).astype(BF)
        pt_ref[...] = dot(pick, panel_ref[...], NT).astype(BF)
        fs_ref[...] = dot(floor_ref[...], pick, NT)
        decays, angles = decay_ref[...], freq_ref[...]
        re, im = jnp.cos(angles), jnp.sin(angles)
        rows = [decays]
        square = decays * decays
        loss = 2.0 * jnp.exp(-decays) * decays * (1.0 + square * (1.0 / 6.0 + square * (1.0 / 120.0)))
        rows.append(jnp.sqrt(loss))
        for _ in range(bits + 1):
            rows += [re, im]
            re, im = re * re - im * im, 2.0 * re * im
        rows += [jnp.zeros_like(re)] * (-len(rows) % 16)
        count = len(rows)
        stack = jnp.concatenate(rows, axis=0)
        hi, mid = split(stack)
        low = (stack - hi.astype(F32) - mid.astype(F32)).astype(BF)
        parts = dot(pick, jnp.concatenate([hi, mid, low], axis=0), NT)
        cols = parts[:, :count] + parts[:, count : 2 * count] + parts[:, 2 * count : 3 * count]
        rate, gain = cols[:, 0:1], cols[:, 1:2]
        lane = lax.broadcasted_iota(jnp.int32, (slots, half), 1)
        cos = jnp.where((lane & 1) != 0, cols[:, 2:3], 1.0)
        sin = jnp.where((lane & 1) != 0, cols[:, 3:4], 0.0)
        for b in range(1, bits - 1):
            on = (lane & (1 << b)) != 0
            step = cols[:, 2 + 2 * b : 3 + 2 * b], cols[:, 3 + 2 * b : 4 + 2 * b]
            new_cos, new_sin = turned((cos, sin), step)
            cos, sin = jnp.where(on, new_cos, cos), jnp.where(on, new_sin, sin)
        at = 2 * bits
        far_cos, far_sin = turned((cos, sin), (cols[:, at : at + 1], cols[:, at + 1 : at + 2]))
        steps = rate * lane.astype(F32)
        shrink, grow = jnp.exp(-steps), gain * jnp.exp(steps)
        far_shrink = shrink * jnp.exp(-rate * float(half))
        far_grow = grow * jnp.exp(rate * float(half))
        near, far = slice(0, half), slice(half, BLK)
        tab_ref[0, :, near], tab_ref[0, :, far] = grow * cos, far_grow * far_cos
        tab_ref[1, :, near], tab_ref[1, :, far] = -grow * sin, -far_grow * far_sin
        tab_ref[2, :, near], tab_ref[2, :, far] = shrink * cos, far_shrink * far_cos
        tab_ref[3, :, near], tab_ref[3, :, far] = shrink * sin, far_shrink * far_sin
        fade = jnp.exp(-rate * float(BLK))
        turn_ref[...] = fade * cols[:, at + 2 : at + 4]
        own_ref[...] = tab_ref[:, :mode_dev]

    return pl.pallas_call(
        body,
        in_specs=whole(5),
        out_specs=tuple(whole(5)),
        out_shape=(
            jax.ShapeDtypeStruct((slots, panels), BF),
            jax.ShapeDtypeStruct((floors, slots), F32),
            jax.ShapeDtypeStruct((4, slots, BLK), F32),
            jax.ShapeDtypeStruct((slots, 2), F32),
            jax.ShapeDtypeStruct((4, mode_dev, BLK), F32),
        ),
        scratch_shapes=[pltpu.VMEM((modes, TILE), F32)],
        compiler_params=params(),
        cost_estimate=cost(2),
        name="mode_tables",
    )(order, decay, freq, panel_shape, floor_shape)


def slot_forces(sums, pt, nz):
    slots, panels = pt.shape
    time = sums[0].shape[1]
    nc = len(sums)
    mode_dev = slots // nz

    def body(*refs):
        sum_refs, pt_ref, out_refs, load_ref = refs[:nc], refs[nc], refs[nc + 1 : -1], refs[-1]
        left = pt_ref[...]
        load = sum_refs[0][panels:]
        for ref in sum_refs[1:]:
            load = load + ref[panels:]
        load_ref[...] = load
        for b in range(time // BLK):
            cols = slice(b * BLK, (b + 1) * BLK)
            total = sum_refs[0][:panels, cols]
            for ref in sum_refs[1:]:
                total = total + ref[:panels, cols]
            forces = dot_exact_left(left, total)
            for d in range(nz):
                out_refs[d][:, cols] = forces[d * mode_dev : (d + 1) * mode_dev]

    out = pl.pallas_call(
        body,
        in_specs=whole(nc + 1),
        out_specs=whole(nz + 1),
        out_shape=[jax.ShapeDtypeStruct((mode_dev, time), F32)] * nz
        + [jax.ShapeDtypeStruct((sums[0].shape[0] - panels, time), F32)],
        compiler_params=params(),
        cost_estimate=cost(1),
        name="slot_forces",
    )(*sums, pt)
    return out[:nz], out[nz]


def triangle():
    row = lax.broadcasted_iota(jnp.int32, (BLK, BLK), 0)
    col = lax.broadcasted_iota(jnp.int32, (BLK, BLK), 1)
    return jnp.where(row <= col, 1.0, 0.0).astype(BF)


def turned(a, b):
    return (a[0] * b[0] - a[1] * b[1], a[0] * b[1] + a[1] * b[0])


def partial_states(forces, tables, turns, floor_slots):
    nz = len(forces)
    mode_dev, time = forces[0].shape
    slots = turns.shape[0]
    floors = floor_slots.shape[0]
    blocks = time // BLK

    def body(*refs):
        force_refs = refs[:nz]
        tab_ref, turn_ref, fs_ref, motion_ref, ends_ref, all_ref = refs[nz:]
        for d in range(nz):
            all_ref[d * mode_dev : (d + 1) * mode_dev] = force_refs[d][...]
        tri = triangle()
        pad = jnp.zeros((TILE, TILE - 4), F32)
        for i in range(slots // TILE):
            at = slice(i * TILE, (i + 1) * TILE)
            pr, pi, qr, qi = tab_ref[0, at], tab_ref[1, at], tab_ref[2, at], tab_ref[3, at]
            turn = turn_ref[at, 0:1], turn_ref[at, 1:2]
            here = fs_ref[:, at].astype(BF)
            ar = jnp.zeros((TILE, 1), F32)
            ai = jnp.zeros((TILE, 1), F32)
            for b in range(blocks):
                cols = slice(b * BLK, (b + 1) * BLK)
                force = all_ref[at, cols]
                cr = dot_exact_right(force * pr, tri) + ar
                ci = dot_exact_right(force * pi, tri) + ai
                part = dot_exact_left(here, qr * cr - qi * ci)
                motion_ref[:, cols] = part if i == 0 else motion_ref[:, cols] + part
                ar, ai = turned(turn, (cr[:, BLK - 1 :], ci[:, BLK - 1 :]))
            ends_ref[:, at] = jnp.concatenate([ar, ai, *turn, pad], axis=1).T[:8]

    return pl.pallas_call(
        body,
        in_specs=whole(nz + 3),
        out_specs=tuple(whole(2)),
        out_shape=(
            jax.ShapeDtypeStruct((floors, time), F32),
            jax.ShapeDtypeStruct((8, slots), F32),
        ),
        scratch_shapes=[pltpu.VMEM((slots, time), F32)],
        compiler_params=params(),
        cost_estimate=cost(3),
        name="partial_states",
    )(*forces, tables, turns, floor_slots)


def floor_shares(motion, ends, enter, tables, floor_slots, forces):
    floors, time = motion.shape
    blocks = time // BLK

    def body(motion_ref, ends_ref, enter_ref, tab_ref, fs_ref, *refs):
        force_refs, out_ref, force_ref = refs[:-2], refs[-2], refs[-1]
        force = force_refs[0][...]
        for ref in force_refs[1:]:
            force = force + ref[...]
        force_ref[...] = force
        shape = fs_ref[...]
        turn = (ends_ref[2:3, :], ends_ref[3:4, :])
        later = lax.axis_index("tm") > 0
        state = tuple(jnp.where(later, enter_ref[i : i + 1, :], 0.0) for i in (0, 1))
        left_re, left_im = [], []
        for b in range(blocks):
            left_re.append(shape * state[0])
            left_im.append(shape * state[1])
            state = turned(turn, state)
        qr_hi, qr_lo = split(tab_ref[2])
        qi_hi, qi_lo = split(tab_ref[3])
        re_hi, re_lo = split(jnp.concatenate(left_re, axis=0))
        im_hi, im_lo = split(jnp.concatenate(left_im, axis=0))
        free = dot(re_hi, qr_hi) + dot(re_hi, qr_lo) + dot(re_lo, qr_hi)
        free = free - (dot(im_hi, qi_hi) + dot(im_hi, qi_lo) + dot(im_lo, qi_hi))
        for b in range(blocks):
            cols = slice(b * BLK, (b + 1) * BLK)
            out_ref[:, cols] = motion_ref[:, cols] + free[b * floors : (b + 1) * floors]

    return pl.pallas_call(
        body,
        in_specs=whole(5 + len(forces)),
        out_specs=tuple(whole(2)),
        out_shape=(jax.ShapeDtypeStruct((floors, time), F32), jax.ShapeDtypeStruct(forces[0].shape, F32)),
        compiler_params=params(),
        cost_estimate=cost(1),
        name="floor_shares",
    )(motion, ends, enter, tables, floor_slots, *forces)


def owner_shares(motions, load, enter, nz, floor_dev, mode_dev):
    nc = len(motions)
    floors, time = motions[0].shape
    rows = -(-(2 * floor_dev + 2) // 8) * 8
    owners = nz * nc

    def body(*refs):
        motion_refs, load_ref, enter_ref = refs[:nc], refs[nc], refs[nc + 1]
        out_refs, motion_all, load_all = refs[nc + 2 : nc + 2 + nz], refs[-2], refs[-1]
        z, c = lax.axis_index("taps"), lax.axis_index("floors")
        later = lax.axis_index("tm") > 0
        motion = motion_refs[0][...]
        for ref in motion_refs[1:]:
            motion = motion + ref[...]
        for o in range(owners):
            at = slice(o * floor_dev, (o + 1) * floor_dev)
            motion_all[o] = motion[at]
            load_all[o] = load_ref[at]
        for d in range(nz):
            owner = lax.rem(z + d, nz) * nc + c
            out = out_refs[d]
            out[...] = jnp.zeros_like(out)
            out[:floor_dev] = motion_all[owner]
            out[floor_dev : 2 * floor_dev] = load_all[owner]
            at = slice(d * mode_dev, (d + 1) * mode_dev)
            out[2 * floor_dev : 2 * floor_dev + 2, :mode_dev] = jnp.where(later, enter_ref[0:2, at], 0.0)

    return pl.pallas_call(
        body,
        in_specs=whole(nc + 2),
        out_specs=whole(nz),
        out_shape=[jax.ShapeDtypeStruct((rows, time), F32)] * nz,
        scratch_shapes=[pltpu.VMEM((owners, floor_dev, time), F32)] * 2,
        compiler_params=params(),
        cost_estimate=cost(1),
        name="owner_shares",
    )(*motions, load, enter)


def own_response(forces, shares, tables, turns, floor_dev, load_scale):
    mode_dev, time = forces[0].shape
    n, m = len(forces), len(shares)
    blocks = time // BLK

    def body(*refs):
        force_refs, share_refs = refs[:n], refs[n : n + m]
        tab_ref, turn_ref, resp_ref, motion_ref, load_ref = refs[n + m :]
        share = share_refs[0][...]
        for ref in share_refs[1:]:
            share = share + ref[...]
        motion_ref[...] = share[:floor_dev]
        load_ref[...] = share[floor_dev : 2 * floor_dev] * load_scale
        pr, pi, qr, qi = (tab_ref[i] for i in range(4))
        turn = turn_ref[:mode_dev, 0:1], turn_ref[:mode_dev, 1:2]
        column = share[:, :TILE].T
        at = 2 * floor_dev
        ar, ai = column[:mode_dev, at : at + 1], column[:mode_dev, at + 1 : at + 2]
        tri = triangle()
        for b in range(blocks):
            cols = slice(b * BLK, (b + 1) * BLK)
            force = force_refs[0][:, cols]
            for ref in force_refs[1:]:
                force = force + ref[:, cols]
            cr = dot_exact_right(force * pr, tri) + ar
            ci = dot_exact_right(force * pi, tri) + ai
            resp_ref[:, cols] = qr * cr - qi * ci
            ar, ai = turned(turn, (cr[:, BLK - 1 :], ci[:, BLK - 1 :]))

    return pl.pallas_call(
        body,
        in_specs=whole(n + m + 2),
        out_specs=tuple(whole(3)),
        out_shape=(
            jax.ShapeDtypeStruct((mode_dev, time), F32),
            jax.ShapeDtypeStruct((floor_dev, time), F32),
            jax.ShapeDtypeStruct((floor_dev, time), F32),
        ),
        compiler_params=params(),
        cost_estimate=cost(2),
        name="own_response",
    )(*forces, *shares, tables, turns)


def shifts(x, axis, n):
    return [lax.ppermute(x, axis, [(i, (i + d) % n) for i in range(n)]) for d in range(1, n)]


def along(parts, n):
    return [parts[0]] + [
        lax.ppermute(parts[d], "taps", [(i, (i + d) % n) for i in range(n)]) for d in range(1, n)
    ]


def on_device(
    pressures,
    tap_area,
    tap_panel,
    tap_floor,
    panel_shape,
    floor_shape,
    mode_order,
    mode_decay,
    mode_freq,
):
    nz = lax.axis_size("taps")
    nc = lax.axis_size("floors")
    nt = lax.axis_size("tm")
    owners = nz * nc
    modes = mode_order.shape[0]
    mode_dev = modes // owners
    time, taps = pressures.shape
    panels = panel_shape.shape[0]
    floors = floor_shape.shape[0]
    floor_dev = floors // owners
    load_scale = (floors / (taps * owners)) ** 0.5

    mine, kept = tap_sums(
        pressures,
        tap_panel[None],
        tap_floor[None],
        tap_area,
        (mode_order[None], mode_decay[None], mode_freq[None], panel_shape, floor_shape),
        panels,
        floors,
    )
    sums = [mine] + shifts(mine, "floors", nc)
    pt, floor_slots, tables, turns, own = mode_tables(*kept, nz, nc)
    forces, load = slot_forces(sums, pt, nz)
    got_forces = along(forces, nz)
    motion, ends = partial_states(forces, tables, turns, floor_slots)
    enter = jnp.zeros_like(ends)
    for hop in range(nt - 1):
        passed = ends
        if hop:
            turn = (ends[2:3], ends[3:4])
            over = turn
            for _ in range(time // BLK - 1):
                over = turned(over, turn)
            enter = jnp.where(lax.axis_index("tm") > 0, enter, 0.0)
            passed = ends + jnp.concatenate(
                [*turned(over, (enter[0:1], enter[1:2])), jnp.zeros_like(ends[2:])]
            )
        enter = lax.ppermute(passed, "tm", [(i, (i + 1) % nt) for i in range(nt)])
        enter = jnp.where(lax.axis_index("tm") > 0, enter, 0.0)
    early = [x for d, x in enumerate(got_forces) if d != nz // 2]
    motion, force = floor_shares(motion, ends, enter, tables, floor_slots, early)
    got_forces = [force, got_forces[nz // 2]]
    motions = [motion] + shifts(motion, "floors", nc)
    shares = owner_shares(motions, load, enter, nz, floor_dev, mode_dev)
    return own_response(
        got_forces, along(shares, nz), own, turns, floor_dev, load_scale
    )


def solution(mesh):
    in_specs = (
        P(("dirs", "tm"), ("taps", "floors")),
        P(("taps", "floors")),
        P(("taps", "floors")),
        P(("taps", "floors")),
        P(),
        P(),
        P(),
        P(),
        P(),
    )
    out_specs = (
        P(("taps", "floors"), ("dirs", "tm")),
        P(("taps", "floors"), ("dirs", "tm")),
        P(("taps", "floors"), ("dirs", "tm")),
    )
    return jax.shard_map(
        on_device, mesh=mesh, in_specs=in_specs, out_specs=out_specs, check_vma=False
    )
```

```python
import jax
import jax.numpy as jnp
from jax import lax
from jax.experimental import pallas as pl
from jax.experimental.pallas import tpu as pltpu
from jax.sharding import PartitionSpec as P

BLK = 256
PAIRED = 4
TILE = 128
BF = jnp.bfloat16
F32 = jnp.float32
NN = (((1,), (0,)), ((), ()))
NT = (((1,), (1,)), ((), ()))
VMEM_LIMIT = 16 * 1024 * 1024


def dot(a, b, dims=NN):
    return lax.dot_general(a, b, dims, preferred_element_type=F32)


def split(x):
    hi = x.astype(BF)
    return hi, (x - hi.astype(F32)).astype(BF)


def dot_exact_left(a, x, dims=NN):
    hi, lo = split(x)
    return dot(a, hi, dims) + dot(a, lo, dims)


def dot_exact_right(x, b, dims=NN):
    hi, lo = split(x)
    return dot(hi, b, dims) + dot(lo, b, dims)


def params():
    return pltpu.CompilerParams(vmem_limit_bytes=VMEM_LIMIT)


def in_hbm(x):
    return pltpu.with_memory_space_constraint(x, pltpu.HBM)


def cost(us):
    return pl.CostEstimate(flops=int(us * 5e8), bytes_accessed=int(us * 2e6), transcendentals=0)


def whole(n):
    return [pl.BlockSpec(memory_space=pltpu.VMEM)] * n


def tap_sums(pressures, tap_panel, tap_floor, tap_area, others, panels, floors):
    time, taps = pressures.shape
    rows = panels + floors
    chunks = 2 if time % (2 * BLK) == 0 else 1
    span = time // chunks
    n = len(others)
    given = (tap_panel, tap_floor, tap_area)

    def body(press_hbm, *refs):
        from_refs, sums_refs, kept = refs[: n + 3], refs[n + 3 : n + 3 + chunks], refs[n + 3 + chunks : -6]
        press, panel, floor, area, weights, sems = refs[-6:]
        small = [
            pltpu.make_async_copy(a, b, sems.at[chunks + i])
            for i, (a, b) in enumerate(zip(from_refs, (panel, floor, area, *kept)))
        ]
        large = []
        for i in range(chunks):
            at = pl.ds(i * span, span)
            large.append(pltpu.make_async_copy(press_hbm.at[at], press.at[at], sems.at[i]))
        for copy in [*small[:3], *large, *small[3:]]:
            copy.start()
        for copy in small[:3]:
            copy.wait()
        each = jnp.broadcast_to(area[...].astype(F32).reshape(1, taps), (16, taps))
        row = lax.broadcasted_iota(jnp.int32, (16, taps), 0)
        for ids, first, count in ((panel, 0, panels), (floor, panels, floors)):
            at = jnp.broadcast_to(ids[...], (16, taps)) - row
            for r in range(0, count, 16):
                weights[first + r : first + r + 16] = jnp.where(at == r, each, 0.0).astype(BF)
        for i in range(chunks):
            at = slice(i * span, (i + 1) * span)
            large[i].wait()
            sums_refs[i][...] = dot(weights[...], press[at], NT)
        for copy in small[3:]:
            copy.wait()

    out = pl.pallas_call(
        body,
        in_specs=[pl.BlockSpec(memory_space=pltpu.HBM)] * (n + 4),
        out_specs=tuple(whole(n + chunks)),
        out_shape=(*[jax.ShapeDtypeStruct((rows, span), F32)] * chunks, *(jax.ShapeDtypeStruct(x.shape, x.dtype) for x in others)),
        scratch_shapes=[
            pltpu.VMEM((time, taps), BF),
            *(pltpu.VMEM(x.shape, x.dtype) for x in given),
            pltpu.VMEM((rows, taps), BF),
            pltpu.SemaphoreType.DMA((chunks + n + 3,)),
        ],
        compiler_params=params(),
        cost_estimate=cost(3),
        name="tap_sums",
    )(in_hbm(pressures), *(in_hbm(x) for x in given), *(in_hbm(x) for x in others))
    return out[:chunks], out[chunks:]


def placed(z, nz):
    if nz != PAIRED:
        return [lax.rem(z + d, nz) for d in range(nz)]
    return [z, lax.rem(z + 2, nz), z + 1 - 2 * lax.rem(z, 2), nz - 1 - z]


def mode_tables(order, decay, freq, panel_shape, floor_shape, nz, nc):
    modes = order.shape[1]
    panels = panel_shape.shape[0]
    floors = floor_shape.shape[0]
    mode_dev = modes // (nz * nc)
    slots = mode_dev * nz
    bits = BLK.bit_length() - 1
    half = BLK // 2

    def body(*refs):
        order_ref, decay_ref, freq_ref, panel_ref, floor_ref = refs[:5]
        pt_ref, fs_ref, tab_ref, turn_ref, own_ref, column_ref = refs[5:]
        column_ref[...] = jnp.broadcast_to(order_ref[...].astype(F32), (TILE, modes)).T
        z, c = lax.axis_index("taps"), lax.axis_index("floors")
        picked = []
        for at in placed(z, nz):
            owner = at * nc + c
            picked.append(column_ref[pl.ds(pl.multiple_of(owner * mode_dev, mode_dev), mode_dev), :])
        column = jnp.concatenate(picked, axis=0)[:, :1]
        ids = lax.broadcasted_iota(jnp.int32, (slots, modes), 1).astype(F32)
        pick = jnp.where(column == ids, 1.0, 0.0).astype(BF)
        pt_ref[...] = dot(pick, panel_ref[...], NT).astype(BF)
        fs_ref[...] = dot(floor_ref[...], pick, NT)
        decays, angles = decay_ref[...], freq_ref[...]
        re, im = jnp.cos(angles), jnp.sin(angles)
        rows = [decays]
        square = decays * decays
        loss = 2.0 * jnp.exp(-decays) * decays * (1.0 + square * (1.0 / 6.0 + square * (1.0 / 120.0)))
        rows.append(jnp.sqrt(loss))
        for _ in range(bits + 1):
            rows += [re, im]
            re, im = re * re - im * im, 2.0 * re * im
        rows += [jnp.zeros_like(re)] * (-len(rows) % 16)
        count = len(rows)
        stack = jnp.concatenate(rows, axis=0)
        hi, mid = split(stack)
        low = (stack - hi.astype(F32) - mid.astype(F32)).astype(BF)
        parts = dot(pick, jnp.concatenate([hi, mid, low], axis=0), NT)
        cols = parts[:, :count] + parts[:, count : 2 * count] + parts[:, 2 * count : 3 * count]
        rate, gain = cols[:, 0:1], cols[:, 1:2]
        lane = lax.broadcasted_iota(jnp.int32, (slots, half), 1)
        cos = jnp.where((lane & 1) != 0, cols[:, 2:3], 1.0)
        sin = jnp.where((lane & 1) != 0, cols[:, 3:4], 0.0)
        for b in range(1, bits - 1):
            on = (lane & (1 << b)) != 0
            step = cols[:, 2 + 2 * b : 3 + 2 * b], cols[:, 3 + 2 * b : 4 + 2 * b]
            new_cos, new_sin = turned((cos, sin), step)
            cos, sin = jnp.where(on, new_cos, cos), jnp.where(on, new_sin, sin)
        at = 2 * bits
        far_cos, far_sin = turned((cos, sin), (cols[:, at : at + 1], cols[:, at + 1 : at + 2]))
        steps = rate * lane.astype(F32)
        shrink, grow = jnp.exp(-steps), gain * jnp.exp(steps)
        far_shrink = shrink * jnp.exp(-rate * float(half))
        far_grow = grow * jnp.exp(rate * float(half))
        near, far = slice(0, half), slice(half, BLK)
        tab_ref[0, :, near], tab_ref[0, :, far] = grow * cos, far_grow * far_cos
        tab_ref[1, :, near], tab_ref[1, :, far] = -grow * sin, -far_grow * far_sin
        tab_ref[2, :, near], tab_ref[2, :, far] = shrink * cos, far_shrink * far_cos
        tab_ref[3, :, near], tab_ref[3, :, far] = shrink * sin, far_shrink * far_sin
        fade = jnp.exp(-rate * float(BLK))
        turn_ref[...] = fade * cols[:, at + 2 : at + 4]
        own_ref[...] = tab_ref[:, :mode_dev]

    return pl.pallas_call(
        body,
        in_specs=whole(5),
        out_specs=tuple(whole(5)),
        out_shape=(
            jax.ShapeDtypeStruct((slots, panels), BF),
            jax.ShapeDtypeStruct((floors, slots), F32),
            jax.ShapeDtypeStruct((4, slots, BLK), F32),
            jax.ShapeDtypeStruct((slots, 2), F32),
            jax.ShapeDtypeStruct((4, mode_dev, BLK), F32),
        ),
        scratch_shapes=[pltpu.VMEM((modes, TILE), F32)],
        compiler_params=params(),
        cost_estimate=cost(2),
        name="mode_tables",
    )(order, decay, freq, panel_shape, floor_shape)


def slot_forces(sums, pt, tables, turns, nz, before):
    slots, panels = pt.shape
    rows, time = sums[0].shape
    nc = len(sums)
    mode_dev = slots // nz
    plan = [(0, 1), (1, 1), (2, 2)] if nz == PAIRED else [(d, 1) for d in range(nz)]
    n = len(before)

    def body(*refs):
        sum_refs, (pt_ref, tab_ref, turn_ref) = refs[:nc], refs[nc : nc + 3]
        before_refs, out_refs = refs[nc + 3 : nc + 3 + n], refs[nc + 3 + n : -3]
        load_ref, state_refs = refs[-3], refs[-2:]
        load = sum_refs[0][panels:]
        for ref in sum_refs[1:]:
            load = load + ref[panels:]
        load_ref[...] = load
        left = pt_ref[...]
        turn = turn_ref[:, 0:1], turn_ref[:, 1:2]
        state = [ref[...] for ref in before_refs]
        for b in range(time // BLK):
            cols = slice(b * BLK, (b + 1) * BLK)
            total = sum_refs[0][:panels, cols]
            for ref in sum_refs[1:]:
                total = total + ref[:panels, cols]
            forces = dot_exact_left(left, total)
            for ref, (p, count) in zip(out_refs, plan):
                ref[:, cols] = forces[p * mode_dev : (p + count) * mode_dev]
            new = []
            for part in (forces * tab_ref[0], forces * tab_ref[1]):
                near = part[:, :TILE]
                for k in range(TILE, BLK, TILE):
                    near = near + part[:, k : k + TILE]
                new.append(near)
            if state:
                new = [a + b for a, b in zip(new, state)]
            state = turned(turn, new)
        state_refs[0][...], state_refs[1][...] = state

    out = pl.pallas_call(
        body,
        in_specs=whole(nc + 3 + n),
        out_specs=whole(len(plan) + 3),
        out_shape=[jax.ShapeDtypeStruct((count * mode_dev, time), F32) for _, count in plan]
        + [jax.ShapeDtypeStruct((rows - panels, time), F32)]
        + [jax.ShapeDtypeStruct((slots, TILE), F32)] * 2,
        compiler_params=params(),
        cost_estimate=cost(1),
        name="slot_forces",
    )(*sums, pt, tables, turns, *before)
    return out[:-3], out[-3], out[-2:]


def end_states(spread, turns, after):
    slots = turns.shape[0]

    def body(re_ref, im_ref, turn_ref, after_ref, out_ref):
        pad = jnp.zeros((TILE, TILE - 4), F32)
        for k in range(0, slots, TILE):
            at = slice(k, k + TILE)
            state = [jnp.sum(ref[at], axis=1, keepdims=True) for ref in (re_ref, im_ref)]
            four = [*state, turn_ref[at, 0:1], turn_ref[at, 1:2]]
            out_ref[:, at] = jnp.concatenate([*four, pad], axis=1).T[:8]

    return pl.pallas_call(
        body,
        in_specs=whole(4),
        out_specs=whole(1)[0],
        out_shape=jax.ShapeDtypeStruct((8, slots), F32),
        compiler_params=params(),
        cost_estimate=cost(1),
        name="end_states",
    )(*spread, turns, after)


def triangle():
    row = lax.broadcasted_iota(jnp.int32, (BLK, BLK), 0)
    col = lax.broadcasted_iota(jnp.int32, (BLK, BLK), 1)
    return jnp.where(row <= col, 1.0, 0.0).astype(BF)


def turned(a, b):
    return (a[0] * b[0] - a[1] * b[1], a[0] * b[1] + a[1] * b[0])


def motion_from_rest(forces, tables, turns, floor_slots):
    slots = turns.shape[0]
    floors = floor_slots.shape[0]
    time = max(start + x.shape[1] for x, _, start in forces)
    blocks = time // BLK
    n = len(forces)
    places = [(row, start, x.shape) for x, row, start in forces]

    def body(*refs):
        tab_ref, turn_ref, fs_ref, motion_ref = refs[n:]
        tri = triangle()
        here = fs_ref[...].astype(BF)
        turn = turn_ref[:, 0:1], turn_ref[:, 1:2]
        state = None
        for b in range(blocks):
            found = [
                (row, ref[:, b * BLK - start : (b + 1) * BLK - start])
                for ref, (row, start, shape) in zip(refs, places)
                if start <= b * BLK < start + shape[1]
            ]
            force = jnp.concatenate([x for _, x in sorted(found, key=lambda f: f[0])], axis=0)
            cr = dot_exact_right(force * tab_ref[0], tri)
            ci = dot_exact_right(force * tab_ref[1], tri)
            if state is not None:
                cr, ci = cr + state[0], ci + state[1]
            part = dot_exact_left(here, tab_ref[2] * cr - tab_ref[3] * ci)
            motion_ref[:, b * BLK : (b + 1) * BLK] = part
            if b < blocks - 1:
                state = turned(turn, (cr[:, BLK - 1 :], ci[:, BLK - 1 :]))

    return pl.pallas_call(
        body,
        in_specs=whole(n + 3),
        out_specs=whole(1)[0],
        out_shape=jax.ShapeDtypeStruct((floors, time), F32),
        compiler_params=params(),
        cost_estimate=cost(2),
        name="motion_from_rest",
    )(*(x for x, _, _ in forces), tables, turns, floor_slots)


def floor_shares(motion, ends, enter, tables, floor_slots, onward):
    floors, time = motion.shape
    blocks = time // BLK
    n = len(onward)

    def body(motion_ref, ends_ref, enter_ref, tab_ref, fs_ref, *refs):
        out_ref = refs[n]
        if n:
            refs[n + 1][...] = refs[0][...] + refs[1][refs[0].shape[0] :]
        shape = fs_ref[...]
        turn = (ends_ref[2:3, :], ends_ref[3:4, :])
        later = lax.axis_index("tm") > 0
        state = tuple(jnp.where(later, enter_ref[i : i + 1, :], 0.0) for i in (0, 1))
        left_re, left_im = [], []
        for b in range(blocks):
            left_re.append(shape * state[0])
            left_im.append(shape * state[1])
            state = turned(turn, state)
        qr_hi, qr_lo = split(tab_ref[2])
        qi_hi, qi_lo = split(tab_ref[3])
        re_hi, re_lo = split(jnp.concatenate(left_re, axis=0))
        im_hi, im_lo = split(jnp.concatenate(left_im, axis=0))
        free = dot(re_hi, qr_hi) + dot(re_hi, qr_lo) + dot(re_lo, qr_hi)
        free = free - (dot(im_hi, qi_hi) + dot(im_hi, qi_lo) + dot(im_lo, qi_hi))
        for b in range(blocks):
            cols = slice(b * BLK, (b + 1) * BLK)
            out_ref[:, cols] = motion_ref[:, cols] + free[b * floors : (b + 1) * floors]

    return pl.pallas_call(
        body,
        in_specs=whole(5 + n),
        out_specs=whole(1 + len(onward[:1])),
        out_shape=[
            jax.ShapeDtypeStruct(x, F32) for x in [(floors, time)] + [x.shape for x in onward[:1]]
        ],
        compiler_params=params(),
        cost_estimate=cost(1),
        name="floor_shares",
    )(motion, ends, enter, tables, floor_slots, *onward)


def owner_shares(motions, loads, enter, nz, floor_dev):
    nc, parts = len(motions), len(loads)
    floors, time = motions[0].shape
    rows = share_rows(floor_dev)
    owners = nz * nc
    mode_dev = enter.shape[1] // nz
    span = time // parts
    paired = nz == PAIRED
    shapes = [(rows, time)] * 2 + [(2 * rows, time)] if paired else [(rows, time)] * nz

    def body(*refs):
        motion_refs, load_refs, enter_ref = refs[:nc], refs[nc : nc + parts], refs[nc + parts]
        out_refs, motion_all, load_all = refs[nc + parts + 1 : -2], refs[-2], refs[-1]
        z, c = lax.axis_index("taps"), lax.axis_index("floors")
        later = lax.axis_index("tm") > 0
        motion = motion_refs[0][...]
        for ref in motion_refs[1:]:
            motion = motion + ref[...]
        for o in range(owners):
            at = slice(o * floor_dev, (o + 1) * floor_dev)
            motion_all[o] = motion[at]
            for k in range(parts):
                load_all[o, :, k * span : (k + 1) * span] = load_refs[k][at]
        for p, place in enumerate(placed(z, nz)):
            owner = place * nc + c
            out = out_refs[2].at[(p - 2) * rows : (p - 1) * rows] if paired and p > 1 else out_refs[p]
            out[...] = jnp.zeros((rows, time), F32)
            out[:floor_dev] = motion_all[owner]
            out[floor_dev : 2 * floor_dev] = load_all[owner]
            state = enter_ref[0:2, p * mode_dev : (p + 1) * mode_dev]
            out[2 * floor_dev : 2 * floor_dev + 2, :mode_dev] = jnp.where(later, state, 0.0)

    return pl.pallas_call(
        body,
        in_specs=whole(nc + parts + 1),
        out_specs=whole(len(shapes)),
        out_shape=[jax.ShapeDtypeStruct(x, F32) for x in shapes],
        scratch_shapes=[pltpu.VMEM((owners, floor_dev, time), F32)] * 2,
        compiler_params=params(),
        cost_estimate=cost(1),
        name="owner_shares",
    )(*motions, *loads, enter)


def share_rows(floor_dev):
    return -(-(2 * floor_dev + 2) // 8) * 8


def onward_second(two, arrived, share, share_arrived):
    mode_dev, half = two.shape
    rows = share.shape[0]

    def body(two_ref, arrived_ref, share_ref, share_arrived_ref, out_ref):
        out_ref[:mode_dev] = two_ref[...] + arrived_ref[mode_dev:]
        total = share_ref[...] + share_arrived_ref[rows:]
        out_ref[mode_dev : mode_dev + rows] = total[:, :half]
        out_ref[mode_dev + rows :] = total[:, half:]

    return pl.pallas_call(
        body,
        in_specs=whole(4),
        out_specs=whole(1)[0],
        out_shape=jax.ShapeDtypeStruct((mode_dev + 2 * rows, half), F32),
        compiler_params=params(),
        cost_estimate=cost(1),
        name="onward_second",
    )(two, arrived, share, share_arrived)


def block_sums(force, tables, tri):
    return [dot_exact_right(force * table, tri) for table in tables]


def sum_at(refs, forces, b, mode_dev):
    total = None
    for ref, (x, row, start) in zip(refs, forces):
        if start <= b * BLK < start + x.shape[1]:
            part = ref[row : row + mode_dev, b * BLK - start : (b + 1) * BLK - start]
            total = part if total is None else total + part
    return total


def own_start(forces, tables, turns, until):
    mode_dev = forces[0][0].shape[0]
    n = len(forces)

    def body(*refs):
        tab_ref, turn_ref, resp_ref, state_ref = refs[n:]
        turn = turn_ref[:mode_dev, 0:1], turn_ref[:mode_dev, 1:2]
        tri = triangle()
        state = None
        for b in range(until // BLK):
            cr, ci = block_sums(sum_at(refs, forces, b, mode_dev), (tab_ref[0], tab_ref[1]), tri)
            if state is not None:
                cr, ci = cr + state[0], ci + state[1]
            resp_ref[:, b * BLK : (b + 1) * BLK] = tab_ref[2] * cr - tab_ref[3] * ci
            state = turned(turn, (cr[:, BLK - 1 :], ci[:, BLK - 1 :]))
        state_ref[:, 0:1], state_ref[:, 1:2] = state

    return pl.pallas_call(
        body,
        in_specs=whole(n + 2),
        out_specs=tuple(whole(2)),
        out_shape=(
            jax.ShapeDtypeStruct((mode_dev, until), F32),
            jax.ShapeDtypeStruct((mode_dev, 2), F32),
        ),
        compiler_params=params(),
        cost_estimate=cost(1),
        name="own_start",
    )(*(x for x, _, _ in forces), tables, turns)


def own_response(forces, shares, tables, turns, floor_dev, load_scale, begun):
    mode_dev = forces[0][0].shape[0]
    rows = share_rows(floor_dev)
    n, m, k = len(shares), len(forces), len(begun)
    time = shares[0][0].shape[1]
    blocks = time // BLK
    until = begun[0].shape[1] // BLK if begun else 0

    def body(*refs):
        begun_refs = refs[m + n : m + n + k]
        tab_ref, turn_ref, resp_ref, motion_ref, load_ref, share_ref = refs[m + n + k :]
        for i, (x, row, start) in enumerate(shares):
            at = slice(start, start + x.shape[1])
            part = refs[m + i][row : row + rows]
            share_ref[:, at] = part if i == 0 else share_ref[:, at] + part
        share = share_ref[...]
        motion_ref[...] = share[:floor_dev]
        load_ref[...] = share[floor_dev : 2 * floor_dev] * load_scale
        qr, qi = tab_ref[2], tab_ref[3]
        turn = turn_ref[:mode_dev, 0:1], turn_ref[:mode_dev, 1:2]
        column = share[:, :TILE].T
        at = 2 * floor_dev
        state = column[:mode_dev, at : at + 1], column[:mode_dev, at + 1 : at + 2]
        tri = triangle()
        sums = {
            b: block_sums(sum_at(refs, forces, b, mode_dev), (tab_ref[0], tab_ref[1]), tri)
            for b in range(until, blocks)
        }
        for b in range(blocks):
            cols = slice(b * BLK, (b + 1) * BLK)
            if b < until:
                resp_ref[:, cols] = begun_refs[0][:, cols] + (qr * state[0] - qi * state[1])
                state = turned(turn, state)
                if b == until - 1:
                    state = state[0] + begun_refs[1][:, 0:1], state[1] + begun_refs[1][:, 1:2]
            else:
                cr, ci = (x + y for x, y in zip(sums[b], state))
                resp_ref[:, cols] = qr * cr - qi * ci
                state = turned(turn, (cr[:, BLK - 1 :], ci[:, BLK - 1 :]))

    return pl.pallas_call(
        body,
        in_specs=whole(m + n + k + 2),
        out_specs=tuple(whole(3)),
        out_shape=(
            jax.ShapeDtypeStruct((mode_dev, time), F32),
            jax.ShapeDtypeStruct((floor_dev, time), F32),
            jax.ShapeDtypeStruct((floor_dev, time), F32),
        ),
        scratch_shapes=[pltpu.VMEM((rows, time), F32)],
        compiler_params=params(),
        cost_estimate=cost(1),
        name="own_response",
    )(*(x for x, _, _ in forces), *(x for x, _, _ in shares), *begun, tables, turns)


def shifts(x, axis, n):
    return [lax.ppermute(x, axis, [(i, (i + d) % n) for i in range(n)]) for d in range(1, n)]


def along(parts, n):
    return [parts[0]] + [
        lax.ppermute(parts[d], "taps", [(i, (i + d) % n) for i in range(n)]) for d in range(1, n)
    ]


def on_device(
    pressures,
    tap_area,
    tap_panel,
    tap_floor,
    panel_shape,
    floor_shape,
    mode_order,
    mode_decay,
    mode_freq,
):
    nz = lax.axis_size("taps")
    nc = lax.axis_size("floors")
    nt = lax.axis_size("tm")
    owners = nz * nc
    modes = mode_order.shape[0]
    mode_dev = modes // owners
    time, taps = pressures.shape
    panels = panel_shape.shape[0]
    floors = floor_shape.shape[0]
    floor_dev = floors // owners
    load_scale = (floors / (taps * owners)) ** 0.5

    mine, kept = tap_sums(
        pressures,
        tap_panel[None],
        tap_floor[None],
        tap_area,
        (mode_order[None], mode_decay[None], mode_freq[None], panel_shape, floor_shape),
        panels,
        floors,
    )
    sums = [[x] + shifts(x, "floors", nc) for x in mine]
    pt, floor_slots, tables, turns, own = mode_tables(*kept, nz, nc)
    forces, loads, spread = [], [], []
    for part in sums:
        force, load, spread = slot_forces(part, pt, tables, turns, nz, spread)
        forces.append(force)
        loads.append(load)
    half = time // 2
    span = time // len(forces)
    pair, two = ([(i, i ^ d) for i in range(nz)] for d in (1, 2))
    laid = [(x, p * mode_dev, k * span) for k, part in enumerate(forces) for p, x in enumerate(part)]
    if nz == PAIRED:
        crossed = [lax.ppermute(part[2], "taps", pair) for part in forces]
        onward = [forces[0][1], crossed[0]]
    else:
        crossed, onward = [(x, 0, k * span) for k, part in enumerate(forces) for x in along(part, nz)], []
    motion = motion_from_rest(laid, tables, turns, floor_slots)
    ends = end_states(spread, turns, motion)
    enter = jnp.zeros_like(ends)
    for hop in range(nt - 1):
        passed = ends
        if hop:
            turn = (ends[2:3], ends[3:4])
            over = turn
            for _ in range(time // BLK - 1):
                over = turned(over, turn)
            enter = jnp.where(lax.axis_index("tm") > 0, enter, 0.0)
            passed = ends + jnp.concatenate(
                [*turned(over, (enter[0:1], enter[1:2])), jnp.zeros_like(ends[2:])]
            )
        enter = lax.ppermute(passed, "tm", [(i, (i + 1) % nt) for i in range(nt)])
        enter = jnp.where(lax.axis_index("tm") > 0, enter, 0.0)
    motion, *onward = floor_shares(motion, ends, enter, tables, floor_slots, onward)
    motions = [motion] + shifts(motion, "floors", nc)
    shares = owner_shares(motions, loads, enter, nz, floor_dev)
    if nz == PAIRED:
        rows = share_rows(floor_dev)
        other = lax.ppermute(shares[2], "taps", pair)
        first = lax.ppermute(onward[0], "taps", two)
        second = lax.ppermute(onward_second(forces[1][1], crossed[1], shares[1], other), "taps", two)
        begun = own_start([(forces[0][0], 0, 0), (crossed[0], 0, 0), (first, 0, 0)], own, turns, half)
        crossed = [(forces[1][0], 0, half), (crossed[1], 0, half), (second, 0, half)]
        shares = [(shares[0], 0, 0), (other, 0, 0), (second, mode_dev, 0), (second, mode_dev + rows, half)]
    else:
        begun = []
        shares = [(x, 0, 0) for x in along(shares, nz)]
    return own_response(crossed, shares, own, turns, floor_dev, load_scale, begun)


def solution(mesh):
    in_specs = (
        P(("dirs", "tm"), ("taps", "floors")),
        P(("taps", "floors")),
        P(("taps", "floors")),
        P(("taps", "floors")),
        P(),
        P(),
        P(),
        P(),
        P(),
    )
    out_specs = (
        P(("taps", "floors"), ("dirs", "tm")),
        P(("taps", "floors"), ("dirs", "tm")),
        P(("taps", "floors"), ("dirs", "tm")),
    )
    return jax.shard_map(
        on_device, mesh=mesh, in_specs=in_specs, out_specs=out_specs, check_vma=False
    )
```

```python
import jax
import jax.numpy as jnp
from jax import lax
from jax.experimental import pallas as pl
from jax.experimental.pallas import tpu as pltpu
from jax.sharding import PartitionSpec as P

BLK = 256
PAIRED = 4
TILE = 128
BF = jnp.bfloat16
F32 = jnp.float32
NN = (((1,), (0,)), ((), ()))
NT = (((1,), (1,)), ((), ()))
VMEM_LIMIT = 16 * 1024 * 1024


def dot(a, b, dims=NN):
    return lax.dot_general(a, b, dims, preferred_element_type=F32)


def split(x):
    hi = x.astype(BF)
    return hi, (x - hi.astype(F32)).astype(BF)


def dot_exact_left(a, x, dims=NN):
    hi, lo = split(x)
    return dot(a, hi, dims) + dot(a, lo, dims)


def dot_exact_right(x, b, dims=NN):
    hi, lo = split(x)
    return dot(hi, b, dims) + dot(lo, b, dims)


def params():
    return pltpu.CompilerParams(vmem_limit_bytes=VMEM_LIMIT)


def in_hbm(x):
    return pltpu.with_memory_space_constraint(x, pltpu.HBM)


def cost(us):
    return pl.CostEstimate(flops=int(us * 5e8), bytes_accessed=int(us * 2e6), transcendentals=0)


def whole(n):
    return [pl.BlockSpec(memory_space=pltpu.VMEM)] * n


def tap_sums(pressures, tap_panel, tap_floor, tap_area, others, panels, floors):
    time, taps = pressures.shape
    rows = panels + floors
    chunks = 2 if time % (2 * BLK) == 0 else 1
    span = time // chunks
    n = len(others)
    given = (tap_panel, tap_floor, tap_area)

    def body(press_hbm, *refs):
        from_refs, sums_ref, kept = refs[: n + 3], refs[n + 3], refs[n + 4 : 2 * n + 4]
        press, panel, floor, area, weights, sems = refs[2 * n + 4 :]
        small = [
            pltpu.make_async_copy(a, b, sems.at[chunks + i])
            for i, (a, b) in enumerate(zip(from_refs, (panel, floor, area, *kept)))
        ]
        large = []
        for i in range(chunks):
            at = pl.ds(i * span, span)
            large.append(pltpu.make_async_copy(press_hbm.at[at], press.at[at], sems.at[i]))
        for copy in [*small[:3], *large, *small[3:]]:
            copy.start()
        for copy in small[:3]:
            copy.wait()
        each = jnp.broadcast_to(area[...].astype(F32).reshape(1, taps), (16, taps))
        row = lax.broadcasted_iota(jnp.int32, (16, taps), 0)
        for ids, first, count in ((panel, 0, panels), (floor, panels, floors)):
            at = jnp.broadcast_to(ids[...], (16, taps)) - row
            for r in range(0, count, 16):
                weights[first + r : first + r + 16] = jnp.where(at == r, each, 0.0).astype(BF)
        for i in range(chunks):
            at = slice(i * span, (i + 1) * span)
            large[i].wait()
            sums_ref[:, at] = dot(weights[...], press[at], NT)
        for copy in small[3:]:
            copy.wait()

    out = pl.pallas_call(
        body,
        in_specs=[pl.BlockSpec(memory_space=pltpu.HBM)] * (n + 4),
        out_specs=tuple(whole(n + 1)),
        out_shape=(jax.ShapeDtypeStruct((rows, time), F32), *(jax.ShapeDtypeStruct(x.shape, x.dtype) for x in others)),
        scratch_shapes=[
            pltpu.VMEM((time, taps), BF),
            *(pltpu.VMEM(x.shape, x.dtype) for x in given),
            pltpu.VMEM((rows, taps), BF),
            pltpu.SemaphoreType.DMA((chunks + n + 3,)),
        ],
        compiler_params=params(),
        cost_estimate=cost(3),
        name="tap_sums",
    )(in_hbm(pressures), *(in_hbm(x) for x in given), *(in_hbm(x) for x in others))
    return out[0], out[1:]


def placed(z, nz):
    if nz != PAIRED:
        return [lax.rem(z + d, nz) for d in range(nz)]
    return [z, lax.rem(z + 2, nz), z + 1 - 2 * lax.rem(z, 2), nz - 1 - z]


def mode_tables(order, decay, freq, panel_shape, floor_shape, nz, nc):
    modes = order.shape[1]
    panels = panel_shape.shape[0]
    floors = floor_shape.shape[0]
    mode_dev = modes // (nz * nc)
    slots = mode_dev * nz
    bits = BLK.bit_length() - 1
    half = BLK // 2

    def body(*refs):
        order_ref, decay_ref, freq_ref, panel_ref, floor_ref = refs[:5]
        pt_ref, fs_ref, tab_ref, turn_ref, own_ref, column_ref = refs[5:]
        column_ref[...] = jnp.broadcast_to(order_ref[...].astype(F32), (TILE, modes)).T
        z, c = lax.axis_index("taps"), lax.axis_index("floors")
        picked = []
        for at in placed(z, nz):
            owner = at * nc + c
            picked.append(column_ref[pl.ds(pl.multiple_of(owner * mode_dev, mode_dev), mode_dev), :])
        column = jnp.concatenate(picked, axis=0)[:, :1]
        ids = lax.broadcasted_iota(jnp.int32, (slots, modes), 1).astype(F32)
        pick = jnp.where(column == ids, 1.0, 0.0).astype(BF)
        pt_ref[...] = dot(pick, panel_ref[...], NT).astype(BF)
        fs_ref[...] = dot(floor_ref[...], pick, NT)
        decays, angles = decay_ref[...], freq_ref[...]
        re, im = jnp.cos(angles), jnp.sin(angles)
        rows = [decays]
        square = decays * decays
        loss = 2.0 * jnp.exp(-decays) * decays * (1.0 + square * (1.0 / 6.0 + square * (1.0 / 120.0)))
        rows.append(jnp.sqrt(loss))
        for _ in range(bits + 1):
            rows += [re, im]
            re, im = re * re - im * im, 2.0 * re * im
        rows += [jnp.zeros_like(re)] * (-len(rows) % 16)
        count = len(rows)
        stack = jnp.concatenate(rows, axis=0)
        hi, mid = split(stack)
        low = (stack - hi.astype(F32) - mid.astype(F32)).astype(BF)
        parts = dot(pick, jnp.concatenate([hi, mid, low], axis=0), NT)
        cols = parts[:, :count] + parts[:, count : 2 * count] + parts[:, 2 * count : 3 * count]
        rate, gain = cols[:, 0:1], cols[:, 1:2]
        lane = lax.broadcasted_iota(jnp.int32, (slots, half), 1)
        cos = jnp.where((lane & 1) != 0, cols[:, 2:3], 1.0)
        sin = jnp.where((lane & 1) != 0, cols[:, 3:4], 0.0)
        for b in range(1, bits - 1):
            on = (lane & (1 << b)) != 0
            step = cols[:, 2 + 2 * b : 3 + 2 * b], cols[:, 3 + 2 * b : 4 + 2 * b]
            new_cos, new_sin = turned((cos, sin), step)
            cos, sin = jnp.where(on, new_cos, cos), jnp.where(on, new_sin, sin)
        at = 2 * bits
        far_cos, far_sin = turned((cos, sin), (cols[:, at : at + 1], cols[:, at + 1 : at + 2]))
        steps = rate * lane.astype(F32)
        shrink, grow = jnp.exp(-steps), gain * jnp.exp(steps)
        far_shrink = shrink * jnp.exp(-rate * float(half))
        far_grow = grow * jnp.exp(rate * float(half))
        near, far = slice(0, half), slice(half, BLK)
        tab_ref[0, :, near], tab_ref[0, :, far] = grow * cos, far_grow * far_cos
        tab_ref[1, :, near], tab_ref[1, :, far] = -grow * sin, -far_grow * far_sin
        tab_ref[2, :, near], tab_ref[2, :, far] = shrink * cos, far_shrink * far_cos
        tab_ref[3, :, near], tab_ref[3, :, far] = shrink * sin, far_shrink * far_sin
        fade = jnp.exp(-rate * float(BLK))
        turn_ref[...] = fade * cols[:, at + 2 : at + 4]
        own_ref[...] = tab_ref[:, :mode_dev]

    return pl.pallas_call(
        body,
        in_specs=whole(5),
        out_specs=tuple(whole(5)),
        out_shape=(
            jax.ShapeDtypeStruct((slots, panels), BF),
            jax.ShapeDtypeStruct((floors, slots), F32),
            jax.ShapeDtypeStruct((4, slots, BLK), F32),
            jax.ShapeDtypeStruct((slots, 2), F32),
            jax.ShapeDtypeStruct((4, mode_dev, BLK), F32),
        ),
        scratch_shapes=[pltpu.VMEM((modes, TILE), F32)],
        compiler_params=params(),
        cost_estimate=cost(2),
        name="mode_tables",
    )(order, decay, freq, panel_shape, floor_shape)


def slot_forces(sums, pt, tables, turns, nz, before):
    slots, panels = pt.shape
    rows, time = sums[0].shape
    nc = len(sums)
    mode_dev = slots // nz
    n = len(before)

    def body(*refs):
        sum_refs, (pt_ref, tab_ref, turn_ref) = refs[:nc], refs[nc : nc + 3]
        before_refs, out_refs = refs[nc + 3 : nc + 3 + n], refs[nc + 3 + n : -3]
        load_ref, state_refs = refs[-3], refs[-2:]
        load = sum_refs[0][panels:]
        for ref in sum_refs[1:]:
            load = load + ref[panels:]
        load_ref[...] = load
        left = pt_ref[...]
        turn = turn_ref[:, 0:1], turn_ref[:, 1:2]
        state = [ref[...] for ref in before_refs]
        for b in range(time // BLK):
            cols = slice(b * BLK, (b + 1) * BLK)
            total = sum_refs[0][:panels, cols]
            for ref in sum_refs[1:]:
                total = total + ref[:panels, cols]
            forces = dot_exact_left(left, total)
            for p, ref in enumerate(out_refs):
                ref[:, cols] = forces[p * mode_dev : (p + 1) * mode_dev]
            new = []
            for part in (forces * tab_ref[0], forces * tab_ref[1]):
                near = part[:, :TILE]
                for k in range(TILE, BLK, TILE):
                    near = near + part[:, k : k + TILE]
                new.append(near)
            if state:
                new = [a + b for a, b in zip(new, state)]
            state = turned(turn, new)
        state_refs[0][...], state_refs[1][...] = state

    out = pl.pallas_call(
        body,
        in_specs=whole(nc + 3 + n),
        out_specs=whole(nz + 3),
        out_shape=[jax.ShapeDtypeStruct((mode_dev, time), F32)] * nz
        + [jax.ShapeDtypeStruct((rows - panels, time), F32)]
        + [jax.ShapeDtypeStruct((slots, TILE), F32)] * 2,
        compiler_params=params(),
        cost_estimate=cost(1),
        name="slot_forces",
    )(*sums, pt, tables, turns, *before)
    return out[:-3], out[-3], out[-2:]


def end_states(spread, turns, after):
    slots = turns.shape[0]

    def body(re_ref, im_ref, turn_ref, after_ref, out_ref):
        pad = jnp.zeros((TILE, TILE - 4), F32)
        for k in range(0, slots, TILE):
            at = slice(k, k + TILE)
            state = [jnp.sum(ref[at], axis=1, keepdims=True) for ref in (re_ref, im_ref)]
            four = [*state, turn_ref[at, 0:1], turn_ref[at, 1:2]]
            out_ref[:, at] = jnp.concatenate([*four, pad], axis=1).T[:8]

    return pl.pallas_call(
        body,
        in_specs=whole(4),
        out_specs=whole(1)[0],
        out_shape=jax.ShapeDtypeStruct((8, slots), F32),
        compiler_params=params(),
        cost_estimate=cost(1),
        name="end_states",
    )(*spread, turns, after)


def triangle():
    row = lax.broadcasted_iota(jnp.int32, (BLK, BLK), 0)
    col = lax.broadcasted_iota(jnp.int32, (BLK, BLK), 1)
    return jnp.where(row <= col, 1.0, 0.0).astype(BF)


def turned(a, b):
    return (a[0] * b[0] - a[1] * b[1], a[0] * b[1] + a[1] * b[0])


def motion_from_rest(forces, tables, turns, floor_slots):
    slots = turns.shape[0]
    floors = floor_slots.shape[0]
    time = max(start + x.shape[1] for x, _, start in forces)
    blocks = time // BLK
    n = len(forces)
    places = [(row, start, x.shape) for x, row, start in forces]

    def body(*refs):
        tab_ref, turn_ref, fs_ref, motion_ref = refs[n:]
        tri = triangle()
        here = fs_ref[...].astype(BF)
        turn = turn_ref[:, 0:1], turn_ref[:, 1:2]
        state = None
        for b in range(blocks):
            found = [
                (row, ref[:, b * BLK - start : (b + 1) * BLK - start])
                for ref, (row, start, shape) in zip(refs, places)
                if start <= b * BLK < start + shape[1]
            ]
            force = jnp.concatenate([x for _, x in sorted(found, key=lambda f: f[0])], axis=0)
            cr = dot_exact_right(force * tab_ref[0], tri)
            ci = dot_exact_right(force * tab_ref[1], tri)
            if state is not None:
                cr, ci = cr + state[0], ci + state[1]
            part = dot_exact_left(here, tab_ref[2] * cr - tab_ref[3] * ci)
            motion_ref[:, b * BLK : (b + 1) * BLK] = part
            if b < blocks - 1:
                state = turned(turn, (cr[:, BLK - 1 :], ci[:, BLK - 1 :]))

    return pl.pallas_call(
        body,
        in_specs=whole(n + 3),
        out_specs=whole(1)[0],
        out_shape=jax.ShapeDtypeStruct((floors, time), F32),
        compiler_params=params(),
        cost_estimate=cost(2),
        name="motion_from_rest",
    )(*(x for x, _, _ in forces), tables, turns, floor_slots)


def floor_shares(motion, ends, enter, tables, floor_slots, onward):
    floors, time = motion.shape
    blocks = time // BLK
    n = len(onward)

    def body(motion_ref, ends_ref, enter_ref, tab_ref, fs_ref, *refs):
        out_ref = refs[n]
        if n:
            refs[n + 1][...] = refs[0][...] + refs[1][...]
        shape = fs_ref[...]
        turn = (ends_ref[2:3, :], ends_ref[3:4, :])
        later = lax.axis_index("tm") > 0
        state = tuple(jnp.where(later, enter_ref[i : i + 1, :], 0.0) for i in (0, 1))
        left_re, left_im = [], []
        for b in range(blocks):
            left_re.append(shape * state[0])
            left_im.append(shape * state[1])
            state = turned(turn, state)
        qr_hi, qr_lo = split(tab_ref[2])
        qi_hi, qi_lo = split(tab_ref[3])
        re_hi, re_lo = split(jnp.concatenate(left_re, axis=0))
        im_hi, im_lo = split(jnp.concatenate(left_im, axis=0))
        free = dot(re_hi, qr_hi) + dot(re_hi, qr_lo) + dot(re_lo, qr_hi)
        free = free - (dot(im_hi, qi_hi) + dot(im_hi, qi_lo) + dot(im_lo, qi_hi))
        for b in range(blocks):
            cols = slice(b * BLK, (b + 1) * BLK)
            out_ref[:, cols] = motion_ref[:, cols] + free[b * floors : (b + 1) * floors]

    return pl.pallas_call(
        body,
        in_specs=whole(5 + n),
        out_specs=whole(1 + len(onward[:1])),
        out_shape=[
            jax.ShapeDtypeStruct(x, F32) for x in [(floors, time)] + [x.shape for x in onward[:1]]
        ],
        compiler_params=params(),
        cost_estimate=cost(1),
        name="floor_shares",
    )(motion, ends, enter, tables, floor_slots, *onward)


def owner_shares(motions, loads, enter, nz, floor_dev):
    nc, parts = len(motions), len(loads)
    floors, time = motions[0].shape
    rows = share_rows(floor_dev)
    owners = nz * nc
    mode_dev = enter.shape[1] // nz
    span = time // parts
    paired = nz == PAIRED
    shapes = [(rows, time)] * 2 + [(2 * rows, time)] if paired else [(rows, time)] * nz

    def body(*refs):
        motion_refs, load_refs, enter_ref = refs[:nc], refs[nc : nc + parts], refs[nc + parts]
        out_refs, motion_all, load_all = refs[nc + parts + 1 : -2], refs[-2], refs[-1]
        z, c = lax.axis_index("taps"), lax.axis_index("floors")
        later = lax.axis_index("tm") > 0
        motion = motion_refs[0][...]
        for ref in motion_refs[1:]:
            motion = motion + ref[...]
        for o in range(owners):
            at = slice(o * floor_dev, (o + 1) * floor_dev)
            motion_all[o] = motion[at]
            for k in range(parts):
                load_all[o, :, k * span : (k + 1) * span] = load_refs[k][at]
        for p, place in enumerate(placed(z, nz)):
            owner = place * nc + c
            out = out_refs[2].at[(p - 2) * rows : (p - 1) * rows] if paired and p > 1 else out_refs[p]
            out[...] = jnp.zeros((rows, time), F32)
            out[:floor_dev] = motion_all[owner]
            out[floor_dev : 2 * floor_dev] = load_all[owner]
            state = enter_ref[0:2, p * mode_dev : (p + 1) * mode_dev]
            out[2 * floor_dev : 2 * floor_dev + 2, :mode_dev] = jnp.where(later, state, 0.0)

    return pl.pallas_call(
        body,
        in_specs=whole(nc + parts + 1),
        out_specs=whole(len(shapes)),
        out_shape=[jax.ShapeDtypeStruct(x, F32) for x in shapes],
        scratch_shapes=[pltpu.VMEM((owners, floor_dev, time), F32)] * 2,
        compiler_params=params(),
        cost_estimate=cost(1),
        name="owner_shares",
    )(*motions, *loads, enter)


def share_rows(floor_dev):
    return -(-(2 * floor_dev + 2) // 8) * 8


def share_onward(share, arrived):
    rows = share.shape[0]

    def body(share_ref, arrived_ref, out_ref):
        out_ref[...] = share_ref[...] + arrived_ref[rows:]

    return pl.pallas_call(
        body,
        in_specs=whole(2),
        out_specs=whole(1)[0],
        out_shape=jax.ShapeDtypeStruct(share.shape, F32),
        compiler_params=params(),
        cost_estimate=cost(1),
        name="share_onward",
    )(share, arrived)


def block_sums(force, tables, tri):
    return [dot_exact_right(force * table, tri) for table in tables]


def sum_at(refs, forces, b, mode_dev):
    total = None
    for ref, (x, row, start) in zip(refs, forces):
        if start <= b * BLK < start + x.shape[1]:
            part = ref[row : row + mode_dev, b * BLK - start : (b + 1) * BLK - start]
            total = part if total is None else total + part
    return total


def own_response(forces, shares, tables, turns, floor_dev, load_scale):
    mode_dev = forces[0][0].shape[0]
    rows = share_rows(floor_dev)
    n, m = len(shares), len(forces)
    time = shares[0][0].shape[1]
    blocks = time // BLK

    def body(*refs):
        tab_ref, turn_ref, resp_ref, motion_ref, load_ref, share_ref = refs[m + n :]
        for i, (x, row, start) in enumerate(shares):
            at = slice(start, start + x.shape[1])
            part = refs[m + i][row : row + rows]
            share_ref[:, at] = part if i == 0 else share_ref[:, at] + part
        share = share_ref[...]
        motion_ref[...] = share[:floor_dev]
        load_ref[...] = share[floor_dev : 2 * floor_dev] * load_scale
        qr, qi = tab_ref[2], tab_ref[3]
        turn = turn_ref[:mode_dev, 0:1], turn_ref[:mode_dev, 1:2]
        column = share[:, :TILE].T
        at = 2 * floor_dev
        state = column[:mode_dev, at : at + 1], column[:mode_dev, at + 1 : at + 2]
        tri = triangle()
        for b in range(blocks):
            sums = block_sums(sum_at(refs, forces, b, mode_dev), (tab_ref[0], tab_ref[1]), tri)
            cr, ci = (x + y for x, y in zip(sums, state))
            resp_ref[:, b * BLK : (b + 1) * BLK] = qr * cr - qi * ci
            state = turned(turn, (cr[:, BLK - 1 :], ci[:, BLK - 1 :]))

    return pl.pallas_call(
        body,
        in_specs=whole(m + n + 2),
        out_specs=tuple(whole(3)),
        out_shape=(
            jax.ShapeDtypeStruct((mode_dev, time), F32),
            jax.ShapeDtypeStruct((floor_dev, time), F32),
            jax.ShapeDtypeStruct((floor_dev, time), F32),
        ),
        scratch_shapes=[pltpu.VMEM((rows, time), F32)],
        compiler_params=params(),
        cost_estimate=cost(1),
        name="own_response",
    )(*(x for x, _, _ in forces), *(x for x, _, _ in shares), tables, turns)


def shifts(x, axis, n):
    return [lax.ppermute(x, axis, [(i, (i + d) % n) for i in range(n)]) for d in range(1, n)]


def along(parts, n):
    return [parts[0]] + [
        lax.ppermute(parts[d], "taps", [(i, (i + d) % n) for i in range(n)]) for d in range(1, n)
    ]


def on_device(
    pressures,
    tap_area,
    tap_panel,
    tap_floor,
    panel_shape,
    floor_shape,
    mode_order,
    mode_decay,
    mode_freq,
):
    nz = lax.axis_size("taps")
    nc = lax.axis_size("floors")
    nt = lax.axis_size("tm")
    owners = nz * nc
    modes = mode_order.shape[0]
    mode_dev = modes // owners
    time, taps = pressures.shape
    panels = panel_shape.shape[0]
    floors = floor_shape.shape[0]
    floor_dev = floors // owners
    load_scale = (floors / (taps * owners)) ** 0.5

    mine, kept = tap_sums(
        pressures,
        tap_panel[None],
        tap_floor[None],
        tap_area,
        (mode_order[None], mode_decay[None], mode_freq[None], panel_shape, floor_shape),
        panels,
        floors,
    )
    sums = [[mine] + shifts(mine, "floors", nc)]
    pt, floor_slots, tables, turns, own = mode_tables(*kept, nz, nc)
    forces, loads, spread = [], [], []
    for part in sums:
        force, load, spread = slot_forces(part, pt, tables, turns, nz, spread)
        forces.append(force)
        loads.append(load)
    span = time // len(forces)
    pair, two = ([(i, i ^ d) for i in range(nz)] for d in (1, 2))
    laid = [(x, p * mode_dev, k * span) for k, part in enumerate(forces) for p, x in enumerate(part)]
    if nz == PAIRED:
        onward = [forces[0][1], lax.ppermute(forces[0][3], "taps", pair)]
        direct = lax.ppermute(forces[0][2], "taps", pair)
    else:
        crossed, onward = [(x, 0, 0) for x in along(forces[0], nz)], []
    motion = motion_from_rest(laid, tables, turns, floor_slots)
    ends = end_states(spread, turns, motion)
    enter = jnp.zeros_like(ends)
    for hop in range(nt - 1):
        passed = ends
        if hop:
            turn = (ends[2:3], ends[3:4])
            over = turn
            for _ in range(time // BLK - 1):
                over = turned(over, turn)
            enter = jnp.where(lax.axis_index("tm") > 0, enter, 0.0)
            passed = ends + jnp.concatenate(
                [*turned(over, (enter[0:1], enter[1:2])), jnp.zeros_like(ends[2:])]
            )
        enter = lax.ppermute(passed, "tm", [(i, (i + 1) % nt) for i in range(nt)])
    motion, *onward = floor_shares(motion, ends, enter, tables, floor_slots, onward)
    motions = [motion] + shifts(motion, "floors", nc)
    shares = owner_shares(motions, loads, enter, nz, floor_dev)
    if nz == PAIRED:
        other = lax.ppermute(shares[2], "taps", pair)
        last = lax.ppermute(share_onward(shares[1], other), "taps", two)
        crossed = [(x, 0, 0) for x in (forces[0][0], direct, lax.ppermute(onward[0], "taps", two))]
        shares = [(x, 0, 0) for x in (shares[0], other, last)]
    else:
        shares = [(x, 0, 0) for x in along(shares, nz)]
    return own_response(crossed, shares, own, turns, floor_dev, load_scale)


def solution(mesh):
    in_specs = (
        P(("dirs", "tm"), ("taps", "floors")),
        P(("taps", "floors")),
        P(("taps", "floors")),
        P(("taps", "floors")),
        P(),
        P(),
        P(),
        P(),
        P(),
    )
    out_specs = (
        P(("taps", "floors"), ("dirs", "tm")),
        P(("taps", "floors"), ("dirs", "tm")),
        P(("taps", "floors"), ("dirs", "tm")),
    )
    return jax.shard_map(
        on_device, mesh=mesh, in_specs=in_specs, out_specs=out_specs, check_vma=False
    )
```

```python
import jax
import jax.numpy as jnp
from jax import lax
from jax.experimental import pallas as pl
from jax.experimental.pallas import tpu as pltpu
from jax.sharding import PartitionSpec as P

BLK = 256
PAIRED = 4
TILE = 128
BF = jnp.bfloat16
F32 = jnp.float32
NN = (((1,), (0,)), ((), ()))
NT = (((1,), (1,)), ((), ()))
VMEM_LIMIT = 16 * 1024 * 1024


def dot(a, b, dims=NN):
    return lax.dot_general(a, b, dims, preferred_element_type=F32)


def split(x):
    hi = x.astype(BF)
    return hi, (x - hi.astype(F32)).astype(BF)


def dot_exact_left(a, x, dims=NN):
    hi, lo = split(x)
    return dot(a, hi, dims) + dot(a, lo, dims)


def dot_exact_right(x, b, dims=NN):
    hi, lo = split(x)
    return dot(hi, b, dims) + dot(lo, b, dims)


def params():
    return pltpu.CompilerParams(vmem_limit_bytes=VMEM_LIMIT)


def in_hbm(x):
    return pltpu.with_memory_space_constraint(x, pltpu.HBM)


def cost(us):
    return pl.CostEstimate(flops=int(us * 5e8), bytes_accessed=int(us * 2e6), transcendentals=0)


def whole(n):
    return [pl.BlockSpec(memory_space=pltpu.VMEM)] * n


def tap_sums(pressures, tap_panel, tap_floor, tap_area, others, panels, floors):
    time, taps = pressures.shape
    rows = panels + floors
    chunks = 2 if time % (2 * BLK) == 0 else 1
    span = time // chunks
    n = len(others)
    given = (tap_panel, tap_floor, tap_area)

    def body(press_hbm, *refs):
        from_refs, sums_ref, kept = refs[: n + 3], refs[n + 3], refs[n + 4 : 2 * n + 4]
        press, panel, floor, area, weights, sems = refs[2 * n + 4 :]
        small = [
            pltpu.make_async_copy(a, b, sems.at[chunks + i])
            for i, (a, b) in enumerate(zip(from_refs, (panel, floor, area, *kept)))
        ]
        large = []
        for i in range(chunks):
            at = pl.ds(i * span, span)
            large.append(pltpu.make_async_copy(press_hbm.at[at], press.at[at], sems.at[i]))
        for copy in [*small[:3], *large, *small[3:]]:
            copy.start()
        for copy in small[:3]:
            copy.wait()
        each = jnp.broadcast_to(area[...].astype(F32).reshape(1, taps), (16, taps))
        row = lax.broadcasted_iota(jnp.int32, (16, taps), 0)
        for ids, first, count in ((panel, 0, panels), (floor, panels, floors)):
            at = jnp.broadcast_to(ids[...], (16, taps)) - row
            for r in range(0, count, 16):
                weights[first + r : first + r + 16] = jnp.where(at == r, each, 0.0).astype(BF)
        for i in range(chunks):
            at = slice(i * span, (i + 1) * span)
            large[i].wait()
            sums_ref[:, at] = dot(weights[...], press[at], NT)
        for copy in small[3:]:
            copy.wait()

    out = pl.pallas_call(
        body,
        in_specs=[pl.BlockSpec(memory_space=pltpu.HBM)] * (n + 4),
        out_specs=tuple(whole(n + 1)),
        out_shape=(jax.ShapeDtypeStruct((rows, time), F32), *(jax.ShapeDtypeStruct(x.shape, x.dtype) for x in others)),
        scratch_shapes=[
            pltpu.VMEM((time, taps), BF),
            *(pltpu.VMEM(x.shape, x.dtype) for x in given),
            pltpu.VMEM((rows, taps), BF),
            pltpu.SemaphoreType.DMA((chunks + n + 3,)),
        ],
        compiler_params=params(),
        cost_estimate=cost(3),
        name="tap_sums",
    )(in_hbm(pressures), *(in_hbm(x) for x in given), *(in_hbm(x) for x in others))
    return out[0], out[1:]


def placed(z, nz):
    if nz != PAIRED:
        return [lax.rem(z + d, nz) for d in range(nz)]
    return [z, lax.rem(z + 2, nz), z + 1 - 2 * lax.rem(z, 2), nz - 1 - z]


def mode_tables(order, decay, freq, panel_shape, floor_shape, nz, nc):
    modes = order.shape[1]
    panels = panel_shape.shape[0]
    floors = floor_shape.shape[0]
    mode_dev = modes // (nz * nc)
    slots = mode_dev * nz
    bits = BLK.bit_length() - 1
    half = BLK // 2

    def body(*refs):
        order_ref, decay_ref, freq_ref, panel_ref, floor_ref = refs[:5]
        pt_ref, fs_ref, tab_ref, turn_ref, own_ref, column_ref = refs[5:]
        column_ref[...] = jnp.broadcast_to(order_ref[...].astype(F32), (TILE, modes)).T
        z, c = lax.axis_index("taps"), lax.axis_index("floors")
        picked = []
        for at in placed(z, nz):
            owner = at * nc + c
            picked.append(column_ref[pl.ds(pl.multiple_of(owner * mode_dev, mode_dev), mode_dev), :])
        column = jnp.concatenate(picked, axis=0)[:, :1]
        ids = lax.broadcasted_iota(jnp.int32, (slots, modes), 1).astype(F32)
        pick = jnp.where(column == ids, 1.0, 0.0).astype(BF)
        pt_ref[...] = dot(pick, panel_ref[...], NT).astype(BF)
        fs_ref[...] = dot(floor_ref[...], pick, NT)
        decays, angles = decay_ref[...], freq_ref[...]
        re, im = jnp.cos(angles), jnp.sin(angles)
        rows = [decays]
        square = decays * decays
        loss = 2.0 * jnp.exp(-decays) * decays * (1.0 + square * (1.0 / 6.0 + square * (1.0 / 120.0)))
        rows.append(jnp.sqrt(loss))
        for _ in range(bits + 1):
            rows += [re, im]
            re, im = re * re - im * im, 2.0 * re * im
        rows += [jnp.zeros_like(re)] * (-len(rows) % 16)
        count = len(rows)
        stack = jnp.concatenate(rows, axis=0)
        hi, mid = split(stack)
        low = (stack - hi.astype(F32) - mid.astype(F32)).astype(BF)
        parts = dot(pick, jnp.concatenate([hi, mid, low], axis=0), NT)
        cols = parts[:, :count] + parts[:, count : 2 * count] + parts[:, 2 * count : 3 * count]
        rate, gain = cols[:, 0:1], cols[:, 1:2]
        lane = lax.broadcasted_iota(jnp.int32, (slots, half), 1)
        cos = jnp.where((lane & 1) != 0, cols[:, 2:3], 1.0)
        sin = jnp.where((lane & 1) != 0, cols[:, 3:4], 0.0)
        for b in range(1, bits - 1):
            on = (lane & (1 << b)) != 0
            step = cols[:, 2 + 2 * b : 3 + 2 * b], cols[:, 3 + 2 * b : 4 + 2 * b]
            new_cos, new_sin = turned((cos, sin), step)
            cos, sin = jnp.where(on, new_cos, cos), jnp.where(on, new_sin, sin)
        at = 2 * bits
        far_cos, far_sin = turned((cos, sin), (cols[:, at : at + 1], cols[:, at + 1 : at + 2]))
        steps = rate * lane.astype(F32)
        shrink, grow = jnp.exp(-steps), gain * jnp.exp(steps)
        far_shrink = shrink * jnp.exp(-rate * float(half))
        far_grow = grow * jnp.exp(rate * float(half))
        near, far = slice(0, half), slice(half, BLK)
        tab_ref[0, :, near], tab_ref[0, :, far] = grow * cos, far_grow * far_cos
        tab_ref[1, :, near], tab_ref[1, :, far] = -grow * sin, -far_grow * far_sin
        tab_ref[2, :, near], tab_ref[2, :, far] = shrink * cos, far_shrink * far_cos
        tab_ref[3, :, near], tab_ref[3, :, far] = shrink * sin, far_shrink * far_sin
        fade = jnp.exp(-rate * float(BLK))
        turn_ref[...] = fade * cols[:, at + 2 : at + 4]
        own_ref[...] = tab_ref[:, :mode_dev]

    return pl.pallas_call(
        body,
        in_specs=whole(5),
        out_specs=tuple(whole(5)),
        out_shape=(
            jax.ShapeDtypeStruct((slots, panels), BF),
            jax.ShapeDtypeStruct((floors, slots), F32),
            jax.ShapeDtypeStruct((4, slots, BLK), F32),
            jax.ShapeDtypeStruct((slots, 2), F32),
            jax.ShapeDtypeStruct((4, mode_dev, BLK), F32),
        ),
        scratch_shapes=[pltpu.VMEM((modes, TILE), F32)],
        compiler_params=params(),
        cost_estimate=cost(2),
        name="mode_tables",
    )(order, decay, freq, panel_shape, floor_shape)


def direct_until(time):
    return time // 4 // BLK * BLK


def send_plan(nz, time):
    until = direct_until(time)
    if nz != PAIRED or not until:
        return [(p, 0, time) for p in range(nz)]
    return [(0, 0, time), (1, until, time), (2, 0, time), (3, until, time), (1, 0, until), (3, 0, until)]


def slot_forces(sums, pt, tables, turns, nz, before):
    slots, panels = pt.shape
    rows, time = sums[0].shape
    nc = len(sums)
    mode_dev = slots // nz
    plan = send_plan(nz, time)
    n = len(before)

    def body(*refs):
        sum_refs, (pt_ref, tab_ref, turn_ref) = refs[:nc], refs[nc : nc + 3]
        before_refs, out_refs = refs[nc + 3 : nc + 3 + n], refs[nc + 3 + n : -3]
        load_ref, state_refs = refs[-3], refs[-2:]
        load = sum_refs[0][panels:]
        for ref in sum_refs[1:]:
            load = load + ref[panels:]
        load_ref[...] = load
        left = pt_ref[...]
        turn = turn_ref[:, 0:1], turn_ref[:, 1:2]
        state = [ref[...] for ref in before_refs]
        for b in range(time // BLK):
            cols = slice(b * BLK, (b + 1) * BLK)
            total = sum_refs[0][:panels, cols]
            for ref in sum_refs[1:]:
                total = total + ref[:panels, cols]
            forces = dot_exact_left(left, total)
            for ref, (p, start, stop) in zip(out_refs, plan):
                if start <= b * BLK < stop:
                    at = slice(b * BLK - start, (b + 1) * BLK - start)
                    ref[:, at] = forces[p * mode_dev : (p + 1) * mode_dev]
            new = []
            for part in (forces * tab_ref[0], forces * tab_ref[1]):
                near = part[:, :TILE]
                for k in range(TILE, BLK, TILE):
                    near = near + part[:, k : k + TILE]
                new.append(near)
            if state:
                new = [a + b for a, b in zip(new, state)]
            state = turned(turn, new)
        state_refs[0][...], state_refs[1][...] = state

    out = pl.pallas_call(
        body,
        in_specs=whole(nc + 3 + n),
        out_specs=whole(len(plan) + 3),
        out_shape=[jax.ShapeDtypeStruct((mode_dev, stop - start), F32) for _, start, stop in plan]
        + [jax.ShapeDtypeStruct((rows - panels, time), F32)]
        + [jax.ShapeDtypeStruct((slots, TILE), F32)] * 2,
        compiler_params=params(),
        cost_estimate=cost(1),
        name="slot_forces",
    )(*sums, pt, tables, turns, *before)
    return out[:-3], out[-3], out[-2:]


def end_states(spread, turns, after):
    slots = turns.shape[0]

    def body(re_ref, im_ref, turn_ref, after_ref, out_ref):
        pad = jnp.zeros((TILE, TILE - 4), F32)
        for k in range(0, slots, TILE):
            at = slice(k, k + TILE)
            state = [jnp.sum(ref[at], axis=1, keepdims=True) for ref in (re_ref, im_ref)]
            four = [*state, turn_ref[at, 0:1], turn_ref[at, 1:2]]
            out_ref[:, at] = jnp.concatenate([*four, pad], axis=1).T[:8]

    return pl.pallas_call(
        body,
        in_specs=whole(4),
        out_specs=whole(1)[0],
        out_shape=jax.ShapeDtypeStruct((8, slots), F32),
        compiler_params=params(),
        cost_estimate=cost(1),
        name="end_states",
    )(*spread, turns, after)


def triangle():
    row = lax.broadcasted_iota(jnp.int32, (BLK, BLK), 0)
    col = lax.broadcasted_iota(jnp.int32, (BLK, BLK), 1)
    return jnp.where(row <= col, 1.0, 0.0).astype(BF)


def turned(a, b):
    return (a[0] * b[0] - a[1] * b[1], a[0] * b[1] + a[1] * b[0])


def motion_from_rest(forces, tables, turns, floor_slots):
    slots = turns.shape[0]
    floors = floor_slots.shape[0]
    time = max(start + x.shape[1] for x, _, start in forces)
    blocks = time // BLK
    n = len(forces)
    places = [(row, start, x.shape) for x, row, start in forces]

    def body(*refs):
        tab_ref, turn_ref, fs_ref, motion_ref = refs[n:]
        tri = triangle()
        here = fs_ref[...].astype(BF)
        turn = turn_ref[:, 0:1], turn_ref[:, 1:2]
        state = None
        for b in range(blocks):
            found = [
                (row, ref[:, b * BLK - start : (b + 1) * BLK - start])
                for ref, (row, start, shape) in zip(refs, places)
                if start <= b * BLK < start + shape[1]
            ]
            force = jnp.concatenate([x for _, x in sorted(found, key=lambda f: f[0])], axis=0)
            cr = dot_exact_right(force * tab_ref[0], tri)
            ci = dot_exact_right(force * tab_ref[1], tri)
            if state is not None:
                cr, ci = cr + state[0], ci + state[1]
            part = dot_exact_left(here, tab_ref[2] * cr - tab_ref[3] * ci)
            motion_ref[:, b * BLK : (b + 1) * BLK] = part
            if b < blocks - 1:
                state = turned(turn, (cr[:, BLK - 1 :], ci[:, BLK - 1 :]))

    return pl.pallas_call(
        body,
        in_specs=whole(n + 3),
        out_specs=whole(1)[0],
        out_shape=jax.ShapeDtypeStruct((floors, time), F32),
        compiler_params=params(),
        cost_estimate=cost(2),
        name="motion_from_rest",
    )(*(x for x, _, _ in forces), tables, turns, floor_slots)


def floor_shares(motion, ends, enter, tables, floor_slots, onward):
    floors, time = motion.shape
    blocks = time // BLK
    n = len(onward)

    def body(motion_ref, ends_ref, enter_ref, tab_ref, fs_ref, *refs):
        out_ref = refs[n]
        if n:
            refs[n + 1][...] = refs[0][...] + refs[1][...]
        shape = fs_ref[...]
        turn = (ends_ref[2:3, :], ends_ref[3:4, :])
        later = lax.axis_index("tm") > 0
        state = tuple(jnp.where(later, enter_ref[i : i + 1, :], 0.0) for i in (0, 1))
        left_re, left_im = [], []
        for b in range(blocks):
            left_re.append(shape * state[0])
            left_im.append(shape * state[1])
            state = turned(turn, state)
        qr_hi, qr_lo = split(tab_ref[2])
        qi_hi, qi_lo = split(tab_ref[3])
        re_hi, re_lo = split(jnp.concatenate(left_re, axis=0))
        im_hi, im_lo = split(jnp.concatenate(left_im, axis=0))
        free = dot(re_hi, qr_hi) + dot(re_hi, qr_lo) + dot(re_lo, qr_hi)
        free = free - (dot(im_hi, qi_hi) + dot(im_hi, qi_lo) + dot(im_lo, qi_hi))
        for b in range(blocks):
            cols = slice(b * BLK, (b + 1) * BLK)
            out_ref[:, cols] = motion_ref[:, cols] + free[b * floors : (b + 1) * floors]

    return pl.pallas_call(
        body,
        in_specs=whole(5 + n),
        out_specs=whole(1 + len(onward[:1])),
        out_shape=[
            jax.ShapeDtypeStruct(x, F32) for x in [(floors, time)] + [x.shape for x in onward[:1]]
        ],
        compiler_params=params(),
        cost_estimate=cost(1),
        name="floor_shares",
    )(motion, ends, enter, tables, floor_slots, *onward)


def owner_shares(motions, loads, enter, direct, begin, nz, floor_dev):
    nc, parts = len(motions), len(loads)
    floors, time = motions[0].shape
    rows, cols = share_shape(floor_dev, time)
    owners = nz * nc
    mode_dev = enter.shape[1] // nz
    span = time // parts
    n, m = len(direct), len(begin)
    half = time // 2
    shapes = [(rows, cols)] * nz
    if n:
        shapes[2] = (mode_dev + 2 * rows, half)
        shapes += [(mode_dev, half), begin[0].shape]

    def body(*refs):
        motion_refs, load_refs, enter_ref = refs[:nc], refs[nc : nc + parts], refs[nc + parts]
        more, out_refs = refs[nc + parts + 1 : nc + parts + 1 + n + m], refs[nc + parts + 1 + n + m : -3]
        motion_all, load_all, share_ref = refs[-3:]
        if n:
            out_refs[2][:mode_dev] = more[0][:, :half]
            out_refs[nz][...] = more[0][:, half:]
            out_refs[nz + 1][...] = more[1][...] + more[2][...]
        z, c = lax.axis_index("taps"), lax.axis_index("floors")
        later = lax.axis_index("tm") > 0
        motion = motion_refs[0][...]
        for ref in motion_refs[1:]:
            motion = motion + ref[...]
        for o in range(owners):
            at = slice(o * floor_dev, (o + 1) * floor_dev)
            motion_all[o] = motion[at]
            for k in range(parts):
                load_all[o, :, k * span : (k + 1) * span] = load_refs[k][at]
        for p, place in enumerate(placed(z, nz)):
            owner = place * nc + c
            out = share_ref if n and p == 2 else out_refs[p]
            out[...] = jnp.zeros((rows, cols), F32)
            for k, ref in enumerate((motion_all, load_all)):
                for h in (0, 1):
                    at = slice((2 * k + h) * floor_dev, (2 * k + h + 1) * floor_dev)
                    out[at, :half] = ref[owner, :, h * half : (h + 1) * half]
            state = enter_ref[0:2, p * mode_dev : (p + 1) * mode_dev]
            out[:2, half : half + mode_dev] = jnp.where(later, state, 0.0)
        if n:
            out_refs[2][mode_dev : mode_dev + rows] = share_ref[:, :half]
            out_refs[2][mode_dev + rows :, :TILE] = share_ref[:, half:]
            out_refs[2][mode_dev + rows :, TILE:] = jnp.zeros((rows, half - TILE), F32)

    return pl.pallas_call(
        body,
        in_specs=whole(nc + parts + 1 + n + m),
        out_specs=whole(len(shapes)),
        out_shape=[jax.ShapeDtypeStruct(x, F32) for x in shapes],
        scratch_shapes=[pltpu.VMEM((owners, floor_dev, time), F32)] * 2 + [pltpu.VMEM((rows, cols), F32)],
        compiler_params=params(),
        cost_estimate=cost(1),
        name="owner_shares",
    )(*motions, *loads, enter, *direct, *begin)


def share_shape(floor_dev, time):
    return -(-4 * floor_dev // 8) * 8, time // 2 + TILE


def block_sums(force, tables, tri):
    return [dot_exact_right(force * table, tri) for table in tables]


def sum_at(refs, forces, b, mode_dev):
    total = None
    for ref, (x, row, start) in zip(refs, forces):
        if start <= b * BLK < start + x.shape[1]:
            part = ref[row : row + mode_dev, b * BLK - start : (b + 1) * BLK - start]
            total = part if total is None else total + part
    return total


def own_response(forces, shares, tables, turns, floor_dev, load_scale):
    mode_dev = forces[0][0].shape[0]
    n, m = len(shares), len(forces)
    half = shares[0][0].shape[1] - TILE
    time = 2 * half
    rows, width = share_shape(floor_dev, time)
    blocks = time // BLK

    def body(*refs):
        tab_ref, turn_ref, resp_ref, motion_ref, load_ref, share_ref = refs[m + n :]
        for i, (_, row, start, stop) in enumerate(shares):
            at = slice(start, stop)
            part = refs[m + i][row : row + rows, : stop - start]
            share_ref[:, at] = part if i == 0 else share_ref[:, at] + part
        share = share_ref[...]
        for h in (0, 1):
            at = slice(h * half, (h + 1) * half)
            motion_ref[:, at] = share[h * floor_dev : (h + 1) * floor_dev, :half]
            load_ref[:, at] = share[(2 + h) * floor_dev : (3 + h) * floor_dev, :half] * load_scale
        qr, qi = tab_ref[2], tab_ref[3]
        turn = turn_ref[:mode_dev, 0:1], turn_ref[:mode_dev, 1:2]
        column = share[:, half:].T
        state = column[:mode_dev, 0:1], column[:mode_dev, 1:2]
        tri = triangle()
        for b in range(blocks):
            sums = block_sums(sum_at(refs, forces, b, mode_dev), (tab_ref[0], tab_ref[1]), tri)
            cr, ci = (x + y for x, y in zip(sums, state))
            resp_ref[:, b * BLK : (b + 1) * BLK] = qr * cr - qi * ci
            state = turned(turn, (cr[:, BLK - 1 :], ci[:, BLK - 1 :]))

    return pl.pallas_call(
        body,
        in_specs=whole(m + n + 2),
        out_specs=tuple(whole(3)),
        out_shape=(
            jax.ShapeDtypeStruct((mode_dev, time), F32),
            jax.ShapeDtypeStruct((floor_dev, time), F32),
            jax.ShapeDtypeStruct((floor_dev, time), F32),
        ),
        scratch_shapes=[pltpu.VMEM((rows, width), F32)],
        compiler_params=params(),
        cost_estimate=cost(1),
        name="own_response",
    )(*(x for x, _, _ in forces), *(x[0] for x in shares), tables, turns)


def shifts(x, axis, n):
    return [lax.ppermute(x, axis, [(i, (i + d) % n) for i in range(n)]) for d in range(1, n)]


def along(parts, n):
    return [parts[0]] + [
        lax.ppermute(parts[d], "taps", [(i, (i + d) % n) for i in range(n)]) for d in range(1, n)
    ]


def on_device(
    pressures,
    tap_area,
    tap_panel,
    tap_floor,
    panel_shape,
    floor_shape,
    mode_order,
    mode_decay,
    mode_freq,
):
    nz = lax.axis_size("taps")
    nc = lax.axis_size("floors")
    nt = lax.axis_size("tm")
    owners = nz * nc
    modes = mode_order.shape[0]
    mode_dev = modes // owners
    time, taps = pressures.shape
    panels = panel_shape.shape[0]
    floors = floor_shape.shape[0]
    floor_dev = floors // owners
    load_scale = (floors / (taps * owners)) ** 0.5

    mine, kept = tap_sums(
        pressures,
        tap_panel[None],
        tap_floor[None],
        tap_area,
        (mode_order[None], mode_decay[None], mode_freq[None], panel_shape, floor_shape),
        panels,
        floors,
    )
    sums = [[mine] + shifts(mine, "floors", nc)]
    pt, floor_slots, tables, turns, own = mode_tables(*kept, nz, nc)
    forces, loads, spread = [], [], []
    for part in sums:
        force, load, spread = slot_forces(part, pt, tables, turns, nz, spread)
        forces.append(force)
        loads.append(load)
    pair, two, mirror = ([(i, i ^ d) for i in range(nz)] for d in (1, 2, 3))
    until = direct_until(time)
    laid = [(x, p * mode_dev, start) for x, (p, start, _) in zip(forces[0], send_plan(nz, time))]
    if nz == PAIRED:
        onward = [forces[0][1], lax.ppermute(forces[0][3], "taps", pair)]
        direct = [forces[0][2]]
        begin = [lax.ppermute(x, "taps", way) for x, way in zip(forces[0][4:], (two, mirror))]
    else:
        crossed, onward = [(x, 0, 0) for x in along(forces[0], nz)], []
        direct, begin = [], []
    motion = motion_from_rest(laid, tables, turns, floor_slots)
    ends = end_states(spread, turns, turns)
    enter = jnp.zeros_like(ends)
    for hop in range(nt - 1):
        passed = ends
        if hop:
            turn = (ends[2:3], ends[3:4])
            over = turn
            for _ in range(time // BLK - 1):
                over = turned(over, turn)
            enter = jnp.where(lax.axis_index("tm") > 0, enter, 0.0)
            passed = ends + jnp.concatenate(
                [*turned(over, (enter[0:1], enter[1:2])), jnp.zeros_like(ends[2:])]
            )
        enter = lax.ppermute(passed, "tm", [(i, (i + 1) % nt) for i in range(nt)])
    motion, *onward = floor_shares(motion, ends, enter, tables, floor_slots, onward)
    motions = [motion] + shifts(motion, "floors", nc)
    shares = owner_shares(motions, loads, enter, direct, begin, nz, floor_dev)
    if nz == PAIRED:
        ways = (two, pair, mirror, pair)
        away, near, far, rest = (lax.ppermute(x, "taps", way) for x, way in zip(shares[1:5], ways))
        onward = lax.ppermute(onward[0], "taps", two)
        half, (rows, cols) = time // 2, share_shape(floor_dev, time)
        crossed = [(forces[0][0], 0, 0), (near, 0, 0), (rest, 0, half)]
        crossed += [(shares[5], 0, 0), (onward, 0, until)]
        shares = [(x, 0, 0, cols) for x in (shares[0], away, far)]
        shares += [(near, mode_dev, 0, half), (near, mode_dev + rows, half, cols)]
    else:
        shares = [(x, 0, 0, x.shape[1]) for x in along(shares, nz)]
    return own_response(crossed, shares, own, turns, floor_dev, load_scale)


def solution(mesh):
    in_specs = (
        P(("dirs", "tm"), ("taps", "floors")),
        P(("taps", "floors")),
        P(("taps", "floors")),
        P(("taps", "floors")),
        P(),
        P(),
        P(),
        P(),
        P(),
    )
    out_specs = (
        P(("taps", "floors"), ("dirs", "tm")),
        P(("taps", "floors"), ("dirs", "tm")),
        P(("taps", "floors"), ("dirs", "tm")),
    )
    return jax.shard_map(
        on_device, mesh=mesh, in_specs=in_specs, out_specs=out_specs, check_vma=False
    )
```

```python
import jax
import jax.numpy as jnp
from jax import lax
from jax.experimental import pallas as pl
from jax.experimental.pallas import tpu as pltpu
from jax.sharding import PartitionSpec as P

BLK = 256
PAIRED = 4
TILE = 128
BF = jnp.bfloat16
F32 = jnp.float32
NN = (((1,), (0,)), ((), ()))
NT = (((1,), (1,)), ((), ()))
VMEM_LIMIT = 16 * 1024 * 1024


def dot(a, b, dims=NN):
    return lax.dot_general(a, b, dims, preferred_element_type=F32)


def split(x):
    hi = x.astype(BF)
    return hi, (x - hi.astype(F32)).astype(BF)


def dot_exact_left(a, x, dims=NN):
    hi, lo = split(x)
    return dot(a, hi, dims) + dot(a, lo, dims)


def dot_exact_right(x, b, dims=NN):
    hi, lo = split(x)
    return dot(hi, b, dims) + dot(lo, b, dims)


def params():
    return pltpu.CompilerParams(vmem_limit_bytes=VMEM_LIMIT)


def in_hbm(x):
    return pltpu.with_memory_space_constraint(x, pltpu.HBM)


def cost(us):
    return pl.CostEstimate(flops=int(us * 5e8), bytes_accessed=int(us * 2e6), transcendentals=0)


def whole(n):
    return [pl.BlockSpec(memory_space=pltpu.VMEM)] * n


def tap_sums(pressures, tap_panel, tap_floor, tap_area, others, panels, floors):
    time, taps = pressures.shape
    rows = panels + floors
    chunks = 2 if time % (2 * BLK) == 0 else 1
    span = time // chunks
    n = len(others)
    given = (tap_panel, tap_floor, tap_area)

    def body(press_hbm, *refs):
        from_refs, sums_ref, kept = refs[: n + 3], refs[n + 3], refs[n + 4 : 2 * n + 4]
        press, panel, floor, area, weights, sems = refs[2 * n + 4 :]
        small = [
            pltpu.make_async_copy(a, b, sems.at[chunks + i])
            for i, (a, b) in enumerate(zip(from_refs, (panel, floor, area, *kept)))
        ]
        large = []
        for i in range(chunks):
            at = pl.ds(i * span, span)
            large.append(pltpu.make_async_copy(press_hbm.at[at], press.at[at], sems.at[i]))
        for copy in [*small[:3], *large, *small[3:]]:
            copy.start()
        for copy in small[:3]:
            copy.wait()
        each = jnp.broadcast_to(area[...].astype(F32).reshape(1, taps), (16, taps))
        row = lax.broadcasted_iota(jnp.int32, (16, taps), 0)
        for ids, first, count in ((panel, 0, panels), (floor, panels, floors)):
            at = jnp.broadcast_to(ids[...], (16, taps)) - row
            for r in range(0, count, 16):
                weights[first + r : first + r + 16] = jnp.where(at == r, each, 0.0).astype(BF)
        for i in range(chunks):
            at = slice(i * span, (i + 1) * span)
            large[i].wait()
            sums_ref[:, at] = dot(weights[...], press[at], NT)
        for copy in small[3:]:
            copy.wait()

    out = pl.pallas_call(
        body,
        in_specs=[pl.BlockSpec(memory_space=pltpu.HBM)] * (n + 4),
        out_specs=tuple(whole(n + 1)),
        out_shape=(jax.ShapeDtypeStruct((rows, time), F32), *(jax.ShapeDtypeStruct(x.shape, x.dtype) for x in others)),
        scratch_shapes=[
            pltpu.VMEM((time, taps), BF),
            *(pltpu.VMEM(x.shape, x.dtype) for x in given),
            pltpu.VMEM((rows, taps), BF),
            pltpu.SemaphoreType.DMA((chunks + n + 3,)),
        ],
        compiler_params=params(),
        cost_estimate=cost(3),
        name="tap_sums",
    )(in_hbm(pressures), *(in_hbm(x) for x in given), *(in_hbm(x) for x in others))
    return out[0], out[1:]


def placed(z, nz):
    if nz != PAIRED:
        return [lax.rem(z + d, nz) for d in range(nz)]
    return [z, lax.rem(z + 2, nz), z + 1 - 2 * lax.rem(z, 2), nz - 1 - z]


def mode_tables(order, decay, freq, panel_shape, floor_shape, nz, nc):
    modes = order.shape[1]
    panels = panel_shape.shape[0]
    floors = floor_shape.shape[0]
    mode_dev = modes // (nz * nc)
    slots = mode_dev * nz
    bits = BLK.bit_length() - 1
    half = BLK // 2

    def body(*refs):
        order_ref, decay_ref, freq_ref, panel_ref, floor_ref = refs[:5]
        pt_ref, fs_ref, tab_ref, turn_ref, own_ref, column_ref = refs[5:]
        column_ref[...] = jnp.broadcast_to(order_ref[...].astype(F32), (TILE, modes)).T
        z, c = lax.axis_index("taps"), lax.axis_index("floors")
        picked = []
        for at in placed(z, nz):
            owner = at * nc + c
            picked.append(column_ref[pl.ds(pl.multiple_of(owner * mode_dev, mode_dev), mode_dev), :])
        column = jnp.concatenate(picked, axis=0)[:, :1]
        ids = lax.broadcasted_iota(jnp.int32, (slots, modes), 1).astype(F32)
        pick = jnp.where(column == ids, 1.0, 0.0).astype(BF)
        pt_ref[...] = dot(pick, panel_ref[...], NT).astype(BF)
        fs_ref[...] = dot(floor_ref[...], pick, NT)
        decays, angles = decay_ref[...], freq_ref[...]
        re, im = jnp.cos(angles), jnp.sin(angles)
        rows = [decays]
        square = decays * decays
        loss = 2.0 * jnp.exp(-decays) * decays * (1.0 + square * (1.0 / 6.0 + square * (1.0 / 120.0)))
        rows.append(jnp.sqrt(loss))
        for _ in range(bits + 1):
            rows += [re, im]
            re, im = re * re - im * im, 2.0 * re * im
        rows += [jnp.zeros_like(re)] * (-len(rows) % 16)
        count = len(rows)
        stack = jnp.concatenate(rows, axis=0)
        hi, mid = split(stack)
        low = (stack - hi.astype(F32) - mid.astype(F32)).astype(BF)
        parts = dot(pick, jnp.concatenate([hi, mid, low], axis=0), NT)
        cols = parts[:, :count] + parts[:, count : 2 * count] + parts[:, 2 * count : 3 * count]
        rate, gain = cols[:, 0:1], cols[:, 1:2]
        lane = lax.broadcasted_iota(jnp.int32, (slots, half), 1)
        cos = jnp.where((lane & 1) != 0, cols[:, 2:3], 1.0)
        sin = jnp.where((lane & 1) != 0, cols[:, 3:4], 0.0)
        for b in range(1, bits - 1):
            on = (lane & (1 << b)) != 0
            step = cols[:, 2 + 2 * b : 3 + 2 * b], cols[:, 3 + 2 * b : 4 + 2 * b]
            new_cos, new_sin = turned((cos, sin), step)
            cos, sin = jnp.where(on, new_cos, cos), jnp.where(on, new_sin, sin)
        at = 2 * bits
        far_cos, far_sin = turned((cos, sin), (cols[:, at : at + 1], cols[:, at + 1 : at + 2]))
        steps = rate * lane.astype(F32)
        shrink, grow = jnp.exp(-steps), gain * jnp.exp(steps)
        far_shrink = shrink * jnp.exp(-rate * float(half))
        far_grow = grow * jnp.exp(rate * float(half))
        near, far = slice(0, half), slice(half, BLK)
        tab_ref[0, :, near], tab_ref[0, :, far] = grow * cos, far_grow * far_cos
        tab_ref[1, :, near], tab_ref[1, :, far] = -grow * sin, -far_grow * far_sin
        tab_ref[2, :, near], tab_ref[2, :, far] = shrink * cos, far_shrink * far_cos
        tab_ref[3, :, near], tab_ref[3, :, far] = shrink * sin, far_shrink * far_sin
        fade = jnp.exp(-rate * float(BLK))
        turn_ref[...] = fade * cols[:, at + 2 : at + 4]
        own_ref[...] = tab_ref[:, :mode_dev]

    return pl.pallas_call(
        body,
        in_specs=whole(5),
        out_specs=tuple(whole(5)),
        out_shape=(
            jax.ShapeDtypeStruct((slots, panels), BF),
            jax.ShapeDtypeStruct((floors, slots), F32),
            jax.ShapeDtypeStruct((4, slots, BLK), F32),
            jax.ShapeDtypeStruct((slots, 2), F32),
            jax.ShapeDtypeStruct((4, mode_dev, BLK), F32),
        ),
        scratch_shapes=[pltpu.VMEM((modes, TILE), F32)],
        compiler_params=params(),
        cost_estimate=cost(2),
        name="mode_tables",
    )(order, decay, freq, panel_shape, floor_shape)


def direct_until(time):
    return time // 4 // BLK * BLK


def send_plan(nz, time):
    until = direct_until(time)
    if nz != PAIRED or not until:
        return [(p, 0, time) for p in range(nz)]
    return [(0, 0, time), (1, until, time), (2, 0, time), (3, until, time), (1, 0, until), (3, 0, until)]


def slot_forces(sums, pt, tables, turns, nz, before):
    slots, panels = pt.shape
    rows, time = sums[0].shape
    nc = len(sums)
    mode_dev = slots // nz
    plan = send_plan(nz, time)
    n = len(before)

    def body(*refs):
        sum_refs, (pt_ref, tab_ref, turn_ref) = refs[:nc], refs[nc : nc + 3]
        before_refs, out_refs = refs[nc + 3 : nc + 3 + n], refs[nc + 3 + n : -3]
        load_ref, state_refs = refs[-3], refs[-2:]
        load = sum_refs[0][panels:]
        for ref in sum_refs[1:]:
            load = load + ref[panels:]
        load_ref[...] = load
        left = pt_ref[...]
        turn = turn_ref[:, 0:1], turn_ref[:, 1:2]
        state = [ref[...] for ref in before_refs]
        for b in range(time // BLK):
            cols = slice(b * BLK, (b + 1) * BLK)
            total = sum_refs[0][:panels, cols]
            for ref in sum_refs[1:]:
                total = total + ref[:panels, cols]
            forces = dot_exact_left(left, total)
            for ref, (p, start, stop) in zip(out_refs, plan):
                if start <= b * BLK < stop:
                    at = slice(b * BLK - start, (b + 1) * BLK - start)
                    ref[:, at] = forces[p * mode_dev : (p + 1) * mode_dev]
            new = []
            for part in (forces * tab_ref[0], forces * tab_ref[1]):
                near = part[:, :TILE]
                for k in range(TILE, BLK, TILE):
                    near = near + part[:, k : k + TILE]
                new.append(near)
            if state:
                new = [a + b for a, b in zip(new, state)]
            state = turned(turn, new)
        state_refs[0][...], state_refs[1][...] = state

    out = pl.pallas_call(
        body,
        in_specs=whole(nc + 3 + n),
        out_specs=whole(len(plan) + 3),
        out_shape=[jax.ShapeDtypeStruct((mode_dev, stop - start), F32) for _, start, stop in plan]
        + [jax.ShapeDtypeStruct((rows - panels, time), F32)]
        + [jax.ShapeDtypeStruct((slots, TILE), F32)] * 2,
        compiler_params=params(),
        cost_estimate=cost(1),
        name="slot_forces",
    )(*sums, pt, tables, turns, *before)
    return out[:-3], out[-3], out[-2:]


def end_states(spread, turns, after):
    slots = turns.shape[0]

    def body(re_ref, im_ref, turn_ref, after_ref, out_ref):
        pad = jnp.zeros((TILE, TILE - 4), F32)
        for k in range(0, slots, TILE):
            at = slice(k, k + TILE)
            state = [jnp.sum(ref[at], axis=1, keepdims=True) for ref in (re_ref, im_ref)]
            four = [*state, turn_ref[at, 0:1], turn_ref[at, 1:2]]
            out_ref[:, at] = jnp.concatenate([*four, pad], axis=1).T[:8]

    return pl.pallas_call(
        body,
        in_specs=whole(4),
        out_specs=whole(1)[0],
        out_shape=jax.ShapeDtypeStruct((8, slots), F32),
        compiler_params=params(),
        cost_estimate=cost(1),
        name="end_states",
    )(*spread, turns, after)


def triangle():
    row = lax.broadcasted_iota(jnp.int32, (BLK, BLK), 0)
    col = lax.broadcasted_iota(jnp.int32, (BLK, BLK), 1)
    return jnp.where(row <= col, 1.0, 0.0).astype(BF)


def turned(a, b):
    return (a[0] * b[0] - a[1] * b[1], a[0] * b[1] + a[1] * b[0])


def motion_from_rest(forces, tables, turns, floor_slots):
    slots = turns.shape[0]
    floors = floor_slots.shape[0]
    time = max(start + x.shape[1] for x, _, start in forces)
    blocks = time // BLK
    n = len(forces)
    places = [(row, start, x.shape) for x, row, start in forces]

    def body(*refs):
        tab_ref, turn_ref, fs_ref, motion_ref = refs[n:]
        tri = triangle()
        here = fs_ref[...].astype(BF)
        turn = [spread(turn_ref[:, i : i + 1]) for i in (0, 1)]
        state = None
        for b in range(blocks):
            found = [
                (row, ref[:, b * BLK - start : (b + 1) * BLK - start])
                for ref, (row, start, shape) in zip(refs, places)
                if start <= b * BLK < start + shape[1]
            ]
            force = jnp.concatenate([x for _, x in sorted(found, key=lambda f: f[0])], axis=0)
            cr, ci = block_sums(force, (tab_ref[0], tab_ref[1]), tri)
            last = [spread(x[:, BLK - 1 :]) for x in (cr, ci)]
            if state is not None:
                cr, ci = cr + widened(state[0]), ci + widened(state[1])
                last = [x + y for x, y in zip(last, state)]
            part = dot_exact_left(here, tab_ref[2] * cr - tab_ref[3] * ci)
            motion_ref[:, b * BLK : (b + 1) * BLK] = part
            state = turned(turn, last)

    return pl.pallas_call(
        body,
        in_specs=whole(n + 3),
        out_specs=whole(1)[0],
        out_shape=jax.ShapeDtypeStruct((floors, time), F32),
        compiler_params=params(),
        cost_estimate=cost(2),
        name="motion_from_rest",
    )(*(x for x, _, _ in forces), tables, turns, floor_slots)


def floor_shares(motion, ends, enter, tables, floor_slots, onward):
    floors, time = motion.shape
    blocks = time // BLK
    n = len(onward)

    def body(motion_ref, ends_ref, enter_ref, tab_ref, fs_ref, *refs):
        out_ref = refs[n]
        if n:
            refs[n + 1][...] = refs[0][...] + refs[1][...]
        shape = fs_ref[...]
        turn = (ends_ref[2:3, :], ends_ref[3:4, :])
        later = lax.axis_index("tm") > 0
        state = tuple(jnp.where(later, enter_ref[i : i + 1, :], 0.0) for i in (0, 1))
        left_re, left_im = [], []
        for b in range(blocks):
            left_re.append(shape * state[0])
            left_im.append(shape * state[1])
            state = turned(turn, state)
        qr_hi, qr_lo = split(tab_ref[2])
        qi_hi, qi_lo = split(tab_ref[3])
        re_hi, re_lo = split(jnp.concatenate(left_re, axis=0))
        im_hi, im_lo = split(jnp.concatenate(left_im, axis=0))
        free = dot(re_hi, qr_hi) + dot(re_hi, qr_lo) + dot(re_lo, qr_hi)
        free = free - (dot(im_hi, qi_hi) + dot(im_hi, qi_lo) + dot(im_lo, qi_hi))
        for b in range(blocks):
            cols = slice(b * BLK, (b + 1) * BLK)
            out_ref[:, cols] = motion_ref[:, cols] + free[b * floors : (b + 1) * floors]

    return pl.pallas_call(
        body,
        in_specs=whole(5 + n),
        out_specs=whole(1 + len(onward[:1])),
        out_shape=[
            jax.ShapeDtypeStruct(x, F32) for x in [(floors, time)] + [x.shape for x in onward[:1]]
        ],
        compiler_params=params(),
        cost_estimate=cost(1),
        name="floor_shares",
    )(motion, ends, enter, tables, floor_slots, *onward)


def owner_shares(motions, loads, enter, direct, begin, nz, floor_dev):
    nc, parts = len(motions), len(loads)
    floors, time = motions[0].shape
    rows, cols = share_shape(floor_dev, time)
    owners = nz * nc
    mode_dev = enter.shape[1] // nz
    span = time // parts
    n, m = len(direct), len(begin)
    half = time // 2
    shapes = [(rows, cols)] * nz
    if n:
        shapes[2] = (mode_dev + 2 * rows, half)
        shapes += [(mode_dev, half), begin[0].shape]

    def body(*refs):
        motion_refs, load_refs, enter_ref = refs[:nc], refs[nc : nc + parts], refs[nc + parts]
        more, out_refs = refs[nc + parts + 1 : nc + parts + 1 + n + m], refs[nc + parts + 1 + n + m : -3]
        motion_all, load_all, share_ref = refs[-3:]
        if n:
            out_refs[2][:mode_dev] = more[0][:, :half]
            out_refs[nz][...] = more[0][:, half:]
            out_refs[nz + 1][...] = more[1][...] + more[2][...]
        z, c = lax.axis_index("taps"), lax.axis_index("floors")
        later = lax.axis_index("tm") > 0
        motion = motion_refs[0][...]
        for ref in motion_refs[1:]:
            motion = motion + ref[...]
        for o in range(owners):
            at = slice(o * floor_dev, (o + 1) * floor_dev)
            motion_all[o] = motion[at]
            for k in range(parts):
                load_all[o, :, k * span : (k + 1) * span] = load_refs[k][at]
        for p, place in enumerate(placed(z, nz)):
            owner = place * nc + c
            out = share_ref if n and p == 2 else out_refs[p]
            out[...] = jnp.zeros((rows, cols), F32)
            for k, ref in enumerate((motion_all, load_all)):
                for h in (0, 1):
                    at = slice((2 * k + h) * floor_dev, (2 * k + h + 1) * floor_dev)
                    out[at, :half] = ref[owner, :, h * half : (h + 1) * half]
            state = enter_ref[0:2, p * mode_dev : (p + 1) * mode_dev]
            out[:2, half : half + mode_dev] = jnp.where(later, state, 0.0)
        if n:
            out_refs[2][mode_dev : mode_dev + rows] = share_ref[:, :half]
            out_refs[2][mode_dev + rows :, :TILE] = share_ref[:, half:]
            out_refs[2][mode_dev + rows :, TILE:] = jnp.zeros((rows, half - TILE), F32)

    return pl.pallas_call(
        body,
        in_specs=whole(nc + parts + 1 + n + m),
        out_specs=whole(len(shapes)),
        out_shape=[jax.ShapeDtypeStruct(x, F32) for x in shapes],
        scratch_shapes=[pltpu.VMEM((owners, floor_dev, time), F32)] * 2 + [pltpu.VMEM((rows, cols), F32)],
        compiler_params=params(),
        cost_estimate=cost(1),
        name="owner_shares",
    )(*motions, *loads, enter, *direct, *begin)


def share_shape(floor_dev, time):
    return -(-4 * floor_dev // 8) * 8, time // 2 + TILE


def spread(column):
    return jnp.broadcast_to(column, (column.shape[0], TILE))


def widened(tile):
    return jnp.concatenate([tile] * (BLK // TILE), axis=1)


def block_sums(force, tables, tri):
    return [dot_exact_right(force * table, tri) for table in tables]


def sum_at(refs, forces, b, mode_dev):
    total = None
    for ref, (x, row, start) in zip(refs, forces):
        if start <= b * BLK < start + x.shape[1]:
            part = ref[row : row + mode_dev, b * BLK - start : (b + 1) * BLK - start]
            total = part if total is None else total + part
    return total


def own_response(forces, shares, tables, turns, floor_dev, load_scale):
    mode_dev = forces[0][0].shape[0]
    n, m = len(shares), len(forces)
    half = shares[0][0].shape[1] - TILE
    time = 2 * half
    rows, width = share_shape(floor_dev, time)
    blocks = time // BLK

    def body(*refs):
        tab_ref, turn_ref, resp_ref, motion_ref, load_ref, share_ref = refs[m + n :]
        for i, (_, row, start, stop) in enumerate(shares):
            at = slice(start, stop)
            part = refs[m + i][row : row + rows, : stop - start]
            share_ref[:, at] = part if i == 0 else share_ref[:, at] + part
        share = share_ref[...]
        for h in (0, 1):
            at = slice(h * half, (h + 1) * half)
            motion_ref[:, at] = share[h * floor_dev : (h + 1) * floor_dev, :half]
            load_ref[:, at] = share[(2 + h) * floor_dev : (3 + h) * floor_dev, :half] * load_scale
        qr, qi = tab_ref[2], tab_ref[3]
        turn = [spread(turn_ref[:mode_dev, i : i + 1]) for i in (0, 1)]
        column = share[:, half:].T
        state = [spread(column[:mode_dev, i : i + 1]) for i in (0, 1)]
        tri = triangle()
        sums = [
            block_sums(sum_at(refs, forces, b, mode_dev), (tab_ref[0], tab_ref[1]), tri)
            for b in range(blocks)
        ]
        for b in range(blocks):
            cr, ci = (x + widened(y) for x, y in zip(sums[b], state))
            resp_ref[:, b * BLK : (b + 1) * BLK] = qr * cr - qi * ci
            state = turned(turn, [spread(x[:, BLK - 1 :]) + y for x, y in zip(sums[b], state)])

    return pl.pallas_call(
        body,
        in_specs=whole(m + n + 2),
        out_specs=tuple(whole(3)),
        out_shape=(
            jax.ShapeDtypeStruct((mode_dev, time), F32),
            jax.ShapeDtypeStruct((floor_dev, time), F32),
            jax.ShapeDtypeStruct((floor_dev, time), F32),
        ),
        scratch_shapes=[pltpu.VMEM((rows, width), F32)],
        compiler_params=params(),
        cost_estimate=cost(1),
        name="own_response",
    )(*(x for x, _, _ in forces), *(x[0] for x in shares), tables, turns)


def shifts(x, axis, n):
    return [lax.ppermute(x, axis, [(i, (i + d) % n) for i in range(n)]) for d in range(1, n)]


def along(parts, n):
    return [parts[0]] + [
        lax.ppermute(parts[d], "taps", [(i, (i + d) % n) for i in range(n)]) for d in range(1, n)
    ]


def on_device(
    pressures,
    tap_area,
    tap_panel,
    tap_floor,
    panel_shape,
    floor_shape,
    mode_order,
    mode_decay,
    mode_freq,
):
    nz = lax.axis_size("taps")
    nc = lax.axis_size("floors")
    nt = lax.axis_size("tm")
    owners = nz * nc
    modes = mode_order.shape[0]
    mode_dev = modes // owners
    time, taps = pressures.shape
    panels = panel_shape.shape[0]
    floors = floor_shape.shape[0]
    floor_dev = floors // owners
    load_scale = (floors / (taps * owners)) ** 0.5

    mine, kept = tap_sums(
        pressures,
        tap_panel[None],
        tap_floor[None],
        tap_area,
        (mode_order[None], mode_decay[None], mode_freq[None], panel_shape, floor_shape),
        panels,
        floors,
    )
    sums = [[mine] + shifts(mine, "floors", nc)]
    pt, floor_slots, tables, turns, own = mode_tables(*kept, nz, nc)
    forces, loads, spread = [], [], []
    for part in sums:
        force, load, spread = slot_forces(part, pt, tables, turns, nz, spread)
        forces.append(force)
        loads.append(load)
    pair, two, mirror = ([(i, i ^ d) for i in range(nz)] for d in (1, 2, 3))
    until = direct_until(time)
    laid = [(x, p * mode_dev, start) for x, (p, start, _) in zip(forces[0], send_plan(nz, time))]
    if nz == PAIRED:
        onward = [forces[0][1], lax.ppermute(forces[0][3], "taps", pair)]
        direct = [forces[0][2]]
        begin = [lax.ppermute(x, "taps", way) for x, way in zip(forces[0][4:], (two, mirror))]
    else:
        crossed, onward = [(x, 0, 0) for x in along(forces[0], nz)], []
        direct, begin = [], []
    motion = motion_from_rest(laid, tables, turns, floor_slots)
    ends = end_states(spread, turns, turns)
    enter = jnp.zeros_like(ends)
    for hop in range(nt - 1):
        passed = ends
        if hop:
            turn = (ends[2:3], ends[3:4])
            over = turn
            for _ in range(time // BLK - 1):
                over = turned(over, turn)
            enter = jnp.where(lax.axis_index("tm") > 0, enter, 0.0)
            passed = ends + jnp.concatenate(
                [*turned(over, (enter[0:1], enter[1:2])), jnp.zeros_like(ends[2:])]
            )
        enter = lax.ppermute(passed, "tm", [(i, (i + 1) % nt) for i in range(nt)])
    motion, *onward = floor_shares(motion, ends, enter, tables, floor_slots, onward)
    motions = [motion] + shifts(motion, "floors", nc)
    shares = owner_shares(motions, loads, enter, direct, begin, nz, floor_dev)
    if nz == PAIRED:
        ways = (two, pair, mirror, pair)
        away, near, far, rest = (lax.ppermute(x, "taps", way) for x, way in zip(shares[1:5], ways))
        onward = lax.ppermute(onward[0], "taps", two)
        half, (rows, cols) = time // 2, share_shape(floor_dev, time)
        crossed = [(forces[0][0], 0, 0), (near, 0, 0), (rest, 0, half)]
        crossed += [(shares[5], 0, 0), (onward, 0, until)]
        shares = [(x, 0, 0, cols) for x in (shares[0], away, far)]
        shares += [(near, mode_dev, 0, half), (near, mode_dev + rows, half, cols)]
    else:
        shares = [(x, 0, 0, x.shape[1]) for x in along(shares, nz)]
    return own_response(crossed, shares, own, turns, floor_dev, load_scale)


def solution(mesh):
    in_specs = (
        P(("dirs", "tm"), ("taps", "floors")),
        P(("taps", "floors")),
        P(("taps", "floors")),
        P(("taps", "floors")),
        P(),
        P(),
        P(),
        P(),
        P(),
    )
    out_specs = (
        P(("taps", "floors"), ("dirs", "tm")),
        P(("taps", "floors"), ("dirs", "tm")),
        P(("taps", "floors"), ("dirs", "tm")),
    )
    return jax.shard_map(
        on_device, mesh=mesh, in_specs=in_specs, out_specs=out_specs, check_vma=False
    )
```

```python
import jax
import jax.numpy as jnp
from jax import lax
from jax.experimental import pallas as pl
from jax.experimental.pallas import tpu as pltpu
from jax.sharding import PartitionSpec as P

BLK = 256
PAIRED = 4
TILE = 128
BF = jnp.bfloat16
F32 = jnp.float32
NN = (((1,), (0,)), ((), ()))
NT = (((1,), (1,)), ((), ()))
VMEM_LIMIT = 16 * 1024 * 1024


def dot(a, b, dims=NN):
    return lax.dot_general(a, b, dims, preferred_element_type=F32)


def split(x):
    hi = x.astype(BF)
    return hi, (x - hi.astype(F32)).astype(BF)


def dot_exact_left(a, x, dims=NN):
    hi, lo = split(x)
    return dot(a, hi, dims) + dot(a, lo, dims)


def dot_exact_right(x, b, dims=NN):
    hi, lo = split(x)
    return dot(hi, b, dims) + dot(lo, b, dims)


def params():
    return pltpu.CompilerParams(vmem_limit_bytes=VMEM_LIMIT)


def in_hbm(x):
    return pltpu.with_memory_space_constraint(x, pltpu.HBM)


def cost(us):
    return pl.CostEstimate(flops=int(us * 5e8), bytes_accessed=int(us * 2e6), transcendentals=0)


def whole(n):
    return [pl.BlockSpec(memory_space=pltpu.VMEM)] * n


def tap_sums(pressures, tap_panel, tap_floor, tap_area, others, panels, floors):
    time, taps = pressures.shape
    rows = panels + floors
    chunks = 2 if time % (2 * BLK) == 0 else 1
    span = time // chunks
    n = len(others)
    given = (tap_panel, tap_floor, tap_area)

    def body(press_hbm, *refs):
        from_refs, sums_ref, kept = refs[: n + 3], refs[n + 3], refs[n + 4 : 2 * n + 4]
        press, panel, floor, area, weights, sems = refs[2 * n + 4 :]
        small = [
            pltpu.make_async_copy(a, b, sems.at[chunks + i])
            for i, (a, b) in enumerate(zip(from_refs, (panel, floor, area, *kept)))
        ]
        large = []
        for i in range(chunks):
            at = pl.ds(i * span, span)
            large.append(pltpu.make_async_copy(press_hbm.at[at], press.at[at], sems.at[i]))
        for copy in [*small[:3], *large, *small[3:]]:
            copy.start()
        for copy in small[:3]:
            copy.wait()
        each = jnp.broadcast_to(area[...].astype(F32).reshape(1, taps), (16, taps))
        row = lax.broadcasted_iota(jnp.int32, (16, taps), 0)
        for ids, first, count in ((panel, 0, panels), (floor, panels, floors)):
            at = jnp.broadcast_to(ids[...], (16, taps)) - row
            for r in range(0, count, 16):
                weights[first + r : first + r + 16] = jnp.where(at == r, each, 0.0).astype(BF)
        for i in range(chunks):
            at = slice(i * span, (i + 1) * span)
            large[i].wait()
            sums_ref[:, at] = dot(weights[...], press[at], NT)
        for copy in small[3:]:
            copy.wait()

    out = pl.pallas_call(
        body,
        in_specs=[pl.BlockSpec(memory_space=pltpu.HBM)] * (n + 4),
        out_specs=tuple(whole(n + 1)),
        out_shape=(jax.ShapeDtypeStruct((rows, time), F32), *(jax.ShapeDtypeStruct(x.shape, x.dtype) for x in others)),
        scratch_shapes=[
            pltpu.VMEM((time, taps), BF),
            *(pltpu.VMEM(x.shape, x.dtype) for x in given),
            pltpu.VMEM((rows, taps), BF),
            pltpu.SemaphoreType.DMA((chunks + n + 3,)),
        ],
        compiler_params=params(),
        cost_estimate=cost(3),
        name="tap_sums",
    )(in_hbm(pressures), *(in_hbm(x) for x in given), *(in_hbm(x) for x in others))
    return out[0], out[1:]


def placed(z, nz):
    if nz != PAIRED:
        return [lax.rem(z + d, nz) for d in range(nz)]
    return [z, lax.rem(z + 2, nz), z + 1 - 2 * lax.rem(z, 2), nz - 1 - z]


def mode_tables(order, decay, freq, panel_shape, floor_shape, nz, nc):
    modes = order.shape[1]
    panels = panel_shape.shape[0]
    floors = floor_shape.shape[0]
    mode_dev = modes // (nz * nc)
    slots = mode_dev * nz
    bits = BLK.bit_length() - 1
    half = BLK // 2

    def body(*refs):
        order_ref, decay_ref, freq_ref, panel_ref, floor_ref = refs[:5]
        pt_ref, fs_ref, tab_ref, turn_ref, own_ref, column_ref = refs[5:]
        column_ref[...] = jnp.broadcast_to(order_ref[...].astype(F32), (TILE, modes)).T
        z, c = lax.axis_index("taps"), lax.axis_index("floors")
        picked = []
        for at in placed(z, nz):
            owner = at * nc + c
            picked.append(column_ref[pl.ds(pl.multiple_of(owner * mode_dev, mode_dev), mode_dev), :])
        column = jnp.concatenate(picked, axis=0)[:, :1]
        ids = lax.broadcasted_iota(jnp.int32, (slots, modes), 1).astype(F32)
        pick = jnp.where(column == ids, 1.0, 0.0).astype(BF)
        pt_ref[...] = dot(pick, panel_ref[...], NT).astype(BF)
        fs_ref[...] = dot(floor_ref[...], pick, NT)
        decays, angles = decay_ref[...], freq_ref[...]
        re, im = jnp.cos(angles), jnp.sin(angles)
        rows = [decays]
        square = decays * decays
        loss = 2.0 * jnp.exp(-decays) * decays * (1.0 + square * (1.0 / 6.0 + square * (1.0 / 120.0)))
        rows.append(jnp.sqrt(loss))
        for _ in range(bits + 1):
            rows += [re, im]
            re, im = re * re - im * im, 2.0 * re * im
        rows += [jnp.zeros_like(re)] * (-len(rows) % 16)
        count = len(rows)
        stack = jnp.concatenate(rows, axis=0)
        hi, mid = split(stack)
        low = (stack - hi.astype(F32) - mid.astype(F32)).astype(BF)
        parts = dot(pick, jnp.concatenate([hi, mid, low], axis=0), NT)
        cols = parts[:, :count] + parts[:, count : 2 * count] + parts[:, 2 * count : 3 * count]
        rate, gain = cols[:, 0:1], cols[:, 1:2]
        lane = lax.broadcasted_iota(jnp.int32, (slots, half), 1)
        cos = jnp.where((lane & 1) != 0, cols[:, 2:3], 1.0)
        sin = jnp.where((lane & 1) != 0, cols[:, 3:4], 0.0)
        for b in range(1, bits - 1):
            on = (lane & (1 << b)) != 0
            step = cols[:, 2 + 2 * b : 3 + 2 * b], cols[:, 3 + 2 * b : 4 + 2 * b]
            new_cos, new_sin = turned((cos, sin), step)
            cos, sin = jnp.where(on, new_cos, cos), jnp.where(on, new_sin, sin)
        at = 2 * bits
        far_cos, far_sin = turned((cos, sin), (cols[:, at : at + 1], cols[:, at + 1 : at + 2]))
        steps = rate * lane.astype(F32)
        shrink, grow = jnp.exp(-steps), gain * jnp.exp(steps)
        far_shrink = shrink * jnp.exp(-rate * float(half))
        far_grow = grow * jnp.exp(rate * float(half))
        near, far = slice(0, half), slice(half, BLK)
        tab_ref[0, :, near], tab_ref[0, :, far] = grow * cos, far_grow * far_cos
        tab_ref[1, :, near], tab_ref[1, :, far] = -grow * sin, -far_grow * far_sin
        tab_ref[2, :, near], tab_ref[2, :, far] = shrink * cos, far_shrink * far_cos
        tab_ref[3, :, near], tab_ref[3, :, far] = shrink * sin, far_shrink * far_sin
        fade = jnp.exp(-rate * float(BLK))
        turn_ref[...] = fade * cols[:, at + 2 : at + 4]
        own_ref[...] = tab_ref[:, :mode_dev]

    return pl.pallas_call(
        body,
        in_specs=whole(5),
        out_specs=tuple(whole(5)),
        out_shape=(
            jax.ShapeDtypeStruct((slots, panels), BF),
            jax.ShapeDtypeStruct((floors, slots), F32),
            jax.ShapeDtypeStruct((4, slots, BLK), F32),
            jax.ShapeDtypeStruct((slots, 2), F32),
            jax.ShapeDtypeStruct((4, mode_dev, BLK), F32),
        ),
        scratch_shapes=[pltpu.VMEM((modes, TILE), F32)],
        compiler_params=params(),
        cost_estimate=cost(2),
        name="mode_tables",
    )(order, decay, freq, panel_shape, floor_shape)


def direct_until(time):
    return time // 4 // BLK * BLK


def send_plan(nz, time):
    until = direct_until(time)
    if nz != PAIRED or not until:
        return [(p, 0, time) for p in range(nz)]
    late = [(p, until, time) for p in (1, 2, 3)]
    return [(0, 0, time), *late, *((p, 0, until) for p in (1, 3, 2))]


def slot_forces(sums, pt, tables, turns, nz, before):
    slots, panels = pt.shape
    rows, time = sums[0].shape
    nc = len(sums)
    mode_dev = slots // nz
    plan = send_plan(nz, time)
    n = len(before)

    def body(*refs):
        sum_refs, (pt_ref, tab_ref, turn_ref) = refs[:nc], refs[nc : nc + 3]
        before_refs, out_refs = refs[nc + 3 : nc + 3 + n], refs[nc + 3 + n : -3]
        load_ref, state_refs = refs[-3], refs[-2:]
        load = sum_refs[0][panels:]
        for ref in sum_refs[1:]:
            load = load + ref[panels:]
        load_ref[...] = load
        left = pt_ref[...]
        turn = turn_ref[:, 0:1], turn_ref[:, 1:2]
        state = [ref[...] for ref in before_refs]
        for b in range(time // BLK):
            cols = slice(b * BLK, (b + 1) * BLK)
            total = sum_refs[0][:panels, cols]
            for ref in sum_refs[1:]:
                total = total + ref[:panels, cols]
            forces = dot_exact_left(left, total)
            for ref, (p, start, stop) in zip(out_refs, plan):
                if start <= b * BLK < stop:
                    at = slice(b * BLK - start, (b + 1) * BLK - start)
                    ref[:, at] = forces[p * mode_dev : (p + 1) * mode_dev]
            new = []
            for part in (forces * tab_ref[0], forces * tab_ref[1]):
                near = part[:, :TILE]
                for k in range(TILE, BLK, TILE):
                    near = near + part[:, k : k + TILE]
                new.append(near)
            if state:
                new = [a + b for a, b in zip(new, state)]
            state = turned(turn, new)
        state_refs[0][...], state_refs[1][...] = state

    out = pl.pallas_call(
        body,
        in_specs=whole(nc + 3 + n),
        out_specs=whole(len(plan) + 3),
        out_shape=[jax.ShapeDtypeStruct((mode_dev, stop - start), F32) for _, start, stop in plan]
        + [jax.ShapeDtypeStruct((rows - panels, time), F32)]
        + [jax.ShapeDtypeStruct((slots, TILE), F32)] * 2,
        compiler_params=params(),
        cost_estimate=cost(1),
        name="slot_forces",
    )(*sums, pt, tables, turns, *before)
    return out[:-3], out[-3], out[-2:]


def end_states(spread, turns, after):
    slots = turns.shape[0]

    def body(re_ref, im_ref, turn_ref, after_ref, out_ref):
        pad = jnp.zeros((TILE, TILE - 4), F32)
        for k in range(0, slots, TILE):
            at = slice(k, k + TILE)
            state = [jnp.sum(ref[at], axis=1, keepdims=True) for ref in (re_ref, im_ref)]
            four = [*state, turn_ref[at, 0:1], turn_ref[at, 1:2]]
            out_ref[:, at] = jnp.concatenate([*four, pad], axis=1).T[:8]

    return pl.pallas_call(
        body,
        in_specs=whole(4),
        out_specs=whole(1)[0],
        out_shape=jax.ShapeDtypeStruct((8, slots), F32),
        compiler_params=params(),
        cost_estimate=cost(1),
        name="end_states",
    )(*spread, turns, after)


def triangle():
    row = lax.broadcasted_iota(jnp.int32, (BLK, BLK), 0)
    col = lax.broadcasted_iota(jnp.int32, (BLK, BLK), 1)
    return jnp.where(row <= col, 1.0, 0.0).astype(BF)


def turned(a, b):
    return (a[0] * b[0] - a[1] * b[1], a[0] * b[1] + a[1] * b[0])


def motion_from_rest(forces, tables, turns, floor_slots):
    slots = turns.shape[0]
    floors = floor_slots.shape[0]
    time = max(start + x.shape[1] for x, _, start in forces)
    blocks = time // BLK
    n = len(forces)
    places = [(row, start, x.shape) for x, row, start in forces]

    def body(*refs):
        tab_ref, turn_ref, fs_ref, motion_ref = refs[n:]
        tri = triangle()
        here = fs_ref[...].astype(BF)
        turn = [spread(turn_ref[:, i : i + 1]) for i in (0, 1)]
        state = None
        for b in range(blocks):
            found = [
                (row, ref[:, b * BLK - start : (b + 1) * BLK - start])
                for ref, (row, start, shape) in zip(refs, places)
                if start <= b * BLK < start + shape[1]
            ]
            force = jnp.concatenate([x for _, x in sorted(found, key=lambda f: f[0])], axis=0)
            cr, ci = block_sums(force, (tab_ref[0], tab_ref[1]), tri)
            last = [spread(x[:, BLK - 1 :]) for x in (cr, ci)]
            if state is not None:
                cr, ci = cr + widened(state[0]), ci + widened(state[1])
                last = [x + y for x, y in zip(last, state)]
            part = dot_exact_left(here, tab_ref[2] * cr - tab_ref[3] * ci)
            motion_ref[:, b * BLK : (b + 1) * BLK] = part
            state = turned(turn, last)

    return pl.pallas_call(
        body,
        in_specs=whole(n + 3),
        out_specs=whole(1)[0],
        out_shape=jax.ShapeDtypeStruct((floors, time), F32),
        compiler_params=params(),
        cost_estimate=cost(2),
        name="motion_from_rest",
    )(*(x for x, _, _ in forces), tables, turns, floor_slots)


def floor_shares(motion, ends, enter, tables, floor_slots, onward):
    floors, time = motion.shape
    blocks = time // BLK
    n = len(onward)

    def body(motion_ref, ends_ref, enter_ref, tab_ref, fs_ref, *refs):
        out_ref = refs[n]
        if n:
            refs[n + 1][...] = refs[0][...] + refs[1][...]
        shape = fs_ref[...]
        turn = (ends_ref[2:3, :], ends_ref[3:4, :])
        later = lax.axis_index("tm") > 0
        state = tuple(jnp.where(later, enter_ref[i : i + 1, :], 0.0) for i in (0, 1))
        left_re, left_im = [], []
        for b in range(blocks):
            left_re.append(shape * state[0])
            left_im.append(shape * state[1])
            state = turned(turn, state)
        qr_hi, qr_lo = split(tab_ref[2])
        qi_hi, qi_lo = split(tab_ref[3])
        re_hi, re_lo = split(jnp.concatenate(left_re, axis=0))
        im_hi, im_lo = split(jnp.concatenate(left_im, axis=0))
        free = dot(re_hi, qr_hi) + dot(re_hi, qr_lo) + dot(re_lo, qr_hi)
        free = free - (dot(im_hi, qi_hi) + dot(im_hi, qi_lo) + dot(im_lo, qi_hi))
        for b in range(blocks):
            cols = slice(b * BLK, (b + 1) * BLK)
            out_ref[:, cols] = motion_ref[:, cols] + free[b * floors : (b + 1) * floors]

    return pl.pallas_call(
        body,
        in_specs=whole(5 + n),
        out_specs=whole(1 + len(onward[:1])),
        out_shape=[
            jax.ShapeDtypeStruct(x, F32) for x in [(floors, time)] + [x.shape for x in onward[:1]]
        ],
        compiler_params=params(),
        cost_estimate=cost(1),
        name="floor_shares",
    )(motion, ends, enter, tables, floor_slots, *onward)


def owner_shares(motions, loads, enter, direct, begin, nz, floor_dev):
    nc, parts = len(motions), len(loads)
    floors, time = motions[0].shape
    rows, cols = share_shape(floor_dev, time)
    owners = nz * nc
    mode_dev = enter.shape[1] // nz
    span = time // parts
    n, m = len(direct), len(begin)
    half = time // 2
    shapes = [(rows, cols)] * nz
    if n:
        width = direct[0].shape[1]
        pieces = [(start, min(start + width, cols)) for start in range(0, cols, width)]
        shapes[2] = (mode_dev + len(pieces) * rows, width)
        shapes += [begin[0].shape]

    def body(*refs):
        motion_refs, load_refs, enter_ref = refs[:nc], refs[nc : nc + parts], refs[nc + parts]
        more, out_refs = refs[nc + parts + 1 : nc + parts + 1 + n + m], refs[nc + parts + 1 + n + m : -3]
        motion_all, load_all, share_ref = refs[-3:]
        if n:
            out_refs[2][...] = jnp.zeros(shapes[2], F32)
            out_refs[2][:mode_dev] = more[0][...]
            out_refs[nz][...] = more[1][...] + more[2][...]
        z, c = lax.axis_index("taps"), lax.axis_index("floors")
        later = lax.axis_index("tm") > 0
        motion = motion_refs[0][...]
        for ref in motion_refs[1:]:
            motion = motion + ref[...]
        for o in range(owners):
            at = slice(o * floor_dev, (o + 1) * floor_dev)
            motion_all[o] = motion[at]
            for k in range(parts):
                load_all[o, :, k * span : (k + 1) * span] = load_refs[k][at]
        for p, place in enumerate(placed(z, nz)):
            owner = place * nc + c
            out = share_ref if n and p == 2 else out_refs[p]
            out[...] = jnp.zeros((rows, cols), F32)
            for k, ref in enumerate((motion_all, load_all)):
                for h in (0, 1):
                    at = slice((2 * k + h) * floor_dev, (2 * k + h + 1) * floor_dev)
                    out[at, :half] = ref[owner, :, h * half : (h + 1) * half]
            state = enter_ref[0:2, p * mode_dev : (p + 1) * mode_dev]
            out[:2, half : half + mode_dev] = jnp.where(later, state, 0.0)
        if n:
            for k, (start, stop) in enumerate(pieces):
                at = mode_dev + k * rows
                out_refs[2][at : at + rows, : stop - start] = share_ref[:, start:stop]

    return pl.pallas_call(
        body,
        in_specs=whole(nc + parts + 1 + n + m),
        out_specs=whole(len(shapes)),
        out_shape=[jax.ShapeDtypeStruct(x, F32) for x in shapes],
        scratch_shapes=[pltpu.VMEM((owners, floor_dev, time), F32)] * 2 + [pltpu.VMEM((rows, cols), F32)],
        compiler_params=params(),
        cost_estimate=cost(1),
        name="owner_shares",
    )(*motions, *loads, enter, *direct, *begin)


def share_shape(floor_dev, time):
    return -(-4 * floor_dev // 8) * 8, time // 2 + TILE


def spread(column):
    return jnp.broadcast_to(column, (column.shape[0], TILE))


def widened(tile):
    return jnp.concatenate([tile] * (BLK // TILE), axis=1)


def block_sums(force, tables, tri):
    return [dot_exact_right(force * table, tri) for table in tables]


def sum_at(refs, forces, b, mode_dev):
    total = None
    for ref, (x, row, start) in zip(refs, forces):
        if start <= b * BLK < start + x.shape[1]:
            part = ref[row : row + mode_dev, b * BLK - start : (b + 1) * BLK - start]
            total = part if total is None else total + part
    return total


def own_response(forces, shares, tables, turns, floor_dev, load_scale):
    mode_dev = forces[0][0].shape[0]
    n, m = len(shares), len(forces)
    half = shares[0][0].shape[1] - TILE
    time = 2 * half
    rows, width = share_shape(floor_dev, time)
    blocks = time // BLK

    def body(*refs):
        tab_ref, turn_ref, resp_ref, motion_ref, load_ref, share_ref = refs[m + n :]
        for i, (_, row, start, stop) in enumerate(shares):
            at = slice(start, stop)
            part = refs[m + i][row : row + rows, : stop - start]
            share_ref[:, at] = part if i == 0 else share_ref[:, at] + part
        share = share_ref[...]
        for h in (0, 1):
            at = slice(h * half, (h + 1) * half)
            motion_ref[:, at] = share[h * floor_dev : (h + 1) * floor_dev, :half]
            load_ref[:, at] = share[(2 + h) * floor_dev : (3 + h) * floor_dev, :half] * load_scale
        qr, qi = tab_ref[2], tab_ref[3]
        turn = [spread(turn_ref[:mode_dev, i : i + 1]) for i in (0, 1)]
        column = share[:, half:].T
        state = [spread(column[:mode_dev, i : i + 1]) for i in (0, 1)]
        tri = triangle()
        sums = [
            block_sums(sum_at(refs, forces, b, mode_dev), (tab_ref[0], tab_ref[1]), tri)
            for b in range(blocks)
        ]
        for b in range(blocks):
            cr, ci = (x + widened(y) for x, y in zip(sums[b], state))
            resp_ref[:, b * BLK : (b + 1) * BLK] = qr * cr - qi * ci
            state = turned(turn, [spread(x[:, BLK - 1 :]) + y for x, y in zip(sums[b], state)])

    return pl.pallas_call(
        body,
        in_specs=whole(m + n + 2),
        out_specs=tuple(whole(3)),
        out_shape=(
            jax.ShapeDtypeStruct((mode_dev, time), F32),
            jax.ShapeDtypeStruct((floor_dev, time), F32),
            jax.ShapeDtypeStruct((floor_dev, time), F32),
        ),
        scratch_shapes=[pltpu.VMEM((rows, width), F32)],
        compiler_params=params(),
        cost_estimate=cost(1),
        name="own_response",
    )(*(x for x, _, _ in forces), *(x[0] for x in shares), tables, turns)


def shifts(x, axis, n):
    return [lax.ppermute(x, axis, [(i, (i + d) % n) for i in range(n)]) for d in range(1, n)]


def along(parts, n):
    return [parts[0]] + [
        lax.ppermute(parts[d], "taps", [(i, (i + d) % n) for i in range(n)]) for d in range(1, n)
    ]


def on_device(
    pressures,
    tap_area,
    tap_panel,
    tap_floor,
    panel_shape,
    floor_shape,
    mode_order,
    mode_decay,
    mode_freq,
):
    nz = lax.axis_size("taps")
    nc = lax.axis_size("floors")
    nt = lax.axis_size("tm")
    owners = nz * nc
    modes = mode_order.shape[0]
    mode_dev = modes // owners
    time, taps = pressures.shape
    panels = panel_shape.shape[0]
    floors = floor_shape.shape[0]
    floor_dev = floors // owners
    load_scale = (floors / (taps * owners)) ** 0.5

    mine, kept = tap_sums(
        pressures,
        tap_panel[None],
        tap_floor[None],
        tap_area,
        (mode_order[None], mode_decay[None], mode_freq[None], panel_shape, floor_shape),
        panels,
        floors,
    )
    sums = [[mine] + shifts(mine, "floors", nc)]
    pt, floor_slots, tables, turns, own = mode_tables(*kept, nz, nc)
    forces, loads, spread = [], [], []
    for part in sums:
        force, load, spread = slot_forces(part, pt, tables, turns, nz, spread)
        forces.append(force)
        loads.append(load)
    pair, two, mirror = ([(i, i ^ d) for i in range(nz)] for d in (1, 2, 3))
    until = direct_until(time)
    laid = [(x, p * mode_dev, start) for x, (p, start, _) in zip(forces[0], send_plan(nz, time))]
    if nz == PAIRED:
        onward = [forces[0][1], lax.ppermute(forces[0][3], "taps", pair)]
        direct, tail = [forces[0][6]], lax.ppermute(forces[0][2], "taps", pair)
        begin = [lax.ppermute(x, "taps", way) for x, way in zip(forces[0][4:6], (two, mirror))]
    else:
        crossed, onward = [(x, 0, 0) for x in along(forces[0], nz)], []
        direct, begin = [], []
    motion = motion_from_rest(laid, tables, turns, floor_slots)
    ends = end_states(spread, turns, turns)
    enter = jnp.zeros_like(ends)
    for hop in range(nt - 1):
        passed = ends
        if hop:
            turn = (ends[2:3], ends[3:4])
            over = turn
            for _ in range(time // BLK - 1):
                over = turned(over, turn)
            enter = jnp.where(lax.axis_index("tm") > 0, enter, 0.0)
            passed = ends + jnp.concatenate(
                [*turned(over, (enter[0:1], enter[1:2])), jnp.zeros_like(ends[2:])]
            )
        enter = lax.ppermute(passed, "tm", [(i, (i + 1) % nt) for i in range(nt)])
    motion, *onward = floor_shares(motion, ends, enter, tables, floor_slots, onward)
    motions = [motion] + shifts(motion, "floors", nc)
    shares = owner_shares(motions, loads, enter, direct, begin, nz, floor_dev)
    if nz == PAIRED:
        ways = (two, pair, mirror)
        away, near, far = (lax.ppermute(x, "taps", way) for x, way in zip(shares[1:4], ways))
        onward = lax.ppermute(onward[0], "taps", two)
        rows, cols = share_shape(floor_dev, time)
        crossed = [(forces[0][0], 0, 0), (near, 0, 0), (tail, 0, until)]
        crossed += [(shares[4], 0, 0), (onward, 0, until)]
        shares = [(x, 0, 0, cols) for x in (shares[0], away, far)]
        for k, start in enumerate(range(0, cols, until)):
            shares.append((near, mode_dev + k * rows, start, min(start + until, cols)))
    else:
        shares = [(x, 0, 0, x.shape[1]) for x in along(shares, nz)]
    return own_response(crossed, shares, own, turns, floor_dev, load_scale)


def solution(mesh):
    in_specs = (
        P(("dirs", "tm"), ("taps", "floors")),
        P(("taps", "floors")),
        P(("taps", "floors")),
        P(("taps", "floors")),
        P(),
        P(),
        P(),
        P(),
        P(),
    )
    out_specs = (
        P(("taps", "floors"), ("dirs", "tm")),
        P(("taps", "floors"), ("dirs", "tm")),
        P(("taps", "floors"), ("dirs", "tm")),
    )
    return jax.shard_map(
        on_device, mesh=mesh, in_specs=in_specs, out_specs=out_specs, check_vma=False
    )
```

```python
import jax
import jax.numpy as jnp
from jax import lax
from jax.experimental import pallas as pl
from jax.experimental.pallas import tpu as pltpu
from jax.sharding import PartitionSpec as P

BLK = 256
PAIRED = 4
TILE = 128
BF = jnp.bfloat16
F32 = jnp.float32
NN = (((1,), (0,)), ((), ()))
NT = (((1,), (1,)), ((), ()))
VMEM_LIMIT = 16 * 1024 * 1024


def dot(a, b, dims=NN):
    return lax.dot_general(a, b, dims, preferred_element_type=F32)


def split(x):
    hi = x.astype(BF)
    return hi, (x - hi.astype(F32)).astype(BF)


def dot_exact_left(a, x, dims=NN):
    hi, lo = split(x)
    return dot(a, hi, dims) + dot(a, lo, dims)


def dot_exact_right(x, b, dims=NN):
    hi, lo = split(x)
    return dot(hi, b, dims) + dot(lo, b, dims)


def params():
    return pltpu.CompilerParams(vmem_limit_bytes=VMEM_LIMIT)


def in_hbm(x):
    return pltpu.with_memory_space_constraint(x, pltpu.HBM)


def cost(us):
    return pl.CostEstimate(flops=int(us * 5e8), bytes_accessed=int(us * 2e6), transcendentals=0)


def whole(n):
    return [pl.BlockSpec(memory_space=pltpu.VMEM)] * n


def tap_sums(pressures, tap_panel, tap_floor, tap_area, others, panels, floors):
    time, taps = pressures.shape
    rows = panels + floors
    chunks = 2 if time % (2 * BLK) == 0 else 1
    span = time // chunks
    n = len(others)
    given = (tap_panel, tap_floor, tap_area)

    def body(press_hbm, *refs):
        from_refs, sums_ref, kept = refs[: n + 3], refs[n + 3], refs[n + 4 : 2 * n + 4]
        press, panel, floor, area, weights, sems = refs[2 * n + 4 :]
        small = [
            pltpu.make_async_copy(a, b, sems.at[chunks + i])
            for i, (a, b) in enumerate(zip(from_refs, (panel, floor, area, *kept)))
        ]
        large = []
        for i in range(chunks):
            at = pl.ds(i * span, span)
            large.append(pltpu.make_async_copy(press_hbm.at[at], press.at[at], sems.at[i]))
        for copy in [*small[:3], *large, *small[3:]]:
            copy.start()
        for copy in small[:3]:
            copy.wait()
        each = jnp.broadcast_to(area[...].astype(F32).reshape(1, taps), (16, taps))
        row = lax.broadcasted_iota(jnp.int32, (16, taps), 0)
        for ids, first, count in ((panel, 0, panels), (floor, panels, floors)):
            at = jnp.broadcast_to(ids[...], (16, taps)) - row
            for r in range(0, count, 16):
                weights[first + r : first + r + 16] = jnp.where(at == r, each, 0.0).astype(BF)
        for i in range(chunks):
            at = slice(i * span, (i + 1) * span)
            large[i].wait()
            sums_ref[:, at] = dot(weights[...], press[at], NT)
        for copy in small[3:]:
            copy.wait()

    out = pl.pallas_call(
        body,
        in_specs=[pl.BlockSpec(memory_space=pltpu.HBM)] * (n + 4),
        out_specs=tuple(whole(n + 1)),
        out_shape=(jax.ShapeDtypeStruct((rows, time), F32), *(jax.ShapeDtypeStruct(x.shape, x.dtype) for x in others)),
        scratch_shapes=[
            pltpu.VMEM((time, taps), BF),
            *(pltpu.VMEM(x.shape, x.dtype) for x in given),
            pltpu.VMEM((rows, taps), BF),
            pltpu.SemaphoreType.DMA((chunks + n + 3,)),
        ],
        compiler_params=params(),
        cost_estimate=cost(3),
        name="tap_sums",
    )(in_hbm(pressures), *(in_hbm(x) for x in given), *(in_hbm(x) for x in others))
    return out[0], out[1:]


def placed(z, nz):
    if nz != PAIRED:
        return [lax.rem(z + d, nz) for d in range(nz)]
    return [z, lax.rem(z + 2, nz), z + 1 - 2 * lax.rem(z, 2), nz - 1 - z]


def mode_tables(order, decay, freq, panel_shape, floor_shape, nz, nc):
    modes = order.shape[1]
    panels = panel_shape.shape[0]
    floors = floor_shape.shape[0]
    mode_dev = modes // (nz * nc)
    slots = mode_dev * nz
    bits = BLK.bit_length() - 1
    half = BLK // 2

    def body(*refs):
        order_ref, decay_ref, freq_ref, panel_ref, floor_ref = refs[:5]
        pt_ref, fs_ref, tab_ref, turn_ref, own_ref, column_ref = refs[5:]
        column_ref[...] = jnp.broadcast_to(order_ref[...].astype(F32), (TILE, modes)).T
        z, c = lax.axis_index("taps"), lax.axis_index("floors")
        picked = []
        for at in placed(z, nz):
            owner = at * nc + c
            picked.append(column_ref[pl.ds(pl.multiple_of(owner * mode_dev, mode_dev), mode_dev), :])
        column = jnp.concatenate(picked, axis=0)[:, :1]
        ids = lax.broadcasted_iota(jnp.int32, (slots, modes), 1).astype(F32)
        pick = jnp.where(column == ids, 1.0, 0.0).astype(BF)
        pt_ref[...] = dot(pick, panel_ref[...], NT).astype(BF)
        fs_ref[...] = dot(floor_ref[...], pick, NT)
        decays, angles = decay_ref[...], freq_ref[...]
        re, im = jnp.cos(angles), jnp.sin(angles)
        rows = [decays]
        square = decays * decays
        loss = 2.0 * jnp.exp(-decays) * decays * (1.0 + square * (1.0 / 6.0 + square * (1.0 / 120.0)))
        rows.append(jnp.sqrt(loss))
        for _ in range(bits + 1):
            rows += [re, im]
            re, im = re * re - im * im, 2.0 * re * im
        rows += [jnp.zeros_like(re)] * (-len(rows) % 16)
        count = len(rows)
        stack = jnp.concatenate(rows, axis=0)
        hi, mid = split(stack)
        low = (stack - hi.astype(F32) - mid.astype(F32)).astype(BF)
        parts = dot(pick, jnp.concatenate([hi, mid, low], axis=0), NT)
        cols = parts[:, :count] + parts[:, count : 2 * count] + parts[:, 2 * count : 3 * count]
        rate, gain = cols[:, 0:1], cols[:, 1:2]
        lane = lax.broadcasted_iota(jnp.int32, (slots, half), 1)
        cos = jnp.where((lane & 1) != 0, cols[:, 2:3], 1.0)
        sin = jnp.where((lane & 1) != 0, cols[:, 3:4], 0.0)
        for b in range(1, bits - 1):
            on = (lane & (1 << b)) != 0
            step = cols[:, 2 + 2 * b : 3 + 2 * b], cols[:, 3 + 2 * b : 4 + 2 * b]
            new_cos, new_sin = turned((cos, sin), step)
            cos, sin = jnp.where(on, new_cos, cos), jnp.where(on, new_sin, sin)
        at = 2 * bits
        far_cos, far_sin = turned((cos, sin), (cols[:, at : at + 1], cols[:, at + 1 : at + 2]))
        steps = rate * lane.astype(F32)
        shrink, grow = jnp.exp(-steps), gain * jnp.exp(steps)
        far_shrink = shrink * jnp.exp(-rate * float(half))
        far_grow = grow * jnp.exp(rate * float(half))
        near, far = slice(0, half), slice(half, BLK)
        tab_ref[0, :, near], tab_ref[0, :, far] = grow * cos, far_grow * far_cos
        tab_ref[1, :, near], tab_ref[1, :, far] = -grow * sin, -far_grow * far_sin
        tab_ref[2, :, near], tab_ref[2, :, far] = shrink * cos, far_shrink * far_cos
        tab_ref[3, :, near], tab_ref[3, :, far] = shrink * sin, far_shrink * far_sin
        fade = jnp.exp(-rate * float(BLK))
        turn_ref[...] = fade * cols[:, at + 2 : at + 4]
        own_ref[...] = tab_ref[:, :mode_dev]

    return pl.pallas_call(
        body,
        in_specs=whole(5),
        out_specs=tuple(whole(5)),
        out_shape=(
            jax.ShapeDtypeStruct((slots, panels), BF),
            jax.ShapeDtypeStruct((floors, slots), F32),
            jax.ShapeDtypeStruct((4, slots, BLK), F32),
            jax.ShapeDtypeStruct((slots, 2), F32),
            jax.ShapeDtypeStruct((4, mode_dev, BLK), F32),
        ),
        scratch_shapes=[pltpu.VMEM((modes, TILE), F32)],
        compiler_params=params(),
        cost_estimate=cost(2),
        name="mode_tables",
    )(order, decay, freq, panel_shape, floor_shape)


def direct_until(time):
    return time // 4 // BLK * BLK


def send_plan(nz, time):
    until = direct_until(time)
    if nz != PAIRED or not until:
        return [(p, 0, time) for p in range(nz)]
    late = [(p, until, time) for p in (1, 2, 3)]
    return [(0, 0, time), *late, *((p, 0, until) for p in (1, 3, 2))]


def slot_forces(sums, pt, tables, turns, nz, before):
    slots, panels = pt.shape
    rows, time = sums[0].shape
    nc = len(sums)
    mode_dev = slots // nz
    plan = send_plan(nz, time)
    n = len(before)

    def body(*refs):
        sum_refs, (pt_ref, tab_ref, turn_ref) = refs[:nc], refs[nc : nc + 3]
        before_refs, out_refs = refs[nc + 3 : nc + 3 + n], refs[nc + 3 + n : -3]
        load_ref, state_refs = refs[-3], refs[-2:]
        load = sum_refs[0][panels:]
        for ref in sum_refs[1:]:
            load = load + ref[panels:]
        load_ref[...] = load
        left = pt_ref[...]
        turn = turn_ref[:, 0:1], turn_ref[:, 1:2]
        state = [ref[...] for ref in before_refs]
        for b in range(time // BLK):
            cols = slice(b * BLK, (b + 1) * BLK)
            total = sum_refs[0][:panels, cols]
            for ref in sum_refs[1:]:
                total = total + ref[:panels, cols]
            forces = dot_exact_left(left, total)
            for ref, (p, start, stop) in zip(out_refs, plan):
                if start <= b * BLK < stop:
                    at = slice(b * BLK - start, (b + 1) * BLK - start)
                    ref[:, at] = forces[p * mode_dev : (p + 1) * mode_dev]
            new = []
            for part in (forces * tab_ref[0], forces * tab_ref[1]):
                near = part[:, :TILE]
                for k in range(TILE, BLK, TILE):
                    near = near + part[:, k : k + TILE]
                new.append(near)
            if state:
                new = [a + b for a, b in zip(new, state)]
            state = turned(turn, new)
        state_refs[0][...], state_refs[1][...] = state

    out = pl.pallas_call(
        body,
        in_specs=whole(nc + 3 + n),
        out_specs=whole(len(plan) + 3),
        out_shape=[jax.ShapeDtypeStruct((mode_dev, stop - start), F32) for _, start, stop in plan]
        + [jax.ShapeDtypeStruct((rows - panels, time), F32)]
        + [jax.ShapeDtypeStruct((slots, TILE), F32)] * 2,
        compiler_params=params(),
        cost_estimate=cost(1),
        name="slot_forces",
    )(*sums, pt, tables, turns, *before)
    return out[:-3], out[-3], out[-2:]


def end_states(spread, turns, after):
    slots = turns.shape[0]

    def body(re_ref, im_ref, turn_ref, after_ref, out_ref):
        pad = jnp.zeros((TILE, TILE - 4), F32)
        for k in range(0, slots, TILE):
            at = slice(k, k + TILE)
            state = [jnp.sum(ref[at], axis=1, keepdims=True) for ref in (re_ref, im_ref)]
            four = [*state, turn_ref[at, 0:1], turn_ref[at, 1:2]]
            out_ref[:, at] = jnp.concatenate([*four, pad], axis=1).T[:8]

    return pl.pallas_call(
        body,
        in_specs=whole(4),
        out_specs=whole(1)[0],
        out_shape=jax.ShapeDtypeStruct((8, slots), F32),
        compiler_params=params(),
        cost_estimate=cost(1),
        name="end_states",
    )(*spread, turns, after)


def triangle():
    row = lax.broadcasted_iota(jnp.int32, (BLK, BLK), 0)
    col = lax.broadcasted_iota(jnp.int32, (BLK, BLK), 1)
    return jnp.where(row <= col, 1.0, 0.0).astype(BF)


def turned(a, b):
    return (a[0] * b[0] - a[1] * b[1], a[0] * b[1] + a[1] * b[0])


def motion_from_rest(forces, tables, turns, floor_slots):
    slots = turns.shape[0]
    floors = floor_slots.shape[0]
    time = max(start + x.shape[1] for x, _, start in forces)
    blocks = time // BLK
    n = len(forces)
    places = [(row, start, x.shape) for x, row, start in forces]

    def body(*refs):
        tab_ref, turn_ref, fs_ref, motion_ref = refs[n:]
        tri = triangle()
        here = fs_ref[...].astype(BF)
        turn = [spread(turn_ref[:, i : i + 1]) for i in (0, 1)]
        state = None
        for b in range(blocks):
            found = [
                (row, ref[:, b * BLK - start : (b + 1) * BLK - start])
                for ref, (row, start, shape) in zip(refs, places)
                if start <= b * BLK < start + shape[1]
            ]
            force = jnp.concatenate([x for _, x in sorted(found, key=lambda f: f[0])], axis=0)
            cr, ci = block_sums(force, (tab_ref[0], tab_ref[1]), tri)
            last = [spread(x[:, BLK - 1 :]) for x in (cr, ci)]
            if state is not None:
                cr, ci = cr + widened(state[0]), ci + widened(state[1])
                last = [x + y for x, y in zip(last, state)]
            part = dot_exact_left(here, tab_ref[2] * cr - tab_ref[3] * ci)
            motion_ref[:, b * BLK : (b + 1) * BLK] = part
            state = turned(turn, last)

    return pl.pallas_call(
        body,
        in_specs=whole(n + 3),
        out_specs=whole(1)[0],
        out_shape=jax.ShapeDtypeStruct((floors, time), F32),
        compiler_params=params(),
        cost_estimate=cost(2),
        name="motion_from_rest",
    )(*(x for x, _, _ in forces), tables, turns, floor_slots)


def floor_shares(motion, ends, enter, tables, floor_slots, onward):
    floors, time = motion.shape
    blocks = time // BLK
    n = len(onward)

    def body(motion_ref, ends_ref, enter_ref, tab_ref, fs_ref, *refs):
        out_ref = refs[n]
        if n:
            refs[n + 1][...] = refs[0][...] + refs[1][...]
        shape = fs_ref[...]
        turn = (ends_ref[2:3, :], ends_ref[3:4, :])
        later = lax.axis_index("tm") > 0
        state = tuple(jnp.where(later, enter_ref[i : i + 1, :], 0.0) for i in (0, 1))
        left_re, left_im = [], []
        for b in range(blocks):
            left_re.append(shape * state[0])
            left_im.append(shape * state[1])
            state = turned(turn, state)
        qr_hi, qr_lo = split(tab_ref[2])
        qi_hi, qi_lo = split(tab_ref[3])
        re_hi, re_lo = split(jnp.concatenate(left_re, axis=0))
        im_hi, im_lo = split(jnp.concatenate(left_im, axis=0))
        free = dot(re_hi, qr_hi) + dot(re_hi, qr_lo) + dot(re_lo, qr_hi)
        free = free - (dot(im_hi, qi_hi) + dot(im_hi, qi_lo) + dot(im_lo, qi_hi))
        for b in range(blocks):
            cols = slice(b * BLK, (b + 1) * BLK)
            out_ref[:, cols] = motion_ref[:, cols] + free[b * floors : (b + 1) * floors]

    return pl.pallas_call(
        body,
        in_specs=whole(5 + n),
        out_specs=whole(1 + len(onward[:1])),
        out_shape=[
            jax.ShapeDtypeStruct(x, F32) for x in [(floors, time)] + [x.shape for x in onward[:1]]
        ],
        compiler_params=params(),
        cost_estimate=cost(1),
        name="floor_shares",
    )(motion, ends, enter, tables, floor_slots, *onward)


def owner_shares(motions, loads, enter, direct, begin, nz, floor_dev):
    nc, parts = len(motions), len(loads)
    floors, time = motions[0].shape
    rows, cols = share_shape(floor_dev, time)
    owners = nz * nc
    mode_dev = enter.shape[1] // nz
    span = time // parts
    n, m = len(direct), len(begin)
    half = time // 2
    shapes = [(rows, cols)] * nz
    if n:
        width = direct[0].shape[1]
        pieces = [(start, min(start + width, cols)) for start in range(0, cols, width)]
        shapes[2] = (mode_dev + len(pieces) * rows, width)
        shapes += [begin[0].shape]

    def body(*refs):
        motion_refs, load_refs, enter_ref = refs[:nc], refs[nc : nc + parts], refs[nc + parts]
        more, out_refs = refs[nc + parts + 1 : nc + parts + 1 + n + m], refs[nc + parts + 1 + n + m : -3]
        motion_all, load_all, share_ref = refs[-3:]
        if n:
            out_refs[2][...] = jnp.zeros(shapes[2], F32)
            out_refs[2][:mode_dev] = more[0][...]
            out_refs[nz][...] = more[1][...] + more[2][...]
        z, c = lax.axis_index("taps"), lax.axis_index("floors")
        later = lax.axis_index("tm") > 0
        motion = motion_refs[0][...]
        for ref in motion_refs[1:]:
            motion = motion + ref[...]
        for o in range(owners):
            at = slice(o * floor_dev, (o + 1) * floor_dev)
            motion_all[o] = motion[at]
            for k in range(parts):
                load_all[o, :, k * span : (k + 1) * span] = load_refs[k][at]
        for p, place in enumerate(placed(z, nz)):
            owner = place * nc + c
            out = share_ref if n and p == 2 else out_refs[p]
            out[...] = jnp.zeros((rows, cols), F32)
            for k, ref in enumerate((motion_all, load_all)):
                for h in (0, 1):
                    at = slice((2 * k + h) * floor_dev, (2 * k + h + 1) * floor_dev)
                    out[at, :half] = ref[owner, :, h * half : (h + 1) * half]
            state = enter_ref[0:2, p * mode_dev : (p + 1) * mode_dev]
            out[:2, half : half + mode_dev] = jnp.where(later, state, 0.0)
        if n:
            for k, (start, stop) in enumerate(pieces):
                at = mode_dev + k * rows
                out_refs[2][at : at + rows, : stop - start] = share_ref[:, start:stop]

    return pl.pallas_call(
        body,
        in_specs=whole(nc + parts + 1 + n + m),
        out_specs=whole(len(shapes)),
        out_shape=[jax.ShapeDtypeStruct(x, F32) for x in shapes],
        scratch_shapes=[pltpu.VMEM((owners, floor_dev, time), F32)] * 2 + [pltpu.VMEM((rows, cols), F32)],
        compiler_params=params(),
        cost_estimate=cost(1),
        name="owner_shares",
    )(*motions, *loads, enter, *direct, *begin)


def share_shape(floor_dev, time):
    return -(-4 * floor_dev // 8) * 8, time // 2 + TILE


def spread(column):
    return jnp.broadcast_to(column, (column.shape[0], TILE))


def widened(tile):
    return jnp.concatenate([tile] * (BLK // TILE), axis=1)


def block_sums(force, tables, tri):
    return [dot_exact_right(force * table, tri) for table in tables]


def sum_at(refs, forces, b, mode_dev):
    total = None
    for ref, (x, row, start) in zip(refs, forces):
        if start <= b * BLK < start + x.shape[1]:
            part = ref[row : row + mode_dev, b * BLK - start : (b + 1) * BLK - start]
            total = part if total is None else total + part
    return total


def own_response(forces, shares, tables, turns, floor_dev, load_scale):
    mode_dev = forces[0][0].shape[0]
    n, m = len(shares), len(forces)
    half = shares[0][0].shape[1] - TILE
    time = 2 * half
    rows, width = share_shape(floor_dev, time)
    blocks = time // BLK

    def body(*refs):
        tab_ref, turn_ref, resp_ref, motion_ref, load_ref, share_ref = refs[m + n :]
        for i, (_, row, start, stop) in enumerate(shares):
            at = slice(start, stop)
            part = refs[m + i][row : row + rows, : stop - start]
            share_ref[:, at] = part if i == 0 else share_ref[:, at] + part
        share = share_ref[...]
        for h in (0, 1):
            at = slice(h * half, (h + 1) * half)
            motion_ref[:, at] = share[h * floor_dev : (h + 1) * floor_dev, :half]
            load_ref[:, at] = share[(2 + h) * floor_dev : (3 + h) * floor_dev, :half] * load_scale
        qr, qi = tab_ref[2], tab_ref[3]
        turn = [spread(turn_ref[:mode_dev, i : i + 1]) for i in (0, 1)]
        column = share[:, half:].T
        state = [spread(column[:mode_dev, i : i + 1]) for i in (0, 1)]
        tri = triangle()
        sums = [
            block_sums(sum_at(refs, forces, b, mode_dev), (tab_ref[0], tab_ref[1]), tri)
            for b in range(blocks)
        ]
        for b in range(blocks):
            cr, ci = (x + widened(y) for x, y in zip(sums[b], state))
            resp_ref[:, b * BLK : (b + 1) * BLK] = qr * cr - qi * ci
            state = turned(turn, [spread(x[:, BLK - 1 :]) + y for x, y in zip(sums[b], state)])

    return pl.pallas_call(
        body,
        in_specs=whole(m + n + 2),
        out_specs=tuple(whole(3)),
        out_shape=(
            jax.ShapeDtypeStruct((mode_dev, time), F32),
            jax.ShapeDtypeStruct((floor_dev, time), F32),
            jax.ShapeDtypeStruct((floor_dev, time), F32),
        ),
        scratch_shapes=[pltpu.VMEM((rows, width), F32)],
        compiler_params=params(),
        cost_estimate=cost(1),
        name="own_response",
    )(*(x for x, _, _ in forces), *(x[0] for x in shares), tables, turns)


def shifts(x, axis, n):
    return [lax.ppermute(x, axis, [(i, (i + d) % n) for i in range(n)]) for d in range(1, n)]


def along(parts, n):
    return [parts[0]] + [
        lax.ppermute(parts[d], "taps", [(i, (i + d) % n) for i in range(n)]) for d in range(1, n)
    ]


def on_device(
    pressures,
    tap_area,
    tap_panel,
    tap_floor,
    panel_shape,
    floor_shape,
    mode_order,
    mode_decay,
    mode_freq,
):
    nz = lax.axis_size("taps")
    nc = lax.axis_size("floors")
    nt = lax.axis_size("tm")
    owners = nz * nc
    modes = mode_order.shape[0]
    mode_dev = modes // owners
    time, taps = pressures.shape
    panels = panel_shape.shape[0]
    floors = floor_shape.shape[0]
    floor_dev = floors // owners
    load_scale = (floors / (taps * owners)) ** 0.5

    mine, kept = tap_sums(
        pressures,
        tap_panel[None],
        tap_floor[None],
        tap_area,
        (mode_order[None], mode_decay[None], mode_freq[None], panel_shape, floor_shape),
        panels,
        floors,
    )
    sums = [[mine] + shifts(mine, "floors", nc)]
    pt, floor_slots, tables, turns, own = mode_tables(*kept, nz, nc)
    forces, loads, spread = [], [], []
    for part in sums:
        force, load, spread = slot_forces(part, pt, tables, turns, nz, spread)
        forces.append(force)
        loads.append(load)
    pair, two, mirror = ([(i, i ^ d) for i in range(nz)] for d in (1, 2, 3))
    until = direct_until(time)
    laid = [(x, p * mode_dev, start) for x, (p, start, _) in zip(forces[0], send_plan(nz, time))]
    if nz == PAIRED:
        onward = [forces[0][1], lax.ppermute(forces[0][3], "taps", pair)]
        direct, tail = [forces[0][6]], lax.ppermute(forces[0][2], "taps", pair)
        begin = [lax.ppermute(x, "taps", way) for x, way in zip(forces[0][4:6], (two, mirror))]
    else:
        crossed, onward = [(x, 0, 0) for x in along(forces[0], nz)], []
        direct, begin = [], []
    motion = motion_from_rest(laid, tables, turns, floor_slots)
    ends = end_states(spread, turns, motion)
    enter = jnp.zeros_like(ends)
    for hop in range(nt - 1):
        passed = ends
        if hop:
            turn = (ends[2:3], ends[3:4])
            over = turn
            for _ in range(time // BLK - 1):
                over = turned(over, turn)
            enter = jnp.where(lax.axis_index("tm") > 0, enter, 0.0)
            passed = ends + jnp.concatenate(
                [*turned(over, (enter[0:1], enter[1:2])), jnp.zeros_like(ends[2:])]
            )
        enter = lax.ppermute(passed, "tm", [(i, (i + 1) % nt) for i in range(nt)])
    motion, *onward = floor_shares(motion, ends, enter, tables, floor_slots, onward)
    motions = [motion] + shifts(motion, "floors", nc)
    shares = owner_shares(motions, loads, enter, direct, begin, nz, floor_dev)
    if nz == PAIRED:
        ways = (two, pair, mirror)
        away, near, far = (lax.ppermute(x, "taps", way) for x, way in zip(shares[1:4], ways))
        onward = lax.ppermute(onward[0], "taps", two)
        rows, cols = share_shape(floor_dev, time)
        crossed = [(forces[0][0], 0, 0), (near, 0, 0), (tail, 0, until)]
        crossed += [(shares[4], 0, 0), (onward, 0, until)]
        shares = [(x, 0, 0, cols) for x in (shares[0], away, far)]
        for k, start in enumerate(range(0, cols, until)):
            shares.append((near, mode_dev + k * rows, start, min(start + until, cols)))
    else:
        shares = [(x, 0, 0, x.shape[1]) for x in along(shares, nz)]
    return own_response(crossed, shares, own, turns, floor_dev, load_scale)


def solution(mesh):
    in_specs = (
        P(("dirs", "tm"), ("taps", "floors")),
        P(("taps", "floors")),
        P(("taps", "floors")),
        P(("taps", "floors")),
        P(),
        P(),
        P(),
        P(),
        P(),
    )
    out_specs = (
        P(("taps", "floors"), ("dirs", "tm")),
        P(("taps", "floors"), ("dirs", "tm")),
        P(("taps", "floors"), ("dirs", "tm")),
    )
    return jax.shard_map(
        on_device, mesh=mesh, in_specs=in_specs, out_specs=out_specs, check_vma=False
    )
```

```python
import jax
import jax.numpy as jnp
from jax import lax
from jax.experimental import pallas as pl
from jax.experimental.pallas import tpu as pltpu
from jax.sharding import PartitionSpec as P

BLK = 256
PAIRED = 4
TILE = 128
BF = jnp.bfloat16
F32 = jnp.float32
NN = (((1,), (0,)), ((), ()))
NT = (((1,), (1,)), ((), ()))
VMEM_LIMIT = 16 * 1024 * 1024


def dot(a, b, dims=NN):
    return lax.dot_general(a, b, dims, preferred_element_type=F32)


def split(x):
    hi = x.astype(BF)
    return hi, (x - hi.astype(F32)).astype(BF)


def dot_exact_left(a, x, dims=NN):
    hi, lo = split(x)
    return dot(a, hi, dims) + dot(a, lo, dims)


def dot_exact_right(x, b, dims=NN):
    hi, lo = split(x)
    return dot(hi, b, dims) + dot(lo, b, dims)


def params():
    return pltpu.CompilerParams(vmem_limit_bytes=VMEM_LIMIT)


def in_hbm(x):
    return pltpu.with_memory_space_constraint(x, pltpu.HBM)


def cost(us):
    return pl.CostEstimate(flops=int(us * 5e8), bytes_accessed=int(us * 2e6), transcendentals=0)


def whole(n):
    return [pl.BlockSpec(memory_space=pltpu.VMEM)] * n


def tap_sums(pressures, tap_panel, tap_floor, tap_area, others, panels, floors):
    time, taps = pressures.shape
    rows = panels + floors
    chunks = 2 if time % (2 * BLK) == 0 else 1
    span = time // chunks
    n = len(others)
    given = (tap_panel, tap_floor, tap_area)

    def body(press_hbm, *refs):
        from_refs, sums_ref, kept = refs[: n + 3], refs[n + 3], refs[n + 4 : 2 * n + 4]
        press, panel, floor, area, weights, sems = refs[2 * n + 4 :]
        small = [
            pltpu.make_async_copy(a, b, sems.at[chunks + i])
            for i, (a, b) in enumerate(zip(from_refs, (panel, floor, area, *kept)))
        ]
        large = []
        for i in range(chunks):
            at = pl.ds(i * span, span)
            large.append(pltpu.make_async_copy(press_hbm.at[at], press.at[at], sems.at[i]))
        for copy in [*small[:3], *large, *small[3:]]:
            copy.start()
        for copy in small[:3]:
            copy.wait()
        each = jnp.broadcast_to(area[...].astype(F32).reshape(1, taps), (16, taps))
        row = lax.broadcasted_iota(jnp.int32, (16, taps), 0)
        for ids, first, count in ((panel, 0, panels), (floor, panels, floors)):
            at = jnp.broadcast_to(ids[...], (16, taps)) - row
            for r in range(0, count, 16):
                weights[first + r : first + r + 16] = jnp.where(at == r, each, 0.0).astype(BF)
        for i in range(chunks):
            at = slice(i * span, (i + 1) * span)
            large[i].wait()
            sums_ref[:, at] = dot(weights[...], press[at], NT)
        for copy in small[3:]:
            copy.wait()

    out = pl.pallas_call(
        body,
        in_specs=[pl.BlockSpec(memory_space=pltpu.HBM)] * (n + 4),
        out_specs=tuple(whole(n + 1)),
        out_shape=(jax.ShapeDtypeStruct((rows, time), F32), *(jax.ShapeDtypeStruct(x.shape, x.dtype) for x in others)),
        scratch_shapes=[
            pltpu.VMEM((time, taps), BF),
            *(pltpu.VMEM(x.shape, x.dtype) for x in given),
            pltpu.VMEM((rows, taps), BF),
            pltpu.SemaphoreType.DMA((chunks + n + 3,)),
        ],
        compiler_params=params(),
        cost_estimate=cost(3),
        name="tap_sums",
    )(in_hbm(pressures), *(in_hbm(x) for x in given), *(in_hbm(x) for x in others))
    return out[0], out[1:]


def placed(z, nz):
    if nz != PAIRED:
        return [lax.rem(z + d, nz) for d in range(nz)]
    return [z, lax.rem(z + 2, nz), z + 1 - 2 * lax.rem(z, 2), nz - 1 - z]


def mode_tables(order, decay, freq, panel_shape, floor_shape, nz, nc):
    modes = order.shape[1]
    panels = panel_shape.shape[0]
    floors = floor_shape.shape[0]
    mode_dev = modes // (nz * nc)
    slots = mode_dev * nz
    bits = BLK.bit_length() - 1
    half = BLK // 2

    def body(*refs):
        order_ref, decay_ref, freq_ref, panel_ref, floor_ref = refs[:5]
        pt_ref, fs_ref, tab_ref, turn_ref, own_ref, column_ref = refs[5:]
        column_ref[...] = jnp.broadcast_to(order_ref[...].astype(F32), (TILE, modes)).T
        z, c = lax.axis_index("taps"), lax.axis_index("floors")
        picked = []
        for at in placed(z, nz):
            owner = at * nc + c
            picked.append(column_ref[pl.ds(pl.multiple_of(owner * mode_dev, mode_dev), mode_dev), :])
        column = jnp.concatenate(picked, axis=0)[:, :1]
        ids = lax.broadcasted_iota(jnp.int32, (slots, modes), 1).astype(F32)
        pick = jnp.where(column == ids, 1.0, 0.0).astype(BF)
        pt_ref[...] = dot(pick, panel_ref[...], NT).astype(BF)
        fs_ref[...] = dot(floor_ref[...], pick, NT)
        decays, angles = decay_ref[...], freq_ref[...]
        re, im = jnp.cos(angles), jnp.sin(angles)
        rows = [decays]
        square = decays * decays
        loss = 2.0 * jnp.exp(-decays) * decays * (1.0 + square * (1.0 / 6.0 + square * (1.0 / 120.0)))
        rows.append(jnp.sqrt(loss))
        for _ in range(bits + 1):
            rows += [re, im]
            re, im = re * re - im * im, 2.0 * re * im
        rows += [jnp.zeros_like(re)] * (-len(rows) % 16)
        count = len(rows)
        stack = jnp.concatenate(rows, axis=0)
        hi, mid = split(stack)
        low = (stack - hi.astype(F32) - mid.astype(F32)).astype(BF)
        parts = dot(pick, jnp.concatenate([hi, mid, low], axis=0), NT)
        cols = parts[:, :count] + parts[:, count : 2 * count] + parts[:, 2 * count : 3 * count]
        rate, gain = cols[:, 0:1], cols[:, 1:2]
        lane = lax.broadcasted_iota(jnp.int32, (slots, half), 1)
        cos = jnp.where((lane & 1) != 0, cols[:, 2:3], 1.0)
        sin = jnp.where((lane & 1) != 0, cols[:, 3:4], 0.0)
        for b in range(1, bits - 1):
            on = (lane & (1 << b)) != 0
            step = cols[:, 2 + 2 * b : 3 + 2 * b], cols[:, 3 + 2 * b : 4 + 2 * b]
            new_cos, new_sin = turned((cos, sin), step)
            cos, sin = jnp.where(on, new_cos, cos), jnp.where(on, new_sin, sin)
        at = 2 * bits
        far_cos, far_sin = turned((cos, sin), (cols[:, at : at + 1], cols[:, at + 1 : at + 2]))
        steps = rate * lane.astype(F32)
        shrink, grow = jnp.exp(-steps), gain * jnp.exp(steps)
        far_shrink = shrink * jnp.exp(-rate * float(half))
        far_grow = grow * jnp.exp(rate * float(half))
        near, far = slice(0, half), slice(half, BLK)
        tab_ref[0, :, near], tab_ref[0, :, far] = grow * cos, far_grow * far_cos
        tab_ref[1, :, near], tab_ref[1, :, far] = -grow * sin, -far_grow * far_sin
        tab_ref[2, :, near], tab_ref[2, :, far] = shrink * cos, far_shrink * far_cos
        tab_ref[3, :, near], tab_ref[3, :, far] = shrink * sin, far_shrink * far_sin
        fade = jnp.exp(-rate * float(BLK))
        turn_ref[...] = fade * cols[:, at + 2 : at + 4]
        own_ref[...] = tab_ref[:, :mode_dev]

    return pl.pallas_call(
        body,
        in_specs=whole(5),
        out_specs=tuple(whole(5)),
        out_shape=(
            jax.ShapeDtypeStruct((slots, panels), BF),
            jax.ShapeDtypeStruct((floors, slots), F32),
            jax.ShapeDtypeStruct((4, slots, BLK), F32),
            jax.ShapeDtypeStruct((slots, 2), F32),
            jax.ShapeDtypeStruct((4, mode_dev, BLK), F32),
        ),
        scratch_shapes=[pltpu.VMEM((modes, TILE), F32)],
        compiler_params=params(),
        cost_estimate=cost(2),
        name="mode_tables",
    )(order, decay, freq, panel_shape, floor_shape)


def direct_until(time):
    return time // 4 // BLK * BLK


def send_plan(nz, time):
    until = direct_until(time)
    if nz != PAIRED or not until:
        return [(p, 0, time) for p in range(nz)]
    late = [(p, until, time) for p in (1, 2, 3)]
    return [(0, 0, time), *late, *((p, 0, until) for p in (3, 1, 2))]


def slot_forces(sums, pt, tables, turns, nz, before):
    slots, panels = pt.shape
    rows, time = sums[0].shape
    nc = len(sums)
    mode_dev = slots // nz
    plan = send_plan(nz, time)
    n = len(before)

    def body(*refs):
        sum_refs, (pt_ref, tab_ref, turn_ref) = refs[:nc], refs[nc : nc + 3]
        before_refs, out_refs = refs[nc + 3 : nc + 3 + n], refs[nc + 3 + n : -3]
        load_ref, state_refs = refs[-3], refs[-2:]
        load = sum_refs[0][panels:]
        for ref in sum_refs[1:]:
            load = load + ref[panels:]
        load_ref[...] = load
        left = pt_ref[...]
        turn = turn_ref[:, 0:1], turn_ref[:, 1:2]
        state = [ref[...] for ref in before_refs]
        for b in range(time // BLK):
            cols = slice(b * BLK, (b + 1) * BLK)
            total = sum_refs[0][:panels, cols]
            for ref in sum_refs[1:]:
                total = total + ref[:panels, cols]
            forces = dot_exact_left(left, total)
            for ref, (p, start, stop) in zip(out_refs, plan):
                if start <= b * BLK < stop:
                    at = slice(b * BLK - start, (b + 1) * BLK - start)
                    ref[:, at] = forces[p * mode_dev : (p + 1) * mode_dev]
            new = []
            for part in (forces * tab_ref[0], forces * tab_ref[1]):
                near = part[:, :TILE]
                for k in range(TILE, BLK, TILE):
                    near = near + part[:, k : k + TILE]
                new.append(near)
            if state:
                new = [a + b for a, b in zip(new, state)]
            state = turned(turn, new)
        state_refs[0][...], state_refs[1][...] = state

    out = pl.pallas_call(
        body,
        in_specs=whole(nc + 3 + n),
        out_specs=whole(len(plan) + 3),
        out_shape=[jax.ShapeDtypeStruct((mode_dev, stop - start), F32) for _, start, stop in plan]
        + [jax.ShapeDtypeStruct((rows - panels, time), F32)]
        + [jax.ShapeDtypeStruct((slots, TILE), F32)] * 2,
        compiler_params=params(),
        cost_estimate=cost(1),
        name="slot_forces",
    )(*sums, pt, tables, turns, *before)
    return out[:-3], out[-3], out[-2:]


def end_states(spread, turns, after):
    slots = turns.shape[0]

    def body(re_ref, im_ref, turn_ref, after_ref, out_ref):
        pad = jnp.zeros((TILE, TILE - 4), F32)
        for k in range(0, slots, TILE):
            at = slice(k, k + TILE)
            state = [jnp.sum(ref[at], axis=1, keepdims=True) for ref in (re_ref, im_ref)]
            four = [*state, turn_ref[at, 0:1], turn_ref[at, 1:2]]
            out_ref[:, at] = jnp.concatenate([*four, pad], axis=1).T[:8]

    return pl.pallas_call(
        body,
        in_specs=whole(4),
        out_specs=whole(1)[0],
        out_shape=jax.ShapeDtypeStruct((8, slots), F32),
        compiler_params=params(),
        cost_estimate=cost(1),
        name="end_states",
    )(*spread, turns, after)


def triangle():
    row = lax.broadcasted_iota(jnp.int32, (BLK, BLK), 0)
    col = lax.broadcasted_iota(jnp.int32, (BLK, BLK), 1)
    return jnp.where(row <= col, 1.0, 0.0).astype(BF)


def turned(a, b):
    return (a[0] * b[0] - a[1] * b[1], a[0] * b[1] + a[1] * b[0])


def motion_from_rest(forces, tables, turns, floor_slots):
    slots = turns.shape[0]
    floors = floor_slots.shape[0]
    time = max(start + x.shape[1] for x, _, start in forces)
    blocks = time // BLK
    n = len(forces)
    places = [(row, start, x.shape) for x, row, start in forces]

    def body(*refs):
        tab_ref, turn_ref, fs_ref, motion_ref = refs[n:]
        tri = triangle()
        here = fs_ref[...].astype(BF)
        turn = [spread(turn_ref[:, i : i + 1]) for i in (0, 1)]
        state = None
        for b in range(blocks):
            found = [
                (row, ref[:, b * BLK - start : (b + 1) * BLK - start])
                for ref, (row, start, shape) in zip(refs, places)
                if start <= b * BLK < start + shape[1]
            ]
            force = jnp.concatenate([x for _, x in sorted(found, key=lambda f: f[0])], axis=0)
            cr, ci = block_sums(force, (tab_ref[0], tab_ref[1]), tri)
            last = [spread(x[:, BLK - 1 :]) for x in (cr, ci)]
            if state is not None:
                cr, ci = cr + widened(state[0]), ci + widened(state[1])
                last = [x + y for x, y in zip(last, state)]
            part = dot_exact_left(here, tab_ref[2] * cr - tab_ref[3] * ci)
            motion_ref[:, b * BLK : (b + 1) * BLK] = part
            state = turned(turn, last)

    return pl.pallas_call(
        body,
        in_specs=whole(n + 3),
        out_specs=whole(1)[0],
        out_shape=jax.ShapeDtypeStruct((floors, time), F32),
        compiler_params=params(),
        cost_estimate=cost(2),
        name="motion_from_rest",
    )(*(x for x, _, _ in forces), tables, turns, floor_slots)


def floor_shares(motion, ends, enter, tables, floor_slots, onward):
    floors, time = motion.shape
    blocks = time // BLK
    n = len(onward)

    def body(motion_ref, ends_ref, enter_ref, tab_ref, fs_ref, *refs):
        out_ref = refs[n]
        if n:
            refs[n + 1][...] = refs[0][...] + refs[1][...]
        shape = fs_ref[...]
        turn = (ends_ref[2:3, :], ends_ref[3:4, :])
        later = lax.axis_index("tm") > 0
        state = tuple(jnp.where(later, enter_ref[i : i + 1, :], 0.0) for i in (0, 1))
        left_re, left_im = [], []
        for b in range(blocks):
            left_re.append(shape * state[0])
            left_im.append(shape * state[1])
            state = turned(turn, state)
        qr_hi, qr_lo = split(tab_ref[2])
        qi_hi, qi_lo = split(tab_ref[3])
        re_hi, re_lo = split(jnp.concatenate(left_re, axis=0))
        im_hi, im_lo = split(jnp.concatenate(left_im, axis=0))
        free = dot(re_hi, qr_hi) + dot(re_hi, qr_lo) + dot(re_lo, qr_hi)
        free = free - (dot(im_hi, qi_hi) + dot(im_hi, qi_lo) + dot(im_lo, qi_hi))
        for b in range(blocks):
            cols = slice(b * BLK, (b + 1) * BLK)
            out_ref[:, cols] = motion_ref[:, cols] + free[b * floors : (b + 1) * floors]

    return pl.pallas_call(
        body,
        in_specs=whole(5 + n),
        out_specs=whole(1 + len(onward[:1])),
        out_shape=[
            jax.ShapeDtypeStruct(x, F32) for x in [(floors, time)] + [x.shape for x in onward[:1]]
        ],
        compiler_params=params(),
        cost_estimate=cost(1),
        name="floor_shares",
    )(motion, ends, enter, tables, floor_slots, *onward)


def owner_shares(motions, loads, enter, direct, begin, nz, floor_dev):
    nc, parts = len(motions), len(loads)
    floors, time = motions[0].shape
    rows, cols = share_shape(floor_dev, time)
    owners = nz * nc
    mode_dev = enter.shape[1] // nz
    span = time // parts
    n, m = len(direct), len(begin)
    half = time // 2
    shapes = [(rows, cols)] * nz
    if n:
        width = direct[0].shape[1]
        pieces = [(start, min(start + width, cols)) for start in range(0, cols, width)]
        shapes[2] = (mode_dev + len(pieces) * rows, width)
        shapes += [begin[0].shape]

    def body(*refs):
        motion_refs, load_refs, enter_ref = refs[:nc], refs[nc : nc + parts], refs[nc + parts]
        more, out_refs = refs[nc + parts + 1 : nc + parts + 1 + n + m], refs[nc + parts + 1 + n + m : -3]
        motion_all, load_all, share_ref = refs[-3:]
        if n:
            out_refs[2][...] = jnp.zeros(shapes[2], F32)
            out_refs[2][:mode_dev] = more[0][...]
            out_refs[nz][...] = more[1][...] + more[2][...]
        z, c = lax.axis_index("taps"), lax.axis_index("floors")
        later = lax.axis_index("tm") > 0
        motion = motion_refs[0][...]
        for ref in motion_refs[1:]:
            motion = motion + ref[...]
        for o in range(owners):
            at = slice(o * floor_dev, (o + 1) * floor_dev)
            motion_all[o] = motion[at]
            for k in range(parts):
                load_all[o, :, k * span : (k + 1) * span] = load_refs[k][at]
        for p, place in enumerate(placed(z, nz)):
            owner = place * nc + c
            out = share_ref if n and p == 2 else out_refs[p]
            out[...] = jnp.zeros((rows, cols), F32)
            for k, ref in enumerate((motion_all, load_all)):
                for h in (0, 1):
                    at = slice((2 * k + h) * floor_dev, (2 * k + h + 1) * floor_dev)
                    out[at, :half] = ref[owner, :, h * half : (h + 1) * half]
            state = enter_ref[0:2, p * mode_dev : (p + 1) * mode_dev]
            out[:2, half : half + mode_dev] = jnp.where(later, state, 0.0)
        if n:
            for k, (start, stop) in enumerate(pieces):
                at = mode_dev + k * rows
                out_refs[2][at : at + rows, : stop - start] = share_ref[:, start:stop]

    return pl.pallas_call(
        body,
        in_specs=whole(nc + parts + 1 + n + m),
        out_specs=whole(len(shapes)),
        out_shape=[jax.ShapeDtypeStruct(x, F32) for x in shapes],
        scratch_shapes=[pltpu.VMEM((owners, floor_dev, time), F32)] * 2 + [pltpu.VMEM((rows, cols), F32)],
        compiler_params=params(),
        cost_estimate=cost(1),
        name="owner_shares",
    )(*motions, *loads, enter, *direct, *begin)


def share_shape(floor_dev, time):
    return -(-4 * floor_dev // 8) * 8, time // 2 + TILE


def spread(column):
    return jnp.broadcast_to(column, (column.shape[0], TILE))


def widened(tile):
    return jnp.concatenate([tile] * (BLK // TILE), axis=1)


def block_sums(force, tables, tri):
    return [dot_exact_right(force * table, tri) for table in tables]


def sum_at(refs, forces, b, mode_dev):
    total = None
    for ref, (x, row, start) in zip(refs, forces):
        if start <= b * BLK < start + x.shape[1]:
            part = ref[row : row + mode_dev, b * BLK - start : (b + 1) * BLK - start]
            total = part if total is None else total + part
    return total


def own_response(forces, shares, tables, turns, floor_dev, load_scale):
    mode_dev = forces[0][0].shape[0]
    n, m = len(shares), len(forces)
    half = shares[0][0].shape[1] - TILE
    time = 2 * half
    rows, width = share_shape(floor_dev, time)
    blocks = time // BLK

    def body(*refs):
        tab_ref, turn_ref, resp_ref, motion_ref, load_ref, share_ref = refs[m + n :]
        for i, (_, row, start, stop) in enumerate(shares):
            at = slice(start, stop)
            part = refs[m + i][row : row + rows, : stop - start]
            share_ref[:, at] = part if i == 0 else share_ref[:, at] + part
        share = share_ref[...]
        for h in (0, 1):
            at = slice(h * half, (h + 1) * half)
            motion_ref[:, at] = share[h * floor_dev : (h + 1) * floor_dev, :half]
            load_ref[:, at] = share[(2 + h) * floor_dev : (3 + h) * floor_dev, :half] * load_scale
        qr, qi = tab_ref[2], tab_ref[3]
        turn = [spread(turn_ref[:mode_dev, i : i + 1]) for i in (0, 1)]
        column = share[:, half:].T
        state = [spread(column[:mode_dev, i : i + 1]) for i in (0, 1)]
        tri = triangle()
        sums = [
            block_sums(sum_at(refs, forces, b, mode_dev), (tab_ref[0], tab_ref[1]), tri)
            for b in range(blocks)
        ]
        for b in range(blocks):
            cr, ci = (x + widened(y) for x, y in zip(sums[b], state))
            resp_ref[:, b * BLK : (b + 1) * BLK] = qr * cr - qi * ci
            state = turned(turn, [spread(x[:, BLK - 1 :]) + y for x, y in zip(sums[b], state)])

    return pl.pallas_call(
        body,
        in_specs=whole(m + n + 2),
        out_specs=tuple(whole(3)),
        out_shape=(
            jax.ShapeDtypeStruct((mode_dev, time), F32),
            jax.ShapeDtypeStruct((floor_dev, time), F32),
            jax.ShapeDtypeStruct((floor_dev, time), F32),
        ),
        scratch_shapes=[pltpu.VMEM((rows, width), F32)],
        compiler_params=params(),
        cost_estimate=cost(1),
        name="own_response",
    )(*(x for x, _, _ in forces), *(x[0] for x in shares), tables, turns)


def shifts(x, axis, n):
    return [lax.ppermute(x, axis, [(i, (i + d) % n) for i in range(n)]) for d in range(1, n)]


def along(parts, n):
    return [parts[0]] + [
        lax.ppermute(parts[d], "taps", [(i, (i + d) % n) for i in range(n)]) for d in range(1, n)
    ]


def on_device(
    pressures,
    tap_area,
    tap_panel,
    tap_floor,
    panel_shape,
    floor_shape,
    mode_order,
    mode_decay,
    mode_freq,
):
    nz = lax.axis_size("taps")
    nc = lax.axis_size("floors")
    nt = lax.axis_size("tm")
    owners = nz * nc
    modes = mode_order.shape[0]
    mode_dev = modes // owners
    time, taps = pressures.shape
    panels = panel_shape.shape[0]
    floors = floor_shape.shape[0]
    floor_dev = floors // owners
    load_scale = (floors / (taps * owners)) ** 0.5

    mine, kept = tap_sums(
        pressures,
        tap_panel[None],
        tap_floor[None],
        tap_area,
        (mode_order[None], mode_decay[None], mode_freq[None], panel_shape, floor_shape),
        panels,
        floors,
    )
    sums = [[mine] + shifts(mine, "floors", nc)]
    pt, floor_slots, tables, turns, own = mode_tables(*kept, nz, nc)
    forces, loads, spread = [], [], []
    for part in sums:
        force, load, spread = slot_forces(part, pt, tables, turns, nz, spread)
        forces.append(force)
        loads.append(load)
    pair, two, mirror = ([(i, i ^ d) for i in range(nz)] for d in (1, 2, 3))
    until = direct_until(time)
    laid = [(x, p * mode_dev, start) for x, (p, start, _) in zip(forces[0], send_plan(nz, time))]
    if nz == PAIRED:
        onward = [forces[0][1], lax.ppermute(forces[0][3], "taps", pair)]
        direct, tail = [forces[0][6]], lax.ppermute(forces[0][2], "taps", pair)
        begin = [lax.ppermute(x, "taps", way) for x, way in zip(forces[0][4:6], (mirror, two))]
    else:
        crossed, onward = [(x, 0, 0) for x in along(forces[0], nz)], []
        direct, begin = [], []
    motion = motion_from_rest(laid, tables, turns, floor_slots)
    ends = end_states(spread, turns, motion)
    enter = jnp.zeros_like(ends)
    for hop in range(nt - 1):
        passed = ends
        if hop:
            turn = (ends[2:3], ends[3:4])
            over = turn
            for _ in range(time // BLK - 1):
                over = turned(over, turn)
            enter = jnp.where(lax.axis_index("tm") > 0, enter, 0.0)
            passed = ends + jnp.concatenate(
                [*turned(over, (enter[0:1], enter[1:2])), jnp.zeros_like(ends[2:])]
            )
        enter = lax.ppermute(passed, "tm", [(i, (i + 1) % nt) for i in range(nt)])
    motion, *onward = floor_shares(motion, ends, enter, tables, floor_slots, onward)
    motions = [motion] + shifts(motion, "floors", nc)
    shares = owner_shares(motions, loads, enter, direct, begin, nz, floor_dev)
    if nz == PAIRED:
        ways = (two, pair, mirror)
        away, near, far = (lax.ppermute(x, "taps", way) for x, way in zip(shares[1:4], ways))
        onward = lax.ppermute(onward[0], "taps", two)
        rows, cols = share_shape(floor_dev, time)
        crossed = [(forces[0][0], 0, 0), (near, 0, 0), (tail, 0, until)]
        crossed += [(shares[4], 0, 0), (onward, 0, until)]
        shares = [(x, 0, 0, cols) for x in (shares[0], away, far)]
        for k, start in enumerate(range(0, cols, until)):
            shares.append((near, mode_dev + k * rows, start, min(start + until, cols)))
    else:
        shares = [(x, 0, 0, x.shape[1]) for x in along(shares, nz)]
    return own_response(crossed, shares, own, turns, floor_dev, load_scale)


def solution(mesh):
    in_specs = (
        P(("dirs", "tm"), ("taps", "floors")),
        P(("taps", "floors")),
        P(("taps", "floors")),
        P(("taps", "floors")),
        P(),
        P(),
        P(),
        P(),
        P(),
    )
    out_specs = (
        P(("taps", "floors"), ("dirs", "tm")),
        P(("taps", "floors"), ("dirs", "tm")),
        P(("taps", "floors"), ("dirs", "tm")),
    )
    return jax.shard_map(
        on_device, mesh=mesh, in_specs=in_specs, out_specs=out_specs, check_vma=False
    )
```
